32 devices in a mesh: group: 2 (over y), patch: 4 (over z), head: 2 (over x), cfg: 2 (over core).
Axes of the slice: x: 2, y: 2, z: 4, core: 2. Of those that a mesh axis runs over, the one named last changes fastest.
Arguments:
- fresh_query: bfloat16 [4, 256, 2560], P(('group', 'cfg'), ('patch', 'head')), parts along dimension 0, may hold values from -32 to 32
- fresh_key: bfloat16 [4, 256, 2560], P(('group', 'cfg'), ('patch', 'head')), parts along dimension 0, may hold values from -9 to 9
- fresh_value: bfloat16 [4, 256, 2560], P(('group', 'cfg'), ('patch', 'head')), parts along dimension 0, may hold values from -12 to 12
- stale_key: bfloat16 [4, 256, 2560], P(('group', 'cfg'), 'patch', 'head'), parts along dimension 0, may hold values from -8 to 8
- stale_value: bfloat16 [4, 256, 2560], P(('group', 'cfg'), 'patch', 'head'), parts along dimension 0, may hold values from -12 to 12
- cross_query: bfloat16 [4, 256, 2560], P(('group', 'cfg'), ('patch', 'head')), parts along dimension 0, may hold values from -32 to 32
- text_key: bfloat16 [4, 512, 2560], P(('group', 'cfg'), None, 'head'), parts along dimension 0, may hold values from -8 to 8
- text_value: bfloat16 [4, 512, 2560], P(('group', 'cfg'), None, 'head'), parts along dimension 0, may hold values from -12 to 12
- text_mask: int32 [4, 512], P(('group', 'cfg')), parts along dimension 0, may hold values from 0 to 1, as said below
Outputs:
- self_mixed: bfloat16 [4, 256, 2560], P(('group', 'cfg'), ('patch', 'head')), parts along dimension 0
- cross_mixed: bfloat16 [4, 256, 2560], P(('group', 'cfg'), ('patch', 'head')), parts along dimension 0
The draws below stay inside these ranges and needn't reach their ends.
There are 2 independent parts, one for each index of `group`. The reference program is written for one: setup_inputs(seed, part) draws one part's arguments, and reference() takes and returns one part's arrays. A program takes and returns all parts, laid end to end along the dimension named above; each array names one. Nothing has to cross between parts.
Inputs may be any that keep to these rules, and one draw needn't show every extreme that they name: In each branch the ones of text_mask form a prefix of 32 or more positions; in one of the two branches all 512 are ones, in the other some are zeros.
All inputs are finite; a program needn't handle non-finite values.
Results may differ from the reference program's by a relative error of at most 0.005.
Values may be sent and summed in bfloat16 or wider, within the bound.
No kernel may reach another device: no remote copies, remote signals or barrier semaphores. Data moves between devices by JAX's collectives and lax.ppermute only.
A program may use at most 128 MiB of HBM per device.

```python
import math
import jax
import jax.numpy as jnp
from jax import lax

HEADS = 20
HD = 128
TXT = 512
HW = 2560
PATCH_TOK = 64
TOKENS = 256
N_PATCH = 4


def keys_table(key, row_count):
    columns = HEADS * HD
    return 1.5 * jax.random.truncated_normal(key, -4.0, 4.0, (2, row_count, columns), jnp.float32)


def query_table(key, row_count):
    columns = HEADS * HD
    return 1.5 * jax.random.truncated_normal(key, -4.0, 4.0, (2, row_count, columns), jnp.float32)


def draw_stale_key(key, part):
    return keys_table(jax.random.fold_in(key, 11), TOKENS).astype(jnp.bfloat16)


def draw_text_key(key, part):
    return keys_table(jax.random.fold_in(key, 13), TXT).astype(jnp.bfloat16)


def draw_fresh_query(key, part):
    return query_table(jax.random.fold_in(key, 17), TOKENS).astype(jnp.bfloat16)


def draw_cross_query(key, part):
    return query_table(jax.random.fold_in(key, 19), TOKENS).astype(jnp.bfloat16)


def draw_text_mask(key, part):
    lowest = max(2, TXT // 16)
    partial_length = jax.random.randint(jax.random.fold_in(key, 31), (), lowest, TXT)
    full_branch = jax.random.randint(jax.random.fold_in(key, 37), (), 0, 2)
    lengths = jnp.where(jnp.arange(2) == full_branch, TXT, partial_length)
    return (jnp.arange(TXT)[None, :] < lengths[:, None]).astype(jnp.int32)


def steps_of(stream_key, dims, split, smallest, top_value):
    factor_of = 1.0
    for dim, shards_of in split:
        draws = jax.random.uniform(jax.random.fold_in(jax.random.fold_in(stream_key, 6), dim), (shards_of,), jnp.float32, smallest / len(split), top_value / len(split))
        factor_of = factor_of * jnp.repeat(jnp.exp(draws), dims[dim] // shards_of).reshape((-1,) + (1,) * (len(dims) - 1 - dim))
    return factor_of


def bell_draw(stream_key, dims, deviation, limit, split=(), kind=jnp.bfloat16):
    array = jax.random.normal(stream_key, dims, jnp.float32) * deviation
    if len(split) > 0:
        array = steps_of(stream_key, dims, split, -0.22, 0.18) * array
    return jnp.clip(array, min=-limit, max=limit).astype(kind)


def setup_inputs(seed: int = 0, part: int = 0) -> dict:
    keys = jax.random.split(jax.random.key(seed), 10)
    part_keys = jax.random.split(jax.random.fold_in(keys[9], part), 10)
    return {
        "fresh_query": draw_fresh_query(jax.random.fold_in(jax.random.fold_in(keys[9], part), 71), part),
        "fresh_key": bell_draw(part_keys[1], (2, TOKENS, HW), 1.5, 9.0, ((0, 2), (1, 8))),
        "fresh_value": bell_draw(part_keys[2], (2, TOKENS, HW), 2.0, 12.0, ((0, 2), (1, 8))),
        "stale_key": draw_stale_key(jax.random.fold_in(jax.random.fold_in(keys[9], part), 71), part),
        "stale_value": bell_draw(part_keys[4], (2, TOKENS, HW), 2.0, 12.0, ((0, 2), (1, 4), (2, 2))),
        "cross_query": draw_cross_query(jax.random.fold_in(jax.random.fold_in(keys[9], part), 71), part),
        "text_key": draw_text_key(jax.random.fold_in(jax.random.fold_in(keys[9], part), 71), part),
        "text_value": bell_draw(part_keys[7], (2, TXT, HW), 2.0, 12.0, ((0, 2), (2, 2))),
        "text_mask": draw_text_mask(jax.random.fold_in(jax.random.fold_in(keys[9], part), 71), part),
    }


def softmax_mix(queries, all_keys, all_values, usable):
    head_queries = queries.reshape(queries.shape[0], HEADS, HD).astype(jnp.float32)
    head_keys = all_keys.reshape(all_keys.shape[0], HEADS, HD).astype(jnp.float32)
    head_values = all_values.reshape(all_values.shape[0], HEADS, HD).astype(jnp.float32)
    scores = jnp.einsum('qhd,khd->qhk', head_queries, head_keys) * (1.0 / math.sqrt(HD))
    if usable is None:
        row_top = lax.optimization_barrier(jnp.max(scores, axis=-1, keepdims=True))
        weights = jnp.exp(scores - row_top)
    else:
        row_top = lax.optimization_barrier(jnp.max(jnp.where(usable, scores, -jnp.inf), axis=-1, keepdims=True))
        weights = jnp.where(usable, jnp.exp(jnp.where(usable, scores, row_top) - row_top), 0.0)
    totals = lax.optimization_barrier(jnp.sum(weights, axis=-1, keepdims=True))
    rounded = lax.optimization_barrier(weights.astype(jnp.bfloat16)).astype(jnp.float32)
    mixture = jnp.einsum('qhk,khd->qhd', rounded, head_values) / totals
    return mixture.reshape(queries.shape[0], HEADS * HD).astype(jnp.bfloat16)

def self_branch(queries, keys_new, values_new, keys_old, values_old):

    def one_patch(patch_index):
        offset = patch_index * PATCH_TOK
        all_keys = lax.dynamic_update_slice(keys_old, lax.dynamic_slice_in_dim(keys_new, offset, PATCH_TOK, 0), (offset, jnp.int32(0)))
        all_values = lax.dynamic_update_slice(values_old, lax.dynamic_slice_in_dim(values_new, offset, PATCH_TOK, 0), (offset, jnp.int32(0)))
        return softmax_mix(lax.dynamic_slice_in_dim(queries, offset, PATCH_TOK, 0), all_keys, all_values, None)
    blocks = lax.map(one_patch, jnp.arange(N_PATCH, dtype=jnp.int32))
    return blocks.reshape(TOKENS, HEADS * HD)

def cross_branch(queries, text_keys, text_values, mask_row):
    usable = (mask_row > 0)[None, None, :]

    def one_patch(patch_index):
        offset = patch_index * PATCH_TOK
        return softmax_mix(lax.dynamic_slice_in_dim(queries, offset, PATCH_TOK, 0), text_keys, text_values, usable)
    blocks = lax.map(one_patch, jnp.arange(N_PATCH, dtype=jnp.int32))
    return blocks.reshape(TOKENS, HEADS * HD)

def reference(fresh_query, fresh_key, fresh_value, stale_key, stale_value, cross_query, text_key, text_value, text_mask):
    self_parts = []
    cross_parts = []
    for branch in range(2):
        self_parts.append(self_branch(fresh_query[branch], fresh_key[branch], fresh_value[branch], stale_key[branch], stale_value[branch]))
        cross_parts.append(cross_branch(cross_query[branch], text_key[branch], text_value[branch], text_mask[branch]))
    return (jnp.stack(self_parts), jnp.stack(cross_parts))
```

```python
import math

import jax
import jax.numpy as jnp
from jax import lax
from jax.experimental import pallas as pl
from jax.experimental.pallas import tpu as pltpu
from jax.sharding import PartitionSpec as P

HD = 128
SCALE = 1.0 / math.sqrt(HD)


def attend(queries, keys, values, usable):
    scores = lax.dot_general(
        queries, keys, (((1,), (1,)), ((), ())), preferred_element_type=jnp.float32
    ) * SCALE
    if usable is not None:
        scores = jnp.where(usable, scores, -jnp.inf)
    weights = jnp.exp(scores - jnp.max(scores, axis=-1, keepdims=True))
    totals = jnp.sum(weights, axis=-1, keepdims=True)
    mixture = lax.dot_general(
        weights.astype(jnp.bfloat16),
        values,
        (((1,), (0,)), ((), ())),
        preferred_element_type=jnp.float32,
    )
    return (mixture / totals).astype(jnp.bfloat16)


def pack_kernel(shards, *refs):
    sources, target = refs[:-1], refs[-1]
    cols = target.shape[-1]
    me = lax.axis_index("head")
    for shift in range(1, shards):
        start = pl.multiple_of(lax.rem(me + shift, shards) * cols, HD)
        for index, source in enumerate(sources):
            target[shift - 1, index] = source[0, :, pl.ds(start, cols)]


def own_columns(ref, cols):
    start = pl.multiple_of(lax.axis_index("head") * cols, HD)
    return ref[0, :, pl.ds(start, cols)]


def rows_of(own, arrived, index, lanes):
    pieces = [own[:, lanes]]
    for ref in arrived:
        pieces.append(ref[index, :, lanes])
    return pieces


def cross_kernel(shards, query_ref, *refs):
    arrived = refs[: shards - 1]
    key_ref, value_ref, mask_ref, own_ref = refs[shards - 1 : shards + 3]
    away = refs[shards + 3 :]
    rows, cols = own_ref.shape
    usable = mask_ref[...] > 0
    own = own_columns(query_ref, cols)
    for head in range(cols // HD):
        lanes = slice(head * HD, (head + 1) * HD)
        queries = jnp.concatenate(rows_of(own, arrived, 3, lanes), axis=0)
        mixed = attend(queries, key_ref[0, :, lanes], value_ref[0, :, lanes], usable)
        own_ref[:, lanes] = mixed[:rows]
        for shift in range(1, shards):
            away[shift - 1][:, lanes] = mixed[shift * rows : (shift + 1) * rows]


def self_kernel(shards, patches, query_ref, fresh_key, fresh_value, *refs):
    arrived = refs[: shards - 1]
    stale_keys = refs[shards - 1 : shards + patches - 2]
    stale_values = refs[shards + patches - 2 : shards + 2 * patches - 3]
    own_ref = refs[shards + 2 * patches - 2]
    away = refs[shards + 2 * patches - 1 :]
    rows, cols = own_ref.shape
    own_q = own_columns(query_ref, cols)
    own_k = own_columns(fresh_key, cols)
    own_v = own_columns(fresh_value, cols)
    for head in range(cols // HD):
        lanes = slice(head * HD, (head + 1) * HD)
        queries = jnp.concatenate(rows_of(own_q, arrived, 0, lanes), axis=0)
        keys = rows_of(own_k, arrived, 1, lanes) + [ref[0, :, lanes] for ref in stale_keys]
        values = rows_of(own_v, arrived, 2, lanes) + [ref[0, :, lanes] for ref in stale_values]
        mixed = attend(
            queries, jnp.concatenate(keys, axis=0), jnp.concatenate(values, axis=0), None
        )
        own_ref[:, lanes] = mixed[:rows]
        for shift in range(1, shards):
            away[shift - 1][:, lanes] = mixed[shift * rows : (shift + 1) * rows]


def place_kernel(shards, own_ref, *refs):
    arrived, target = refs[:-1], refs[-1]
    cols = own_ref.shape[-1]
    me = lax.axis_index("head")
    for shift, ref in enumerate((own_ref, *arrived)):
        start = pl.multiple_of(lax.rem(me + shift, shards) * cols, HD)
        target[0, :, pl.ds(start, cols)] = ref[...]


def solution(mesh):
    shards = mesh.shape["head"]
    patches = mesh.shape["patch"]
    params = pltpu.CompilerParams(vmem_limit_bytes=48 * 1024 * 1024)

    vmem = pl.BlockSpec(memory_space=pltpu.VMEM)

    def shifted(array, axis, size, shift):
        return lax.ppermute(array, axis, [(i, (i + shift) % size) for i in range(size)])

    def per_device(
        fresh_query,
        fresh_key,
        fresh_value,
        stale_key,
        stale_value,
        cross_query,
        text_key,
        text_value,
        text_mask,
    ):
        rows, width = fresh_query.shape[1:]
        cols = width // shards
        kind = fresh_query.dtype
        block = jax.ShapeDtypeStruct((rows, cols), kind)

        stale_keys = [shifted(stale_key, "patch", patches, s) for s in range(1, patches)]
        stale_values = [shifted(stale_value, "patch", patches, s) for s in range(1, patches)]

        packed = pl.pallas_call(
            lambda *refs: pack_kernel(shards, *refs),
            out_shape=jax.ShapeDtypeStruct((shards - 1, 4, rows, cols), kind),
            compiler_params=params,
            name="pack",
        )(fresh_query, fresh_key, fresh_value, cross_query)
        arrived = [shifted(packed[s - 1], "head", shards, s) for s in range(1, shards)]

        cross_own, *cross_away = pl.pallas_call(
            lambda *refs: cross_kernel(shards, *refs),
            out_shape=[block] * shards,
            compiler_params=params,
            name="cross",
        )(cross_query, *arrived, text_key, text_value, text_mask)
        cross_back = [shifted(a, "head", shards, -s - 1) for s, a in enumerate(cross_away)]

        place = pl.pallas_call(
            lambda *refs: place_kernel(shards, *refs),
            out_shape=jax.ShapeDtypeStruct((1, rows, width), kind),
            compiler_params=params,
            name="place",
        )
        cross_mixed = place(cross_own, *cross_back)

        self_own, *self_away = pl.pallas_call(
            lambda *refs: self_kernel(shards, patches, *refs),
            out_shape=[block] * shards,
            in_specs=[vmem] * (shards + 2 * patches) + [pl.BlockSpec(memory_space=pl.ANY)],
            compiler_params=params,
            name="self",
        )(fresh_query, fresh_key, fresh_value, *arrived, *stale_keys, *stale_values, cross_own)
        self_back = [shifted(a, "head", shards, -s - 1) for s, a in enumerate(self_away)]
        return (place(self_own, *self_back), cross_mixed)

    token = P(("group", "cfg"), ("patch", "head"), None)
    stale = P(("group", "cfg"), "patch", "head")
    text = P(("group", "cfg"), None, "head")
    return jax.shard_map(
        per_device,
        mesh=mesh,
        in_specs=(token, token, token, stale, stale, token, text, text, P(("group", "cfg"), None)),
        out_specs=(token, token),
        check_vma=False,
    )
```

```python
import math

import jax
import jax.numpy as jnp
from jax import lax
from jax.experimental import pallas as pl
from jax.experimental.pallas import tpu as pltpu
from jax.sharding import PartitionSpec as P

HD = 128
SCALE = 1.0 / math.sqrt(HD)
QUERY, KEY, VALUE, CROSS = range(4)


def scores_of(queries, keys):
    return lax.dot_general(
        queries, keys, (((1,), (1,)), ((), ())), preferred_element_type=jnp.float32
    ) * SCALE


def weighted(weights, values):
    return lax.dot_general(
        weights.astype(jnp.bfloat16),
        values,
        (((1,), (0,)), ((), ())),
        preferred_element_type=jnp.float32,
    )


def columns_of(ref, owner, cols):
    return ref.at[0, :, pl.ds(pl.multiple_of(owner * cols, HD), cols)]


def run_all(copies):
    for copy in copies:
        copy.start()
    for copy in copies:
        copy.wait()


def pack_kernel(shards, *refs):
    sources, own, away, sems = refs[:4], refs[4], refs[5], refs[6]
    cols = own.shape[-1]
    me = lax.axis_index("head")
    copies = []
    for shift in range(shards):
        owner = lax.rem(me + shift, shards)
        for index, source in enumerate(sources):
            target = own.at[index] if shift == 0 else away.at[shift - 1, index]
            copies.append(
                pltpu.make_async_copy(
                    columns_of(source, owner, cols), target, sems.at[shift, index]
                )
            )
    run_all(copies)


def place_kernel(shards, own_ref, *refs):
    arrived, target, sems = refs[:-2], refs[-2], refs[-1]
    cols = own_ref.shape[-1]
    me = lax.axis_index("head")
    run_all(
        [
            pltpu.make_async_copy(
                ref, columns_of(target, lax.rem(me + shift, shards), cols), sems.at[shift]
            )
            for shift, ref in enumerate((own_ref, *arrived))
        ]
    )


def rows_of(own, arrived, index, lanes):
    return [ref[index, :, lanes] for ref in (own, *arrived)]


def spread(mixed, targets, lanes):
    rows = targets[0].shape[0]
    for place, target in enumerate(targets):
        target[:, lanes] = mixed[place * rows : (place + 1) * rows].astype(target.dtype)


def cross_kernel(shards, own, *refs):
    arrived = refs[: shards - 1]
    text_key, text_value, mask_ref = refs[shards - 1 : shards + 2]
    targets = refs[shards + 2 : 2 * shards + 2]
    key_ref, value_ref, sems = refs[2 * shards + 2 :]
    cols = targets[0].shape[-1]
    copies = []
    for head in range(cols // HD):
        lanes = pl.ds(head * HD, HD)
        pair = [
            pltpu.make_async_copy(
                source.at[0, :, lanes], target.at[:, lanes], sems.at[index, head]
            )
            for index, (source, target) in enumerate(
                ((text_key, key_ref), (text_value, value_ref))
            )
        ]
        for copy in pair:
            copy.start()
        copies.append(pair)
    usable = mask_ref[...] > 0
    for head in range(cols // HD):
        lanes = slice(head * HD, (head + 1) * HD)
        queries = jnp.concatenate(rows_of(own, arrived, CROSS, lanes), axis=0)
        copies[head][0].wait()
        scores = jnp.where(usable, scores_of(queries, key_ref[:, lanes]), -jnp.inf)
        weights = jnp.exp(scores - jnp.max(scores, axis=-1, keepdims=True))
        totals = jnp.sum(weights, axis=-1, keepdims=True)
        copies[head][1].wait()
        spread(weighted(weights, value_ref[:, lanes]) / totals, targets, lanes)


def first_kernel(shards, pieces, own, *refs):
    arrived = refs[: shards - 1]
    keys = refs[shards - 1 : shards - 1 + pieces]
    values = refs[shards - 1 + pieces : shards - 1 + 2 * pieces]
    sums_ref, tops_ref, totals_ref = refs[shards + 2 * pieces - 1 :]
    cols = own.shape[-1]
    for head in range(cols // HD):
        lanes = slice(head * HD, (head + 1) * HD)
        queries = jnp.concatenate(rows_of(own, arrived, QUERY, lanes), axis=0)
        head_keys = rows_of(own, arrived, KEY, lanes) + [ref[0, :, lanes] for ref in keys]
        head_values = rows_of(own, arrived, VALUE, lanes) + [ref[0, :, lanes] for ref in values]
        scores = scores_of(queries, jnp.concatenate(head_keys, axis=0))
        tops = jnp.max(scores, axis=-1, keepdims=True)
        weights = jnp.exp(scores - tops)
        sums_ref[:, lanes] = weighted(weights, jnp.concatenate(head_values, axis=0))
        tops_ref[:, head : head + 1] = tops
        totals_ref[:, head : head + 1] = jnp.sum(weights, axis=-1, keepdims=True)


def last_kernel(shards, own, *refs):
    arrived = refs[: shards - 1]
    key_ref, value_ref, sums_ref, tops_ref, totals_ref = refs[shards - 1 : shards + 4]
    targets = refs[shards + 4 :]
    cols = own.shape[-1]
    for head in range(cols // HD):
        lanes = slice(head * HD, (head + 1) * HD)
        queries = jnp.concatenate(rows_of(own, arrived, QUERY, lanes), axis=0)
        scores = scores_of(queries, key_ref[0, :, lanes])
        old_tops = tops_ref[:, head : head + 1]
        tops = jnp.maximum(old_tops, jnp.max(scores, axis=-1, keepdims=True))
        weights = jnp.exp(scores - tops)
        factor = jnp.exp(old_tops - tops)
        totals = totals_ref[:, head : head + 1] * factor + jnp.sum(
            weights, axis=-1, keepdims=True
        )
        sums = sums_ref[:, lanes] * factor + weighted(weights, value_ref[0, :, lanes])
        spread(sums / totals, targets, lanes)


def solution(mesh):
    shards = mesh.shape["head"]
    patches = mesh.shape["patch"]
    ring = list(range(0, patches, 2)) + list(range(1, patches, 2))[::-1]
    ring_pairs = list(zip(ring, ring[1:] + ring[:1]))
    vmem = pl.BlockSpec(memory_space=pltpu.VMEM)
    hbm = pl.BlockSpec(memory_space=pltpu.HBM)

    def params(mib):
        return pltpu.CompilerParams(vmem_limit_bytes=mib * 1024 * 1024)

    def over_head(array, shift):
        pairs = [(i, (i + shift) % shards) for i in range(shards)]
        return lax.ppermute(array, "head", pairs)

    def onward(array):
        return lax.ppermute(array, "patch", ring_pairs)

    def per_device(
        fresh_query,
        fresh_key,
        fresh_value,
        stale_key,
        stale_value,
        cross_query,
        text_key,
        text_value,
        text_mask,
    ):
        rows, width = fresh_query.shape[1:]
        text_rows = text_key.shape[1]
        cols = width // shards
        heads = cols // HD
        kind = fresh_query.dtype
        everyone = rows * shards
        block = jax.ShapeDtypeStruct((rows, cols), kind)
        state = [
            jax.ShapeDtypeStruct((everyone, cols), jnp.float32),
            jax.ShapeDtypeStruct((everyone, HD), jnp.float32),
            jax.ShapeDtypeStruct((everyone, HD), jnp.float32),
        ]

        keys, values = [stale_key], [stale_value]
        for _ in range(patches - 1):
            keys.append(onward(keys[-1]))
            values.append(onward(values[-1]))

        own, away = pl.pallas_call(
            lambda *refs: pack_kernel(shards, *refs),
            out_shape=[
                jax.ShapeDtypeStruct((4, rows, cols), kind),
                jax.ShapeDtypeStruct((shards - 1, 4, rows, cols), kind),
            ],
            in_specs=[hbm] * 4,
            out_specs=[vmem] * 2,
            scratch_shapes=[pltpu.SemaphoreType.DMA((shards, 4))],
            compiler_params=params(62),
            name="pack",
        )(fresh_query, fresh_key, fresh_value, cross_query)
        arrived = [over_head(away[s - 1], s) for s in range(1, shards)]

        cross_own, *cross_away = pl.pallas_call(
            lambda *refs: cross_kernel(shards, *refs),
            out_shape=[block] * shards,
            in_specs=[vmem] * shards + [hbm] * 2 + [vmem],
            out_specs=[vmem] * shards,
            scratch_shapes=[
                pltpu.VMEM((text_rows, cols), kind),
                pltpu.VMEM((text_rows, cols), kind),
                pltpu.SemaphoreType.DMA((2, heads)),
            ],
            compiler_params=params(62),
            cost_estimate=pl.CostEstimate(
                flops=4 * everyone * text_rows * cols,
                bytes_accessed=4 * text_rows * cols * 3,
                transcendentals=everyone * text_rows * heads,
            ),
            name="cross",
        )(own, *arrived, text_key, text_value, text_mask)
        cross_back = [over_head(a, -s - 1) for s, a in enumerate(cross_away)]

        place = pl.pallas_call(
            lambda *refs: place_kernel(shards, *refs),
            out_shape=jax.ShapeDtypeStruct((1, rows, width), kind),
            in_specs=[vmem] * shards,
            out_specs=hbm,
            scratch_shapes=[pltpu.SemaphoreType.DMA((shards,))],
            compiler_params=params(16),
            name="place",
        )
        cross_mixed = place(cross_own, *cross_back)

        early_keys, early_values = keys[1:-1], values[1:-1]
        pieces = len(early_keys)
        sums, tops, totals = pl.pallas_call(
            lambda *refs: first_kernel(shards, pieces, *refs),
            out_shape=state,
            in_specs=[vmem] * (shards + 2 * pieces),
            out_specs=[vmem] * 3,
            compiler_params=params(32),
            cost_estimate=pl.CostEstimate(
                flops=4 * everyone * everyone * (pieces + 1) * cols,
                bytes_accessed=4 * everyone * cols * (pieces + 2),
                transcendentals=everyone * everyone * (pieces + 1) * heads,
            ),
            name="first",
        )(own, *arrived, *early_keys, *early_values)
        self_own, *self_away = pl.pallas_call(
            lambda *refs: last_kernel(shards, *refs),
            out_shape=[block] * shards,
            in_specs=[vmem] * (shards + 5),
            out_specs=[vmem] * shards,
            compiler_params=params(32),
            name="last",
        )(own, *arrived, keys[-1], values[-1], sums, tops, totals)
        self_back = [over_head(a, -s - 1) for s, a in enumerate(self_away)]
        return (place(self_own, *self_back), cross_mixed)

    token = P(("group", "cfg"), ("patch", "head"), None)
    stale = P(("group", "cfg"), "patch", "head")
    text = P(("group", "cfg"), None, "head")
    return jax.shard_map(
        per_device,
        mesh=mesh,
        in_specs=(token, token, token, stale, stale, token, text, text, P(("group", "cfg"), None)),
        out_specs=(token, token),
        check_vma=False,
    )
```

```python
import math

import jax
import jax.numpy as jnp
from jax import lax
from jax.experimental import pallas as pl
from jax.experimental.pallas import tpu as pltpu
from jax.sharding import PartitionSpec as P

HD = 128
SCALE = 1.0 / math.sqrt(HD)
QUERY, KEY, VALUE, CROSS = range(4)


def scores_of(queries, keys):
    return lax.dot_general(
        queries, keys, (((1,), (1,)), ((), ())), preferred_element_type=jnp.float32
    ) * SCALE


def weighted(weights, values):
    return lax.dot_general(
        weights.astype(values.dtype),
        values,
        (((1,), (0,)), ((), ())),
        preferred_element_type=jnp.float32,
    )


def columns_of(ref, owner, cols):
    return ref.at[0, :, pl.ds(pl.multiple_of(owner * cols, HD), cols)]


def run_all(copies):
    for copy in copies:
        copy.start()
    for copy in copies:
        copy.wait()


def pack_kernel(shards, *refs):
    sources, (own, own_cross, away, away_cross, sems) = refs[:4], refs[4:]
    cols = own.shape[-1]
    me = lax.axis_index("head")
    copies = []
    for shift in range(shards):
        owner = lax.rem(me + shift, shards)
        targets = (own, own_cross) if shift == 0 else (away.at[shift - 1], away_cross.at[shift - 1])
        for index, source in enumerate(sources):
            target = targets[1] if index == CROSS else targets[0].at[index]
            copies.append(
                pltpu.make_async_copy(
                    columns_of(source, owner, cols), target, sems.at[shift, index]
                )
            )
    run_all(copies)


def place_kernel(shards, own_ref, *refs):
    arrived, target, sems = refs[:-2], refs[-2], refs[-1]
    cols = own_ref.shape[-1]
    me = lax.axis_index("head")
    run_all(
        [
            pltpu.make_async_copy(
                ref, columns_of(target, lax.rem(me + shift, shards), cols), sems.at[shift]
            )
            for shift, ref in enumerate((own_ref, *arrived))
        ]
    )


def rows_of(own, arrived, index, lanes):
    return [ref[index, :, lanes] for ref in (own, *arrived)]


def cross_kernel(shards, own, *refs):
    arrived = refs[: shards - 1]
    text_key, text_value, mask_ref = refs[shards - 1 : shards + 2]
    targets = refs[shards + 2 : 2 * shards + 2]
    key_ref, value_ref, sems = refs[2 * shards + 2 :]
    text_rows, cols = key_ref.shape
    step = math.gcd(text_rows, HD)
    copies = [
        [
            pltpu.make_async_copy(
                source.at[0, pl.ds(start, step)],
                target.at[pl.ds(start, step)],
                sems.at[index, start // step],
            )
            for start in range(0, text_rows, step)
        ]
        for index, (source, target) in enumerate(((text_key, key_ref), (text_value, value_ref)))
    ]
    for copy in copies[0] + copies[1]:
        copy.start()
    usable = mask_ref[...] > 0
    for copy in copies[0]:
        copy.wait()
    for head in range(cols // HD):
        lanes = slice(head * HD, (head + 1) * HD)
        queries = jnp.concatenate([ref[:, lanes] for ref in (own, *arrived)], axis=0)
        scores = jnp.where(usable, scores_of(queries, key_ref[:, lanes]), -jnp.inf)
        weights = jnp.exp(scores - jnp.max(scores, axis=-1, keepdims=True))
        totals = jnp.sum(weights, axis=-1, keepdims=True)
        if head == 0:
            for copy in copies[1]:
                copy.wait()
        mixed = weighted(weights, value_ref[:, lanes]) / totals
        rows = targets[0].shape[0]
        for place, target in enumerate(targets):
            target[:, lanes] = mixed[place * rows : (place + 1) * rows].astype(target.dtype)


def weights_kernel(shards, pieces, own, *refs):
    arrived = refs[: shards - 1]
    keys = refs[shards - 1 : shards - 1 + pieces]
    targets = refs[shards - 1 + pieces :]
    rows, cols = own.shape[1:]
    for head in range(cols // HD):
        lanes = slice(head * HD, (head + 1) * HD)
        queries = jnp.concatenate(rows_of(own, arrived, QUERY, lanes), axis=0)
        head_keys = rows_of(own, arrived, KEY, lanes) + [ref[0, :, lanes] for ref in keys]
        scores = scores_of(queries, jnp.concatenate(head_keys, axis=0))
        weights = jnp.exp(scores - jnp.max(scores, axis=-1, keepdims=True))
        weights = weights * (1.0 / jnp.sum(weights, axis=-1, keepdims=True))
        for place, target in enumerate(targets):
            target[head] = weights[place * rows : (place + 1) * rows].astype(target.dtype)


def mix_kernel(shards, weights_ref, own, *refs):
    arrived, values, target = refs[: shards - 1], refs[shards - 1 : -1], refs[-1]
    for head in range(target.shape[-1] // HD):
        lanes = slice(head * HD, (head + 1) * HD)
        head_values = rows_of(own, arrived, VALUE, lanes) + [ref[0, :, lanes] for ref in values]
        mixed = weighted(weights_ref[head], jnp.concatenate(head_values, axis=0))
        target[:, lanes] = mixed.astype(target.dtype)


def gate_kernel(*refs):
    pass


def solution(mesh):
    shards = mesh.shape["head"]
    patches = mesh.shape["patch"]
    ring = list(range(0, patches, 2)) + list(range(1, patches, 2))[::-1]
    ring_pairs = list(zip(ring, ring[1:] + ring[:1]))
    vmem = pl.BlockSpec(memory_space=pltpu.VMEM)
    hbm = pl.BlockSpec(memory_space=pltpu.HBM)

    def params(mib):
        return pltpu.CompilerParams(vmem_limit_bytes=mib * 1024 * 1024)

    def over_head(array, shift):
        pairs = [(i, (i + shift) % shards) for i in range(shards)]
        return lax.ppermute(array, "head", pairs)

    def onward(array):
        return lax.ppermute(array, "patch", ring_pairs)

    def behind(array, *others):
        return pl.pallas_call(
            gate_kernel,
            out_shape=jax.ShapeDtypeStruct(array.shape, array.dtype),
            in_specs=[hbm] * (1 + len(others)),
            out_specs=hbm,
            input_output_aliases={0: 0},
            compiler_params=params(16),
            name="gate",
        )(array, *others)

    def per_device(
        fresh_query,
        fresh_key,
        fresh_value,
        stale_key,
        stale_value,
        cross_query,
        text_key,
        text_value,
        text_mask,
    ):
        rows, width = fresh_query.shape[1:]
        text_rows = text_key.shape[1]
        cols = width // shards
        heads = cols // HD
        kind = fresh_query.dtype
        everyone = rows * shards
        block = jax.ShapeDtypeStruct((rows, cols), kind)

        own, own_cross, away, away_cross = pl.pallas_call(
            lambda *refs: pack_kernel(shards, *refs),
            out_shape=[
                jax.ShapeDtypeStruct((3, rows, cols), kind),
                jax.ShapeDtypeStruct((rows, cols), kind),
                jax.ShapeDtypeStruct((shards - 1, 3, rows, cols), kind),
                jax.ShapeDtypeStruct((shards - 1, rows, cols), kind),
            ],
            in_specs=[hbm] * 4,
            out_specs=[hbm] * 4,
            scratch_shapes=[pltpu.SemaphoreType.DMA((shards, 4))],
            compiler_params=params(62),
            name="pack",
        )(fresh_query, fresh_key, fresh_value, cross_query)
        arrived = [over_head(away[s - 1], s) for s in range(1, shards)]
        arrived_cross = [over_head(away_cross[s - 1], s) for s in range(1, shards)]

        keys, values = [stale_key], [stale_value]
        for step in range(patches - 2):
            keys.append(onward(keys[-1]))
            values.append(onward(values[-1]))
            if step == 0:
                keys[-1] = behind(keys[-1], *arrived_cross)

        cross_own, *cross_away = pl.pallas_call(
            lambda *refs: cross_kernel(shards, *refs),
            out_shape=[block] * shards,
            in_specs=[vmem] * shards + [hbm] * 2 + [vmem],
            out_specs=[vmem] * shards,
            scratch_shapes=[
                pltpu.VMEM((text_rows, cols), kind),
                pltpu.VMEM((text_rows, cols), kind),
                pltpu.SemaphoreType.DMA((2, text_rows // math.gcd(text_rows, HD))),
            ],
            compiler_params=params(58),
            cost_estimate=pl.CostEstimate(
                flops=4 * everyone * text_rows * cols,
                bytes_accessed=4 * text_rows * cols * 3,
                transcendentals=everyone * text_rows * heads,
            ),
            name="cross",
        )(own_cross, *arrived_cross, text_key, text_value, text_mask)
        cross_back = [over_head(a, -s - 1) for s, a in enumerate(cross_away)]

        place = pl.pallas_call(
            lambda *refs: place_kernel(shards, *refs),
            out_shape=jax.ShapeDtypeStruct((1, rows, width), kind),
            in_specs=[vmem] * shards,
            out_specs=hbm,
            scratch_shapes=[pltpu.SemaphoreType.DMA((shards,))],
            compiler_params=params(16),
            name="place",
        )
        cross_mixed = place(cross_own, *cross_back)

        keys[-1] = behind(keys[-1], cross_own)
        keys.append(onward(keys[-1]))
        values.append(onward(values[-1]))

        pieces = patches - 1
        seen = everyone * patches
        own_weights, *away_weights = pl.pallas_call(
            lambda *refs: weights_kernel(shards, pieces, *refs),
            out_shape=[jax.ShapeDtypeStruct((heads, rows, seen), kind)] * shards,
            in_specs=[vmem] * (shards + pieces),
            out_specs=[vmem] * shards,
            compiler_params=params(32),
            cost_estimate=pl.CostEstimate(
                flops=2 * everyone * seen * cols,
                bytes_accessed=2 * seen * cols,
                transcendentals=everyone * seen * heads,
            ),
            name="weights",
        )(own, *arrived, *keys[1:])
        mix = pl.pallas_call(
            lambda *refs: mix_kernel(shards, *refs),
            out_shape=block,
            in_specs=[vmem] * (1 + shards + pieces),
            out_specs=vmem,
            compiler_params=params(32),
            name="mix",
        )
        self_back = [
            over_head(mix(share, own, *arrived, *values[1:]), -s - 1)
            for s, share in enumerate(away_weights)
        ]
        self_own = mix(own_weights, own, *arrived, *values[1:])
        return (place(self_own, *self_back), cross_mixed)

    token = P(("group", "cfg"), ("patch", "head"), None)
    stale = P(("group", "cfg"), "patch", "head")
    text = P(("group", "cfg"), None, "head")
    return jax.shard_map(
        per_device,
        mesh=mesh,
        in_specs=(token, token, token, stale, stale, token, text, text, P(("group", "cfg"), None)),
        out_specs=(token, token),
        check_vma=False,
    )
```

```python
import math

import jax
import jax.numpy as jnp
from jax import lax
from jax.experimental import pallas as pl
from jax.experimental.pallas import tpu as pltpu
from jax.sharding import PartitionSpec as P

HD = 128
SCALE = 1.0 / math.sqrt(HD)
QUERY, KEY, VALUE, CROSS = range(4)


def scores_of(queries, keys):
    return lax.dot_general(
        queries, keys, (((1,), (1,)), ((), ())), preferred_element_type=jnp.float32
    ) * SCALE


def weighted(weights, values):
    return lax.dot_general(
        weights, values, (((1,), (0,)), ((), ())), preferred_element_type=jnp.float32
    )


def softmax_parts(scores):
    weights = jnp.exp(scores - jnp.max(scores, axis=-1, keepdims=True))
    totals = jnp.sum(weights, axis=-1, keepdims=True)
    shares = jnp.broadcast_to(1.0 / totals, (scores.shape[0], HD))
    return weights.astype(jnp.bfloat16), shares


def columns_of(ref, owner, cols):
    return ref.at[0, :, pl.ds(pl.multiple_of(owner * cols, HD), cols)]


def run_all(copies):
    for copy in copies:
        copy.start()
    for copy in copies:
        copy.wait()


def pack_kernel(shards, *refs):
    sources, (own, own_cross, away, away_cross, sems) = refs[:4], refs[4:]
    cols = own.shape[-1]
    me = lax.axis_index("head")
    copies = []
    for shift in range(shards):
        owner = lax.rem(me + shift, shards)
        targets = (own, own_cross) if shift == 0 else (away.at[shift - 1], away_cross.at[shift - 1])
        for index, source in enumerate(sources):
            target = targets[1] if index == CROSS else targets[0].at[index]
            copies.append(
                pltpu.make_async_copy(
                    columns_of(source, owner, cols), target, sems.at[shift, index]
                )
            )
    run_all(copies)


def load_kernel(*refs):
    half = len(refs) // 2
    run_all(
        [
            pltpu.make_async_copy(source, target, refs[-1].at[index])
            for index, (source, target) in enumerate(zip(refs[:half], refs[half:-1]))
        ]
    )


def place_kernel(shards, own_ref, *refs):
    arrived, target, sems = refs[:-2], refs[-2], refs[-1]
    cols = own_ref.shape[-1]
    me = lax.axis_index("head")
    run_all(
        [
            pltpu.make_async_copy(
                ref, columns_of(target, lax.rem(me + shift, shards), cols), sems.at[shift]
            )
            for shift, ref in enumerate((own_ref, *arrived))
        ]
    )


def gate_kernel(*refs):
    pass


def rows_of(own, arrived, index, lanes):
    return [ref[index, :, lanes] for ref in (own, *arrived)]


def cross_kernel(shards, own, *refs):
    arrived = refs[: shards - 1]
    key_ref, value_ref, mask_ref = refs[shards - 1 : shards + 2]
    targets = refs[shards + 2 : 2 * shards + 2]
    weights_ref, shares_ref = refs[2 * shards + 2 :]
    rows, cols = targets[0].shape
    usable = mask_ref[...] > 0
    for head in range(cols // HD):
        lanes = slice(head * HD, (head + 1) * HD)
        queries = jnp.concatenate([ref[:, lanes] for ref in (own, *arrived)], axis=0)
        scores = jnp.where(usable, scores_of(queries, key_ref[0, :, lanes]), -jnp.inf)
        weights_ref[head], shares_ref[head] = softmax_parts(scores)
    for head in range(cols // HD):
        lanes = slice(head * HD, (head + 1) * HD)
        mixed = weighted(weights_ref[head], value_ref[0, :, lanes]) * shares_ref[head]
        for place, target in enumerate(targets):
            target[:, lanes] = mixed[place * rows : (place + 1) * rows].astype(target.dtype)


def weights_kernel(shards, pieces, own, *refs):
    arrived = refs[: shards - 1]
    keys = refs[shards - 1 : shards - 1 + pieces]
    targets = refs[shards - 1 + pieces :]
    rows, cols = own.shape[1:]
    for head in range(cols // HD):
        lanes = slice(head * HD, (head + 1) * HD)
        queries = jnp.concatenate(rows_of(own, arrived, QUERY, lanes), axis=0)
        head_keys = rows_of(own, arrived, KEY, lanes) + [ref[0, :, lanes] for ref in keys]
        weights, shares = softmax_parts(scores_of(queries, jnp.concatenate(head_keys, axis=0)))
        for place in range(shards):
            targets[2 * place][head] = weights[place * rows : (place + 1) * rows]
            targets[2 * place + 1][head] = shares[place * rows : (place + 1) * rows]


def mix_kernel(shards, weights_ref, shares_ref, own, *refs):
    arrived, values, target = refs[: shards - 1], refs[shards - 1 : -1], refs[-1]
    for head in range(target.shape[-1] // HD):
        lanes = slice(head * HD, (head + 1) * HD)
        head_values = rows_of(own, arrived, VALUE, lanes) + [ref[0, :, lanes] for ref in values]
        mixed = weighted(weights_ref[head], jnp.concatenate(head_values, axis=0))
        target[:, lanes] = (mixed * shares_ref[head]).astype(target.dtype)


def solution(mesh):
    shards = mesh.shape["head"]
    patches = mesh.shape["patch"]
    ring = list(range(0, patches, 2)) + list(range(1, patches, 2))[::-1]
    ring_pairs = list(zip(ring, ring[1:] + ring[:1]))
    vmem = pl.BlockSpec(memory_space=pltpu.VMEM)
    hbm = pl.BlockSpec(memory_space=pltpu.HBM)
    anywhere = pl.BlockSpec(memory_space=pl.ANY)
    params = pltpu.CompilerParams(vmem_limit_bytes=32 * 1024 * 1024)

    def over_head(array, shift):
        pairs = [(i, (i + shift) % shards) for i in range(shards)]
        return lax.ppermute(array, "head", pairs)

    def onward(array):
        return lax.ppermute(array, "patch", ring_pairs)

    def in_hbm(*arrays):
        return [pltpu.with_memory_space_constraint(a, pltpu.HBM) for a in arrays]

    def behind(array, *others):
        return pl.pallas_call(
            gate_kernel,
            out_shape=jax.ShapeDtypeStruct(array.shape, array.dtype),
            in_specs=[anywhere] * (1 + len(others)),
            out_specs=anywhere,
            input_output_aliases={0: 0},
            compiler_params=params,
            name="gate",
        )(array, *others)

    def per_device(
        fresh_query,
        fresh_key,
        fresh_value,
        stale_key,
        stale_value,
        cross_query,
        text_key,
        text_value,
        text_mask,
    ):
        rows, width = fresh_query.shape[1:]
        text_rows = text_key.shape[1]
        cols = width // shards
        heads = cols // HD
        kind = fresh_query.dtype
        everyone = rows * shards
        block = jax.ShapeDtypeStruct((rows, cols), kind)

        own, own_cross, away, away_cross = pl.pallas_call(
            lambda *refs: pack_kernel(shards, *refs),
            out_shape=[
                pltpu.VMEM((3, rows, cols), kind),
                pltpu.VMEM((rows, cols), kind),
                pltpu.VMEM((shards - 1, 3, rows, cols), kind),
                pltpu.VMEM((shards - 1, rows, cols), kind),
            ],
            in_specs=[hbm] * 4,
            out_specs=[vmem] * 4,
            scratch_shapes=[pltpu.SemaphoreType.DMA((shards, 4))],
            compiler_params=params,
            name="pack",
        )(*in_hbm(fresh_query, fresh_key, fresh_value, cross_query))
        arrived = [over_head(away[s - 1], s) for s in range(1, shards)]
        arrived_cross = [over_head(away_cross[s - 1], s) for s in range(1, shards)]

        text = [text_key, text_value, text_mask]
        text = pl.pallas_call(
            load_kernel,
            out_shape=[pltpu.VMEM(a.shape, a.dtype) for a in text],
            in_specs=[hbm] * len(text),
            out_specs=[vmem] * len(text),
            scratch_shapes=[pltpu.SemaphoreType.DMA((len(text),))],
            compiler_params=params,
            name="load",
        )(*in_hbm(*text))

        keys, values = [stale_key], [stale_value]
        for step in range(patches - 2):
            keys.append(onward(keys[-1]))
            values.append(onward(values[-1]))
            if step == 0:
                keys[-1] = behind(keys[-1], *arrived_cross, text[-1])

        cross_own, *cross_away = pl.pallas_call(
            lambda *refs: cross_kernel(shards, *refs),
            out_shape=[block] * shards,
            in_specs=[vmem] * (shards + 3),
            out_specs=[vmem] * shards,
            scratch_shapes=[
                pltpu.VMEM((heads, everyone, text_rows), kind),
                pltpu.VMEM((heads, everyone, HD), jnp.float32),
            ],
            compiler_params=params,
            name="cross",
        )(own_cross, *arrived_cross, *text)
        cross_back = [over_head(a, -s - 1) for s, a in enumerate(cross_away)]

        place = pl.pallas_call(
            lambda *refs: place_kernel(shards, *refs),
            out_shape=jax.ShapeDtypeStruct((1, rows, width), kind),
            in_specs=[vmem] * shards,
            out_specs=hbm,
            scratch_shapes=[pltpu.SemaphoreType.DMA((shards,))],
            compiler_params=params,
            name="place",
        )
        cross_mixed = place(cross_own, *cross_back)

        keys[-1] = behind(keys[-1], cross_own)
        keys.append(onward(keys[-1]))
        values.append(onward(values[-1]))

        pieces = patches - 1
        seen = everyone * patches
        parts = pl.pallas_call(
            lambda *refs: weights_kernel(shards, pieces, *refs),
            out_shape=[
                jax.ShapeDtypeStruct((heads, rows, seen), kind),
                jax.ShapeDtypeStruct((heads, rows, HD), jnp.float32),
            ]
            * shards,
            in_specs=[vmem] * (shards + pieces),
            out_specs=[vmem] * (2 * shards),
            compiler_params=params,
            name="weights",
        )(own, *arrived, *keys[1:])
        mix = pl.pallas_call(
            lambda *refs: mix_kernel(shards, *refs),
            out_shape=block,
            in_specs=[vmem] * (2 + shards + pieces),
            out_specs=vmem,
            compiler_params=params,
            name="mix",
        )
        self_back = [
            over_head(mix(*parts[2 * s : 2 * s + 2], own, *arrived, *values[1:]), -s)
            for s in range(1, shards)
        ]
        self_own = mix(*parts[:2], own, *arrived, *values[1:])
        return (place(self_own, *self_back), cross_mixed)

    token = P(("group", "cfg"), ("patch", "head"), None)
    stale = P(("group", "cfg"), "patch", "head")
    text = P(("group", "cfg"), None, "head")
    return jax.shard_map(
        per_device,
        mesh=mesh,
        in_specs=(token, token, token, stale, stale, token, text, text, P(("group", "cfg"), None)),
        out_specs=(token, token),
        check_vma=False,
    )
```

```python
import math

import jax
import jax.numpy as jnp
from jax import lax
from jax.experimental import pallas as pl
from jax.experimental.pallas import tpu as pltpu
from jax.sharding import PartitionSpec as P

HD = 128
SCALE = 1.0 / math.sqrt(HD)


def scores_of(queries, keys):
    return lax.dot_general(
        queries, keys, (((1,), (1,)), ((), ())), preferred_element_type=jnp.float32
    ) * SCALE


def weighted(weights, values):
    return lax.dot_general(
        weights, values, (((1,), (0,)), ((), ())), preferred_element_type=jnp.float32
    )


def softmax_parts(scores):
    weights = jnp.exp(scores - jnp.max(scores, axis=-1, keepdims=True))
    totals = jnp.sum(weights, axis=-1, keepdims=True)
    shares = jnp.broadcast_to(1.0 / totals, (scores.shape[0], HD))
    return weights.astype(jnp.bfloat16), shares


def run_all(copies, sems):
    started = []
    for index, (source, target) in enumerate(copies):
        started.append(pltpu.make_async_copy(source, target, sems.at[index]))
        started[-1].start()
    for copy in started:
        copy.wait()


def load_kernel(*refs):
    half = len(refs) // 2
    run_all(zip(refs[:half], refs[half:-1]), refs[-1])


def gate_kernel(*refs):
    pass


def head_lanes(head):
    return slice(head * HD, (head + 1) * HD)


def cross_kernel(shards, share, own, *refs):
    arrived = refs[: shards - 1]
    key_ref, value_ref, mask_ref = refs[shards - 1 : shards + 2]
    targets = refs[shards + 2 : 2 * shards + 2]
    weights_ref, shares_ref = refs[2 * shards + 2 :]
    rows, cols = targets[0].shape
    width = cols // share
    usable = mask_ref[...] > 0
    for head in range(cols // HD):
        lanes = head_lanes(head)
        part, inner = divmod(head * HD, width)
        queries = [own[:, lanes]]
        for ref in arrived:
            start = ref.shape[0] - (share - part) * rows
            queries.append(ref[start : start + rows, inner : inner + HD])
        scores = scores_of(jnp.concatenate(queries, axis=0), key_ref[0, :, lanes])
        weights_ref[head], shares_ref[head] = softmax_parts(jnp.where(usable, scores, -jnp.inf))
    for head in range(cols // HD):
        lanes = head_lanes(head)
        mixed = weighted(weights_ref[head], value_ref[0, :, lanes]) * shares_ref[head]
        for place, target in enumerate(targets):
            target[:, lanes] = mixed[place * rows : (place + 1) * rows].astype(target.dtype)


def solution(mesh):
    shards = mesh.shape["head"]
    patches = mesh.shape["patch"]
    axes = ("patch", "head")
    vmem = pl.BlockSpec(memory_space=pltpu.VMEM)
    hbm = pl.BlockSpec(memory_space=pltpu.HBM)
    anywhere = pl.BlockSpec(memory_space=pl.ANY)
    params = pltpu.CompilerParams(vmem_limit_bytes=32 * 1024 * 1024)

    def call(kernel, name, out_shape, operands, out_spec=vmem, in_spec=vmem, scratch=(), **more):
        return pl.pallas_call(
            kernel,
            out_shape=out_shape,
            in_specs=[in_spec] * len(operands),
            out_specs=jax.tree.map(lambda _: out_spec, out_shape),
            scratch_shapes=scratch,
            compiler_params=params,
            name=name,
            **more,
        )(*operands)

    def in_hbm(*arrays):
        return [pltpu.with_memory_space_constraint(a, pltpu.HBM) for a in arrays]

    def behind(array, *others):
        return call(
            gate_kernel,
            "gate",
            jax.ShapeDtypeStruct(array.shape, array.dtype),
            (array, *others),
            anywhere,
            anywhere,
            input_output_aliases={0: 0},
        )

    def per_device(
        fresh_query,
        fresh_key,
        fresh_value,
        stale_key,
        stale_value,
        cross_query,
        text_key,
        text_value,
        text_mask,
    ):
        rows, full = fresh_query.shape[1:]
        patch_rows = stale_key.shape[1]
        text_rows = text_key.shape[1]
        kind = fresh_query.dtype
        cols = full // shards
        heads = cols // HD
        share = math.gcd(patches, heads)
        teams = patches // share
        width = cols // share
        share_heads = heads // share
        mates = [(j, s) for j in range(share) for s in range(shards) if (j, s) != (0, 0)]

        ring = list(range(0, teams, 2)) + list(range(1, teams, 2))[::-1]
        ring_next = dict(zip(ring, ring[1:] + ring[:1]))

        def moved(array, step, shift, turn):
            pairs = []
            for patch in range(patches):
                team, member = divmod(patch, share)
                team = ring_next[team] if step else team
                target = team * share + (member + shift) % share
                for shard in range(shards):
                    pairs.append(
                        (patch * shards + shard, target * shards + (shard + turn) % shards)
                    )
            return lax.ppermute(array, axes, pairs)

        def place_of(shift, turn, ref, size):
            shard = lax.rem(lax.axis_index("head") + turn, shards)
            member = lax.rem(lax.axis_index("patch") + shift, share)
            start = pl.multiple_of(shard * cols + member * width, HD)
            return ref.at[0, :, pl.ds(start, size)]

        stale_rows = 2 * patch_rows

        def fresh_start(shift, turn):
            return stale_rows if turn == 0 and shift != 0 else 0

        def message_rows(shift, turn):
            return fresh_start(shift, turn) + 3 * rows + (share * rows if shift == 0 else 0)

        def pack_kernel(query, key, value, old_key, old_value, cross, *refs):
            stale, own, own_cross, messages = refs[:share], refs[share], refs[share + 1], refs[share + 2 : -1]
            me = lax.rem(lax.axis_index("patch"), share)
            copies = []

            def stale_copies(shift, target):
                part = lax.rem(me + shift, share)
                lanes = pl.ds(pl.multiple_of(part * width, HD), width)
                for index, source in enumerate((old_key, old_value)):
                    block = pl.ds(index * patch_rows, patch_rows)
                    copies.append((source.at[0, :, lanes], target.at[block]))

            def fresh_copies(shift, turn, target, first):
                for index, source in enumerate((query, key, value)):
                    block = pl.ds(first + index * rows, rows)
                    copies.append((place_of(shift, turn, source, width), target.at[block]))

            for (shift, turn), message in zip(mates, messages):
                first = fresh_start(shift, turn)
                if first:
                    stale_copies(shift, message)
                fresh_copies(shift, turn, message, first)
                if shift == 0:
                    shard = lax.rem(lax.axis_index("head") + turn, shards)
                    for part in range(share):
                        start = pl.multiple_of(shard * cols + part * width, HD)
                        block = pl.ds(first + (3 + part) * rows, rows)
                        copies.append((cross.at[0, :, pl.ds(start, width)], message.at[block]))
            for shift in range(share):
                stale_copies(shift, stale[shift])
            fresh_copies(0, 0, own, 0)
            start = pl.multiple_of(lax.axis_index("head") * cols, HD)
            copies.append((cross.at[0, :, pl.ds(start, cols)], own_cross))
            run_all(copies, refs[-1])

        packed_shapes = (
            [(stale_rows, width)] * share
            + [(3 * rows, width), (rows, cols)]
            + [(message_rows(*mate), width) for mate in mates]
        )
        copy_count = 2 * share + 4 + sum(
            3 + (2 if fresh_start(*mate) else 0) + (share if mate[0] == 0 else 0) for mate in mates
        )
        packed = call(
            pack_kernel,
            "pack",
            [pltpu.VMEM(shape, kind) for shape in packed_shapes],
            in_hbm(fresh_query, fresh_key, fresh_value, stale_key, stale_value, cross_query),
            in_spec=hbm,
            scratch=[pltpu.SemaphoreType.DMA((copy_count,))],
        )
        stale, own, own_cross = packed[:share], packed[share], packed[share + 1]
        arrived = [
            moved(message, 0, *mate) for mate, message in zip(mates, packed[share + 2 :])
        ]

        pieces = []
        if teams > 1:
            latest = [moved(stale[shift], 1, shift, 0) for shift in range(share)]
            pieces += latest
            for _ in range(teams - 2):
                latest = [moved(piece, 1, 0, 0) for piece in latest]
                pieces += latest

        text = [text_key, text_value, text_mask]
        text = call(
            load_kernel,
            "load",
            [pltpu.VMEM(a.shape, a.dtype) for a in text],
            in_hbm(*text),
            in_spec=hbm,
            scratch=[pltpu.SemaphoreType.DMA((len(text),))],
        )

        from_shards = [a for (shift, _), a in zip(mates, arrived) if shift == 0]
        cross_own, *cross_away = call(
            lambda *refs: cross_kernel(shards, share, *refs),
            "cross",
            [pltpu.VMEM((rows, cols), kind)] * shards,
            (own_cross, *from_shards, *text),
            scratch=[
                pltpu.VMEM((heads, shards * rows, text_rows), kind),
                pltpu.VMEM((heads, shards * rows, HD), jnp.float32),
            ],
        )
        cross_back = [moved(a, 0, 0, -turn - 1) for turn, a in enumerate(cross_away)]

        def place_kernel(spots, size, *refs):
            run_all(
                [
                    (ref, place_of(shift, turn, refs[-2], size))
                    for (shift, turn), ref in zip(spots, refs[:-2])
                ],
                refs[-1],
            )

        def cross_place_kernel(*refs):
            copies = []
            for turn, ref in enumerate(refs[:-2]):
                shard = lax.rem(lax.axis_index("head") + turn, shards)
                start = pl.multiple_of(shard * cols, HD)
                copies.append((ref, refs[-2].at[0, :, pl.ds(start, cols)]))
            run_all(copies, refs[-1])

        whole = jax.ShapeDtypeStruct((1, rows, full), kind)
        cross_mixed = call(
            cross_place_kernel,
            "place_cross",
            whole,
            (cross_own, *cross_back),
            hbm,
            scratch=[pltpu.SemaphoreType.DMA((shards,))],
        )

        spots = [(0, 0)] + mates
        tokens = [own, *arrived]
        first_row = dict(zip(spots, [0] + [fresh_start(*mate) for mate in mates]))

        def token_rows(refs, shift, index, lanes):
            found = []
            for spot, ref in zip(spots, refs):
                if spot[0] == shift:
                    start = first_row[spot] + index * rows
                    found.append(ref[start : start + rows, lanes])
            return found

        def stale_of(refs, shift, index, lanes):
            own_stale, *others = refs[len(spots) :]
            found = []
            if shift != 0:
                found.append(own_stale)
            found += [
                ref for (other, turn), ref in zip(spots, refs) if turn == 0 and other not in (0, shift)
            ]
            block = slice(index * patch_rows, (index + 1) * patch_rows)
            return [ref[block, lanes] for ref in found + others]

        def weights_kernel(*refs):
            sources, targets = refs[: -2 * len(spots)], refs[-2 * len(spots) :]
            for head in range(share_heads):
                lanes = head_lanes(head)
                for shift in range(share):
                    queries = token_rows(sources, shift, 0, lanes)
                    keys = token_rows(sources, shift, 1, lanes) + stale_of(sources, shift, 0, lanes)
                    weights, shares = softmax_parts(
                        scores_of(jnp.concatenate(queries, axis=0), jnp.concatenate(keys, axis=0))
                    )
                    for turn in range(shards):
                        spot = spots.index((shift, turn))
                        block = slice(turn * rows, (turn + 1) * rows)
                        targets[2 * spot][head] = weights[block]
                        targets[2 * spot + 1][head] = shares[block]

        def mix_kernel(shift, weights_ref, shares_ref, *refs):
            sources, target = refs[:-1], refs[-1]
            for head in range(share_heads):
                lanes = head_lanes(head)
                values = token_rows(sources, shift, 2, lanes) + stale_of(sources, shift, 1, lanes)
                mixed = weighted(weights_ref[head], jnp.concatenate(values, axis=0))
                target[:, lanes] = (mixed * shares_ref[head]).astype(target.dtype)

        sources = (*tokens, stale[0], *pieces)
        parts = call(
            weights_kernel,
            "weights",
            [
                pltpu.VMEM((share_heads, rows, patch_rows * patches), kind),
                pltpu.VMEM((share_heads, rows, HD), jnp.float32),
            ]
            * len(spots),
            sources,
        )

        def mixed(spot):
            return call(
                lambda *refs: mix_kernel(spots[spot][0], *refs),
                "mix",
                pltpu.VMEM((rows, width), kind),
                (*parts[2 * spot : 2 * spot + 2], *sources),
            )

        back = [
            moved(mixed(index), 0, -shift, -turn)
            for index, (shift, turn) in enumerate(spots)
            if index > 0
        ]
        self_mixed = call(
            lambda *refs: place_kernel(spots, width, *refs),
            "place_self",
            whole,
            (mixed(0), *back),
            hbm,
            scratch=[pltpu.SemaphoreType.DMA((len(spots),))],
        )
        return (self_mixed, cross_mixed)

    token = P(("group", "cfg"), ("patch", "head"), None)
    stale = P(("group", "cfg"), "patch", "head")
    text = P(("group", "cfg"), None, "head")
    return jax.shard_map(
        per_device,
        mesh=mesh,
        in_specs=(token, token, token, stale, stale, token, text, text, P(("group", "cfg"), None)),
        out_specs=(token, token),
        check_vma=False,
    )
```

```python
import math

import jax
import jax.numpy as jnp
from jax import lax
from jax.experimental import pallas as pl
from jax.experimental.pallas import tpu as pltpu
from jax.sharding import PartitionSpec as P

HD = 128
SCALE = 1.0 / math.sqrt(HD)


def scores_of(queries, keys):
    return lax.dot_general(
        queries, keys, (((1,), (1,)), ((), ())), preferred_element_type=jnp.float32
    ) * SCALE


def weighted(weights, values):
    return lax.dot_general(
        weights, values, (((1,), (0,)), ((), ())), preferred_element_type=jnp.float32
    )


def softmax_parts(scores):
    weights = jnp.exp(scores - jnp.max(scores, axis=-1, keepdims=True))
    totals = jnp.sum(weights, axis=-1, keepdims=True)
    shares = jnp.broadcast_to(1.0 / totals, (scores.shape[0], HD))
    return weights.astype(jnp.bfloat16), shares


def run_all(copies, sems):
    started = []
    for index, (source, target) in enumerate(copies):
        started.append(pltpu.make_async_copy(source, target, sems.at[index]))
        started[-1].start()
    for copy in started:
        copy.wait()


def load_kernel(*refs):
    half = len(refs) // 2
    run_all(zip(refs[:half], refs[half:-1]), refs[-1])


def gate_kernel(*refs):
    pass


def head_lanes(head):
    return slice(head * HD, (head + 1) * HD)


def cross_kernel(shards, share, own, *refs):
    arrived = refs[: shards - 1]
    key_ref, value_ref, mask_ref = refs[shards - 1 : shards + 2]
    targets = refs[shards + 2 : 2 * shards + 2]
    weights_ref, shares_ref = refs[2 * shards + 2 :]
    rows, cols = targets[0].shape
    width = cols // share
    usable = mask_ref[...] > 0
    for head in range(cols // HD):
        lanes = head_lanes(head)
        part, inner = divmod(head * HD, width)
        queries = [own[:, lanes]]
        for ref in arrived:
            start = ref.shape[0] - (share - part) * rows
            queries.append(ref[start : start + rows, inner : inner + HD])
        scores = scores_of(jnp.concatenate(queries, axis=0), key_ref[0, :, lanes])
        weights_ref[head], shares_ref[head] = softmax_parts(jnp.where(usable, scores, -jnp.inf))
    for head in range(cols // HD):
        lanes = head_lanes(head)
        mixed = weighted(weights_ref[head], value_ref[0, :, lanes]) * shares_ref[head]
        for place, target in enumerate(targets):
            target[:, lanes] = mixed[place * rows : (place + 1) * rows].astype(target.dtype)


def solution(mesh):
    shards = mesh.shape["head"]
    patches = mesh.shape["patch"]
    axes = ("patch", "head")
    vmem = pl.BlockSpec(memory_space=pltpu.VMEM)
    hbm = pl.BlockSpec(memory_space=pltpu.HBM)
    anywhere = pl.BlockSpec(memory_space=pl.ANY)
    params = pltpu.CompilerParams(vmem_limit_bytes=32 * 1024 * 1024)

    def call(kernel, name, out_shape, operands, out_spec=vmem, in_spec=vmem, scratch=(), **more):
        return pl.pallas_call(
            kernel,
            out_shape=out_shape,
            in_specs=[in_spec] * len(operands),
            out_specs=jax.tree.map(lambda _: out_spec, out_shape),
            scratch_shapes=scratch,
            compiler_params=params,
            name=name,
            **more,
        )(*operands)

    def in_hbm(*arrays):
        return [pltpu.with_memory_space_constraint(a, pltpu.HBM) for a in arrays]

    def behind(array, *others):
        return call(
            gate_kernel,
            "gate",
            jax.ShapeDtypeStruct(array.shape, array.dtype),
            (array, *others),
            anywhere,
            anywhere,
            input_output_aliases={0: 0},
        )

    def per_device(
        fresh_query,
        fresh_key,
        fresh_value,
        stale_key,
        stale_value,
        cross_query,
        text_key,
        text_value,
        text_mask,
    ):
        rows, full = fresh_query.shape[1:]
        patch_rows = stale_key.shape[1]
        text_rows = text_key.shape[1]
        kind = fresh_query.dtype
        cols = full // shards
        heads = cols // HD
        share = math.gcd(patches, heads)
        teams = patches // share
        width = cols // share
        share_heads = heads // share
        mates = [(j, s) for j in range(share) for s in range(shards) if (j, s) != (0, 0)]

        ring = list(range(0, teams, 2)) + list(range(1, teams, 2))[::-1]
        ring_next = dict(zip(ring, ring[1:] + ring[:1]))

        def moved(array, step, shift, turn):
            pairs = []
            for patch in range(patches):
                team, member = divmod(patch, share)
                team = ring_next[team] if step else team
                target = team * share + (member + shift) % share
                for shard in range(shards):
                    pairs.append(
                        (patch * shards + shard, target * shards + (shard + turn) % shards)
                    )
            return lax.ppermute(array, axes, pairs)

        def place_of(shift, turn, ref, size):
            shard = lax.rem(lax.axis_index("head") + turn, shards)
            member = lax.rem(lax.axis_index("patch") + shift, share)
            start = pl.multiple_of(shard * cols + member * width, HD)
            return ref.at[0, :, pl.ds(start, size)]

        stale_rows = 2 * patch_rows

        def fresh_start(shift, turn):
            return stale_rows if turn == 0 and shift != 0 else 0

        def message_rows(shift, turn):
            return fresh_start(shift, turn) + 3 * rows + (share * rows if shift == 0 else 0)

        def pack_kernel(query, key, value, old_key, old_value, cross, *refs):
            stale, own, own_cross, messages = refs[:share], refs[share], refs[share + 1], refs[share + 2 : -1]
            me = lax.rem(lax.axis_index("patch"), share)
            copies = []

            def stale_copies(shift, target):
                part = lax.rem(me + shift, share)
                lanes = pl.ds(pl.multiple_of(part * width, HD), width)
                for index, source in enumerate((old_key, old_value)):
                    block = pl.ds(index * patch_rows, patch_rows)
                    copies.append((source.at[0, :, lanes], target.at[block]))

            def fresh_copies(shift, turn, target, first):
                for index, source in enumerate((query, key, value)):
                    block = pl.ds(first + index * rows, rows)
                    copies.append((place_of(shift, turn, source, width), target.at[block]))

            for (shift, turn), message in zip(mates, messages):
                first = fresh_start(shift, turn)
                if first:
                    stale_copies(shift, message)
                fresh_copies(shift, turn, message, first)
                if shift == 0:
                    shard = lax.rem(lax.axis_index("head") + turn, shards)
                    for part in range(share):
                        start = pl.multiple_of(shard * cols + part * width, HD)
                        block = pl.ds(first + (3 + part) * rows, rows)
                        copies.append((cross.at[0, :, pl.ds(start, width)], message.at[block]))
            for shift in range(share):
                stale_copies(shift, stale[shift])
            fresh_copies(0, 0, own, 0)
            start = pl.multiple_of(lax.axis_index("head") * cols, HD)
            copies.append((cross.at[0, :, pl.ds(start, cols)], own_cross))
            run_all(copies, refs[-1])

        packed_shapes = (
            [(stale_rows, width)] * share
            + [(3 * rows, width), (rows, cols)]
            + [(message_rows(*mate), width) for mate in mates]
        )
        copy_count = 2 * share + 4 + sum(
            3 + (2 if fresh_start(*mate) else 0) + (share if mate[0] == 0 else 0) for mate in mates
        )
        packed = call(
            pack_kernel,
            "pack",
            [pltpu.VMEM(shape, kind) for shape in packed_shapes],
            in_hbm(fresh_query, fresh_key, fresh_value, stale_key, stale_value, cross_query),
            in_spec=hbm,
            scratch=[pltpu.SemaphoreType.DMA((copy_count,))],
        )
        stale, own, own_cross = packed[:share], packed[share], packed[share + 1]
        arrived = [
            moved(message, 0, *mate) for mate, message in zip(mates, packed[share + 2 :])
        ]

        pieces = []
        if teams > 1:
            latest = [moved(stale[shift], 1, shift, 0) for shift in range(share)]
            pieces += latest
            for _ in range(teams - 2):
                latest = [moved(piece, 1, 0, 0) for piece in latest]
                pieces += latest

        text = [text_key, text_value, text_mask]
        text = call(
            load_kernel,
            "load",
            [pltpu.VMEM(a.shape, a.dtype) for a in text],
            in_hbm(*text),
            in_spec=hbm,
            scratch=[pltpu.SemaphoreType.DMA((len(text),))],
        )

        from_shards = [a for (shift, _), a in zip(mates, arrived) if shift == 0]
        cross_own, *cross_away = call(
            lambda *refs: cross_kernel(shards, share, *refs),
            "cross",
            [pltpu.VMEM((rows, cols), kind)] * shards,
            (own_cross, *from_shards, *text),
            scratch=[
                pltpu.VMEM((heads, shards * rows, text_rows), kind),
                pltpu.VMEM((heads, shards * rows, HD), jnp.float32),
            ],
        )
        cross_back = [moved(a, 0, 0, -turn - 1) for turn, a in enumerate(cross_away)]

        def cross_place_kernel(*refs):
            copies = []
            for turn, ref in enumerate(refs[:-2]):
                shard = lax.rem(lax.axis_index("head") + turn, shards)
                start = pl.multiple_of(shard * cols, HD)
                copies.append((ref, refs[-2].at[0, :, pl.ds(start, cols)]))
            run_all(copies, refs[-1])

        whole = jax.ShapeDtypeStruct((1, rows, full), kind)
        cross_mixed = call(
            cross_place_kernel,
            "place_cross",
            whole,
            (cross_own, *cross_back),
            hbm,
            scratch=[pltpu.SemaphoreType.DMA((shards,))],
        )

        spots = [(0, 0)] + mates
        tokens = [own, *arrived]
        first_row = dict(zip(spots, [0] + [fresh_start(*mate) for mate in mates]))

        def token_rows(refs, shift, index, lanes):
            found = []
            for spot, ref in zip(spots, refs):
                if spot[0] == shift:
                    start = first_row[spot] + index * rows
                    found.append(ref[start : start + rows, lanes])
            return found

        def stale_of(refs, shift, index, lanes):
            own_stale, *others = refs[len(spots) :]
            found = []
            if shift != 0:
                found.append(own_stale)
            found += [
                ref for (other, turn), ref in zip(spots, refs) if turn == 0 and other not in (0, shift)
            ]
            block = slice(index * patch_rows, (index + 1) * patch_rows)
            return [ref[block, lanes] for ref in found + others]

        def weights_kernel(*refs):
            sources, targets = refs[: -2 * len(spots)], refs[-2 * len(spots) :]
            for head in range(share_heads):
                lanes = head_lanes(head)
                for shift in range(share):
                    queries = token_rows(sources, shift, 0, lanes)
                    keys = token_rows(sources, shift, 1, lanes) + stale_of(sources, shift, 0, lanes)
                    weights, shares = softmax_parts(
                        scores_of(jnp.concatenate(queries, axis=0), jnp.concatenate(keys, axis=0))
                    )
                    for turn in range(shards):
                        spot = spots.index((shift, turn))
                        block = slice(turn * rows, (turn + 1) * rows)
                        targets[2 * spot][head] = weights[block]
                        targets[2 * spot + 1][head] = shares[block]

        def mix_kernel(*refs):
            pairs, sources, target = refs[: 2 * len(spots)], refs[2 * len(spots) : -1], refs[-1]
            for shift in range(share):
                member = lax.rem(lax.axis_index("patch") + share - shift, share)
                for head in range(share_heads):
                    lanes = head_lanes(head)
                    values = token_rows(sources, shift, 2, lanes) + stale_of(sources, shift, 1, lanes)
                    values = jnp.concatenate(values, axis=0)
                    for turn in range(shards):
                        spot = spots.index((shift, turn))
                        shard = lax.rem(lax.axis_index("head") + shards - turn, shards)
                        mixed = weighted(pairs[2 * spot][head], values) * pairs[2 * spot + 1][head]
                        target[member * shards + shard, :, lanes] = mixed.astype(target.dtype)

        sources = (*tokens, stale[0], *pieces)
        parts = call(
            weights_kernel,
            "weights",
            [
                pltpu.VMEM((share_heads, rows, patch_rows * patches), kind),
                pltpu.VMEM((share_heads, rows, HD), jnp.float32),
            ]
            * len(spots),
            sources,
        )

        mixed = call(
            mix_kernel,
            "mix",
            pltpu.VMEM((len(spots), rows, width), kind),
            (*parts, *sources),
        )
        size = share * shards
        groups = [list(range(first, first + size)) for first in range(0, patches * shards, size)]
        back = lax.all_to_all(mixed, axes, 0, 0, axis_index_groups=groups, tiled=True)

        def place_kernel(back_ref, target, sems):
            copies = []
            for member in range(share):
                for shard in range(shards):
                    lanes = pl.ds(shard * cols + member * width, width)
                    copies.append((back_ref.at[member * shards + shard], target.at[0, :, lanes]))
            run_all(copies, sems)

        self_mixed = call(
            place_kernel,
            "place_self",
            whole,
            (back,),
            hbm,
            scratch=[pltpu.SemaphoreType.DMA((len(spots),))],
        )
        return (self_mixed, cross_mixed)

    token = P(("group", "cfg"), ("patch", "head"), None)
    stale = P(("group", "cfg"), "patch", "head")
    text = P(("group", "cfg"), None, "head")
    return jax.shard_map(
        per_device,
        mesh=mesh,
        in_specs=(token, token, token, stale, stale, token, text, text, P(("group", "cfg"), None)),
        out_specs=(token, token),
        check_vma=False,
    )
```

```python
import math

import jax
import jax.numpy as jnp
from jax import lax
from jax.experimental import pallas as pl
from jax.experimental.pallas import tpu as pltpu
from jax.sharding import PartitionSpec as P

HD = 128
SCALE = 1.0 / math.sqrt(HD)


def scores_of(queries, keys):
    return lax.dot_general(
        queries, keys, (((1,), (1,)), ((), ())), preferred_element_type=jnp.float32
    ) * SCALE


def weighted(weights, values):
    return lax.dot_general(
        weights, values, (((1,), (0,)), ((), ())), preferred_element_type=jnp.float32
    )


def softmax_parts(scores):
    weights = jnp.exp(scores - jnp.max(scores, axis=-1, keepdims=True))
    totals = jnp.sum(weights, axis=-1, keepdims=True)
    shares = jnp.broadcast_to(1.0 / totals, (scores.shape[0], HD))
    return weights.astype(jnp.bfloat16), shares


def run_all(copies, sems):
    started = []
    for index, (source, target) in enumerate(copies):
        started.append(pltpu.make_async_copy(source, target, sems.at[index]))
        started[-1].start()
    for copy in started:
        copy.wait()


def load_kernel(*refs):
    half = len(refs) // 2
    run_all(zip(refs[:half], refs[half:-1]), refs[-1])


def gate_kernel(*refs):
    pass


def head_lanes(head):
    return slice(head * HD, (head + 1) * HD)


def cross_kernel(shards, share, own, *refs):
    arrived = refs[: shards - 1]
    key_ref, value_ref, mask_ref = refs[shards - 1 : shards + 2]
    targets = refs[shards + 2 : 2 * shards + 2]
    weights_ref, shares_ref = refs[2 * shards + 2 :]
    rows, cols = targets[0].shape
    width = cols // share
    usable = mask_ref[...] > 0
    for head in range(cols // HD):
        lanes = head_lanes(head)
        part, inner = divmod(head * HD, width)
        queries = [own[:, lanes]]
        for ref in arrived:
            start = ref.shape[0] - (share - part) * rows
            queries.append(ref[start : start + rows, inner : inner + HD])
        scores = scores_of(jnp.concatenate(queries, axis=0), key_ref[0, :, lanes])
        weights_ref[head], shares_ref[head] = softmax_parts(jnp.where(usable, scores, -jnp.inf))
    for head in range(cols // HD):
        lanes = head_lanes(head)
        mixed = weighted(weights_ref[head], value_ref[0, :, lanes]) * shares_ref[head]
        for place, target in enumerate(targets):
            target[:, lanes] = mixed[place * rows : (place + 1) * rows].astype(target.dtype)


def solution(mesh):
    shards = mesh.shape["head"]
    patches = mesh.shape["patch"]
    axes = ("patch", "head")
    vmem = pl.BlockSpec(memory_space=pltpu.VMEM)
    hbm = pl.BlockSpec(memory_space=pltpu.HBM)
    anywhere = pl.BlockSpec(memory_space=pl.ANY)
    params = pltpu.CompilerParams(vmem_limit_bytes=32 * 1024 * 1024)

    def call(kernel, name, out_shape, operands, out_spec=vmem, in_spec=vmem, scratch=(), **more):
        return pl.pallas_call(
            kernel,
            out_shape=out_shape,
            in_specs=[in_spec] * len(operands),
            out_specs=jax.tree.map(lambda _: out_spec, out_shape),
            scratch_shapes=scratch,
            compiler_params=params,
            name=name,
            **more,
        )(*operands)

    def in_hbm(*arrays):
        return [pltpu.with_memory_space_constraint(a, pltpu.HBM) for a in arrays]

    def behind(array, *others):
        return call(
            gate_kernel,
            "gate",
            jax.ShapeDtypeStruct(array.shape, array.dtype),
            (array, *others),
            anywhere,
            anywhere,
            input_output_aliases={0: 0},
        )

    def per_device(
        fresh_query,
        fresh_key,
        fresh_value,
        stale_key,
        stale_value,
        cross_query,
        text_key,
        text_value,
        text_mask,
    ):
        rows, full = fresh_query.shape[1:]
        patch_rows = stale_key.shape[1]
        text_rows = text_key.shape[1]
        kind = fresh_query.dtype
        cols = full // shards
        heads = cols // HD
        share = math.gcd(patches, heads)
        teams = patches // share
        width = cols // share
        share_heads = heads // share
        mates = [(j, s) for j in range(share) for s in range(shards) if (j, s) != (0, 0)]

        ring = list(range(0, teams, 2)) + list(range(1, teams, 2))[::-1]
        ring_next = dict(zip(ring, ring[1:] + ring[:1]))

        def moved(array, step, shift, turn):
            pairs = []
            for patch in range(patches):
                team, member = divmod(patch, share)
                team = ring_next[team] if step else team
                target = team * share + (member + shift) % share
                for shard in range(shards):
                    pairs.append(
                        (patch * shards + shard, target * shards + (shard + turn) % shards)
                    )
            return lax.ppermute(array, axes, pairs)

        def place_of(shift, turn, ref, size):
            shard = lax.rem(lax.axis_index("head") + turn, shards)
            member = lax.rem(lax.axis_index("patch") + shift, share)
            start = pl.multiple_of(shard * cols + member * width, HD)
            return ref.at[0, :, pl.ds(start, size)]

        stale_rows = 2 * patch_rows

        def message_rows(shift):
            return 3 * rows + (share * rows if shift == 0 else 0)

        def pack_kernel(query, key, value, old_key, old_value, cross, *refs):
            stale, own, own_cross, messages = refs[:share], refs[share], refs[share + 1], refs[share + 2 : -1]
            me = lax.rem(lax.axis_index("patch"), share)
            copies = []

            def stale_copies(shift, target):
                part = lax.rem(me + shift, share)
                lanes = pl.ds(pl.multiple_of(part * width, HD), width)
                for index, source in enumerate((old_key, old_value)):
                    block = pl.ds(index * patch_rows, patch_rows)
                    copies.append((source.at[0, :, lanes], target.at[block]))

            def fresh_copies(shift, turn, target):
                for index, source in enumerate((query, key, value)):
                    block = pl.ds(index * rows, rows)
                    copies.append((place_of(shift, turn, source, width), target.at[block]))

            for (shift, turn), message in zip(mates, messages):
                fresh_copies(shift, turn, message)
                if shift == 0:
                    shard = lax.rem(lax.axis_index("head") + turn, shards)
                    for part in range(share):
                        start = pl.multiple_of(shard * cols + part * width, HD)
                        block = pl.ds((3 + part) * rows, rows)
                        copies.append((cross.at[0, :, pl.ds(start, width)], message.at[block]))
            for shift in range(share):
                stale_copies(shift, stale[shift])
            fresh_copies(0, 0, own)
            start = pl.multiple_of(lax.axis_index("head") * cols, HD)
            copies.append((cross.at[0, :, pl.ds(start, cols)], own_cross))
            run_all(copies, refs[-1])

        packed_shapes = (
            [(stale_rows, width)] * share
            + [(3 * rows, width), (rows, cols)]
            + [(message_rows(shift), width) for shift, _ in mates]
        )
        copy_count = 2 * share + 4 + sum(
            3 + (share if shift == 0 else 0) for shift, _ in mates
        )
        packed = call(
            pack_kernel,
            "pack",
            [pltpu.VMEM(shape, kind) for shape in packed_shapes],
            in_hbm(fresh_query, fresh_key, fresh_value, stale_key, stale_value, cross_query),
            in_spec=hbm,
            scratch=[pltpu.SemaphoreType.DMA((copy_count,))],
        )
        stale, own, own_cross = packed[:share], packed[share], packed[share + 1]
        arrived = [
            moved(message, 0, *mate) for mate, message in zip(mates, packed[share + 2 :])
        ]

        pieces = [stale[0]] + [moved(stale[shift], 0, shift, 0) for shift in range(1, share)]
        if teams > 1:
            latest = [moved(stale[shift], 1, shift, 0) for shift in range(share)]
            pieces += latest
            for _ in range(teams - 2):
                latest = [moved(piece, 1, 0, 0) for piece in latest]
                pieces += latest

        text = [text_key, text_value, text_mask]
        text = call(
            load_kernel,
            "load",
            [pltpu.VMEM(a.shape, a.dtype) for a in text],
            in_hbm(*text),
            in_spec=hbm,
            scratch=[pltpu.SemaphoreType.DMA((len(text),))],
        )

        from_shards = [a for (shift, _), a in zip(mates, arrived) if shift == 0]
        cross_own, *cross_away = call(
            lambda *refs: cross_kernel(shards, share, *refs),
            "cross",
            [pltpu.VMEM((rows, cols), kind)] * shards,
            (own_cross, *from_shards, *text),
            scratch=[
                pltpu.VMEM((heads, shards * rows, text_rows), kind),
                pltpu.VMEM((heads, shards * rows, HD), jnp.float32),
            ],
        )
        cross_back = [moved(a, 0, 0, -turn - 1) for turn, a in enumerate(cross_away)]

        spots = [(0, 0)] + mates
        tokens = [own, *arrived]

        def token_rows(refs, shift, index, lanes):
            block = slice(index * rows, (index + 1) * rows)
            return [ref[block, lanes] for (other, _), ref in zip(spots, refs) if other == shift]

        def stale_of(refs, shift, index, lanes):
            block = slice(index * patch_rows, (index + 1) * patch_rows)
            return [
                ref[block, lanes]
                for member, ref in enumerate(refs[len(spots) :])
                if member != shift
            ]

        def weights_kernel(*refs):
            sources, targets = refs[: -2 * len(spots)], refs[-2 * len(spots) :]
            for head in range(share_heads):
                lanes = head_lanes(head)
                for shift in range(share):
                    queries = token_rows(sources, shift, 0, lanes)
                    keys = token_rows(sources, shift, 1, lanes) + stale_of(sources, shift, 0, lanes)
                    weights, shares = softmax_parts(
                        scores_of(jnp.concatenate(queries, axis=0), jnp.concatenate(keys, axis=0))
                    )
                    for turn in range(shards):
                        spot = spots.index((shift, turn))
                        block = slice(turn * rows, (turn + 1) * rows)
                        targets[2 * spot][head] = weights[block]
                        targets[2 * spot + 1][head] = shares[block]

        def mix_kernel(shift, weights_ref, shares_ref, *refs):
            sources, target = refs[:-1], refs[-1]
            for head in range(share_heads):
                lanes = head_lanes(head)
                values = token_rows(sources, shift, 2, lanes) + stale_of(sources, shift, 1, lanes)
                mixed = weighted(weights_ref[head], jnp.concatenate(values, axis=0))
                target[:, lanes] = (mixed * shares_ref[head]).astype(target.dtype)

        sources = (*tokens, *pieces)
        parts = call(
            weights_kernel,
            "weights",
            [
                pltpu.VMEM((share_heads, rows, patch_rows * patches), kind),
                pltpu.VMEM((share_heads, rows, HD), jnp.float32),
            ]
            * len(spots),
            sources,
        )

        def mixed(spot):
            return call(
                lambda *refs: mix_kernel(spots[spot][0], *refs),
                "mix",
                pltpu.VMEM((rows, width), kind),
                (*parts[2 * spot : 2 * spot + 2], *sources),
            )

        back = [
            moved(mixed(index), 0, -shift, -turn)
            for index, (shift, turn) in enumerate(spots)
            if index > 0
        ]
        blocks = [mixed(0), *back]

        def place_kernel(*refs):
            outs, sems = refs[-3:-1], refs[-1]
            copies = [
                (ref, place_of(shift, turn, outs[0], width)) for (shift, turn), ref in zip(spots, refs)
            ]
            for turn, ref in enumerate(refs[len(spots) : -3]):
                shard = lax.rem(lax.axis_index("head") + turn, shards)
                start = pl.multiple_of(shard * cols, HD)
                copies.append((ref, outs[1].at[0, :, pl.ds(start, cols)]))
            run_all(copies, sems)

        return call(
            place_kernel,
            "place",
            (jax.ShapeDtypeStruct((1, rows, full), kind),) * 2,
            (*blocks, cross_own, *cross_back),
            hbm,
            scratch=[pltpu.SemaphoreType.DMA((len(spots) + shards,))],
        )

    token = P(("group", "cfg"), ("patch", "head"), None)
    stale = P(("group", "cfg"), "patch", "head")
    text = P(("group", "cfg"), None, "head")
    return jax.shard_map(
        per_device,
        mesh=mesh,
        in_specs=(token, token, token, stale, stale, token, text, text, P(("group", "cfg"), None)),
        out_specs=(token, token),
        check_vma=False,
    )
```

```python
import math

import jax
import jax.numpy as jnp
from jax import lax
from jax.experimental import pallas as pl
from jax.experimental.pallas import tpu as pltpu
from jax.sharding import PartitionSpec as P

HD = 128
SCALE = 1.0 / math.sqrt(HD)


def scores_of(queries, keys):
    return lax.dot_general(
        queries, keys, (((1,), (1,)), ((), ())), preferred_element_type=jnp.float32
    ) * SCALE


def weighted(weights, values):
    return lax.dot_general(
        weights, values, (((1,), (0,)), ((), ())), preferred_element_type=jnp.float32
    )


def softmax_parts(scores):
    weights = jnp.exp(scores - jnp.max(scores, axis=-1, keepdims=True))
    totals = jnp.sum(weights, axis=-1, keepdims=True)
    shares = jnp.broadcast_to(1.0 / totals, (scores.shape[0], HD))
    return weights.astype(jnp.bfloat16), shares


def run_all(copies, sems):
    started = []
    for index, (source, target) in enumerate(copies):
        started.append(pltpu.make_async_copy(source, target, sems.at[index]))
        started[-1].start()
    for copy in started:
        copy.wait()


def load_kernel(*refs):
    half = len(refs) // 2
    run_all(zip(refs[:half], refs[half:-1]), refs[-1])


def gate_kernel(*refs):
    pass


def head_lanes(head):
    return slice(head * HD, (head + 1) * HD)


def cross_kernel(shards, *refs):
    queries, (key_ref, value_ref, mask_ref) = refs[:shards], refs[shards : shards + 3]
    targets, (weights_ref, shares_ref) = refs[shards + 3 : -2], refs[-2:]
    rows, cols = targets[0].shape
    usable = mask_ref[...] > 0
    for head in range(cols // HD):
        lanes = head_lanes(head)
        scores = scores_of(
            jnp.concatenate([ref[:, lanes] for ref in queries], axis=0), key_ref[0, :, lanes]
        )
        weights_ref[head], shares_ref[head] = softmax_parts(jnp.where(usable, scores, -jnp.inf))
    for head in range(cols // HD):
        lanes = head_lanes(head)
        mixed = weighted(weights_ref[head], value_ref[0, :, lanes]) * shares_ref[head]
        for place, target in enumerate(targets):
            target[:, lanes] = mixed[place * rows : (place + 1) * rows].astype(target.dtype)


def solution(mesh):
    shards = mesh.shape["head"]
    patches = mesh.shape["patch"]
    axes = ("patch", "head")
    vmem = pl.BlockSpec(memory_space=pltpu.VMEM)
    hbm = pl.BlockSpec(memory_space=pltpu.HBM)
    anywhere = pl.BlockSpec(memory_space=pl.ANY)
    params = pltpu.CompilerParams(vmem_limit_bytes=32 * 1024 * 1024)

    def call(kernel, name, out_shape, operands, out_spec=vmem, in_spec=vmem, scratch=(), **more):
        return pl.pallas_call(
            kernel,
            out_shape=out_shape,
            in_specs=[in_spec] * len(operands),
            out_specs=jax.tree.map(lambda _: out_spec, out_shape),
            scratch_shapes=scratch,
            compiler_params=params,
            name=name,
            **more,
        )(*operands)

    def in_hbm(*arrays):
        return [pltpu.with_memory_space_constraint(a, pltpu.HBM) for a in arrays]

    def behind(array, *others):
        return call(
            gate_kernel,
            "gate",
            jax.ShapeDtypeStruct(array.shape, array.dtype),
            (array, *others),
            anywhere,
            anywhere,
            input_output_aliases={0: 0},
        )

    def per_device(
        fresh_query,
        fresh_key,
        fresh_value,
        stale_key,
        stale_value,
        cross_query,
        text_key,
        text_value,
        text_mask,
    ):
        rows, full = fresh_query.shape[1:]
        patch_rows = stale_key.shape[1]
        text_rows = text_key.shape[1]
        kind = fresh_query.dtype
        cols = full // shards
        heads = cols // HD
        share = math.gcd(patches, heads)
        teams = patches // share
        width = cols // share
        share_heads = heads // share
        mates = [(j, s) for j in range(share) for s in range(shards) if (j, s) != (0, 0)]

        ring = list(range(0, teams, 2)) + list(range(1, teams, 2))[::-1]
        ring_next = dict(zip(ring, ring[1:] + ring[:1]))

        def moved(array, step, shift, turn):
            pairs = []
            for patch in range(patches):
                team, member = divmod(patch, share)
                team = ring_next[team] if step else team
                target = team * share + (member + shift) % share
                for shard in range(shards):
                    pairs.append(
                        (patch * shards + shard, target * shards + (shard + turn) % shards)
                    )
            return lax.ppermute(array, axes, pairs)

        def place_of(shift, turn, ref, size):
            shard = lax.rem(lax.axis_index("head") + turn, shards)
            member = lax.rem(lax.axis_index("patch") + shift, share)
            start = pl.multiple_of(shard * cols + member * width, HD)
            return ref.at[0, :, pl.ds(start, size)]

        stale_rows = 2 * patch_rows

        def fresh_start(shift, turn):
            return stale_rows if turn == 0 and shift != 0 else 0

        def message_rows(shift, turn):
            return fresh_start(shift, turn) + 3 * rows

        def pack_kernel(query, key, value, old_key, old_value, cross, *refs):
            stale, own, refs = refs[:share], refs[share], refs[share + 1 :]
            crosses, messages = refs[:shards], refs[shards:-1]
            me = lax.rem(lax.axis_index("patch"), share)
            copies = []

            def stale_copies(shift, target):
                part = lax.rem(me + shift, share)
                lanes = pl.ds(pl.multiple_of(part * width, HD), width)
                for index, source in enumerate((old_key, old_value)):
                    block = pl.ds(index * patch_rows, patch_rows)
                    copies.append((source.at[0, :, lanes], target.at[block]))

            def fresh_copies(shift, turn, target, first):
                for index, source in enumerate((query, key, value)):
                    block = pl.ds(first + index * rows, rows)
                    copies.append((place_of(shift, turn, source, width), target.at[block]))

            for (shift, turn), message in zip(mates, messages):
                first = fresh_start(shift, turn)
                if first:
                    stale_copies(shift, message)
                fresh_copies(shift, turn, message, first)
            for shift in range(share):
                stale_copies(shift, stale[shift])
            fresh_copies(0, 0, own, 0)
            for turn, target in enumerate(crosses):
                shard = lax.rem(lax.axis_index("head") + turn, shards)
                lanes = pl.ds(pl.multiple_of(shard * cols, HD), cols)
                copies.append((cross.at[0, :, lanes], target))
            run_all(copies, refs[-1])

        packed_shapes = (
            [(stale_rows, width)] * share
            + [(3 * rows, width)]
            + [(rows, cols)] * shards
            + [(message_rows(*mate), width) for mate in mates]
        )
        copy_count = 2 * share + 3 + shards + sum(
            3 + (2 if fresh_start(*mate) else 0) for mate in mates
        )
        packed = call(
            pack_kernel,
            "pack",
            [pltpu.VMEM(shape, kind) for shape in packed_shapes],
            in_hbm(fresh_query, fresh_key, fresh_value, stale_key, stale_value, cross_query),
            in_spec=hbm,
            scratch=[pltpu.SemaphoreType.DMA((copy_count,))],
        )
        stale, own, packed = packed[:share], packed[share], packed[share + 1 :]
        crosses, messages = packed[:shards], packed[shards:]
        arrived = [
            moved(message, 0, *mate) for mate, message in zip(mates, messages)
        ]
        crosses = [crosses[0]] + [
            moved(behind(a, arrived[shards - 1]) if share > 1 else a, 0, 0, turn)
            for turn, a in enumerate(crosses)
            if turn
        ]

        pieces = []
        if teams > 1:
            latest = [moved(stale[shift], 1, shift, 0) for shift in range(share)]
            pieces += latest
            for _ in range(teams - 2):
                latest = [moved(piece, 1, 0, 0) for piece in latest]
                pieces += latest

        text = [text_key, text_value, text_mask]
        text = call(
            load_kernel,
            "load",
            [pltpu.VMEM(a.shape, a.dtype) for a in text],
            in_hbm(*text),
            in_spec=hbm,
            scratch=[pltpu.SemaphoreType.DMA((len(text),))],
        )

        cross_own, *cross_away = call(
            lambda *refs: cross_kernel(shards, *refs),
            "cross",
            [pltpu.VMEM((rows, cols), kind)] * shards,
            (*crosses, *text),
            scratch=[
                pltpu.VMEM((heads, shards * rows, text_rows), kind),
                pltpu.VMEM((heads, shards * rows, HD), jnp.float32),
            ],
        )
        cross_back = [moved(a, 0, 0, -turn - 1) for turn, a in enumerate(cross_away)]

        spots = [(0, 0)] + mates
        tokens = [own, *arrived]
        first_row = dict(zip(spots, [0] + [fresh_start(*mate) for mate in mates]))

        def token_rows(refs, shift, index, lanes):
            found = []
            for spot, ref in zip(spots, refs):
                if spot[0] == shift:
                    start = first_row[spot] + index * rows
                    found.append(ref[start : start + rows, lanes])
            return found

        def stale_of(refs, shift, index, lanes):
            own_stale, *others = refs[len(spots) :]
            found = []
            if shift != 0:
                found.append(own_stale)
            found += [
                ref for (other, turn), ref in zip(spots, refs) if turn == 0 and other not in (0, shift)
            ]
            block = slice(index * patch_rows, (index + 1) * patch_rows)
            return [ref[block, lanes] for ref in found + others]

        def weights_kernel(*refs):
            sources, targets = refs[: -2 * len(spots)], refs[-2 * len(spots) :]
            for head in range(share_heads):
                lanes = head_lanes(head)
                for shift in range(share):
                    queries = token_rows(sources, shift, 0, lanes)
                    keys = token_rows(sources, shift, 1, lanes) + stale_of(sources, shift, 0, lanes)
                    weights, shares = softmax_parts(
                        scores_of(jnp.concatenate(queries, axis=0), jnp.concatenate(keys, axis=0))
                    )
                    for turn in range(shards):
                        spot = spots.index((shift, turn))
                        block = slice(turn * rows, (turn + 1) * rows)
                        targets[2 * spot][head] = weights[block]
                        targets[2 * spot + 1][head] = shares[block]

        def mix_kernel(shift, weights_ref, shares_ref, *refs):
            sources, target = refs[:-1], refs[-1]
            for head in range(share_heads):
                lanes = head_lanes(head)
                values = token_rows(sources, shift, 2, lanes) + stale_of(sources, shift, 1, lanes)
                mixed = weighted(weights_ref[head], jnp.concatenate(values, axis=0))
                target[:, lanes] = (mixed * shares_ref[head]).astype(target.dtype)

        sources = (*tokens, stale[0], *pieces)
        parts = call(
            weights_kernel,
            "weights",
            [
                pltpu.VMEM((share_heads, rows, patch_rows * patches), kind),
                pltpu.VMEM((share_heads, rows, HD), jnp.float32),
            ]
            * len(spots),
            sources,
        )

        def mixed(spot):
            return call(
                lambda *refs: mix_kernel(spots[spot][0], *refs),
                "mix",
                pltpu.VMEM((rows, width), kind),
                (*parts[2 * spot : 2 * spot + 2], *sources),
            )

        back = [
            moved(mixed(index), 0, -shift, -turn)
            for index, (shift, turn) in enumerate(spots)
            if index > 0
        ]
        blocks = [mixed(0), *back]

        def place_kernel(*refs):
            outs, sems = refs[-3:-1], refs[-1]
            copies = [
                (ref, place_of(shift, turn, outs[0], width)) for (shift, turn), ref in zip(spots, refs)
            ]
            for turn, ref in enumerate(refs[len(spots) : -3]):
                shard = lax.rem(lax.axis_index("head") + turn, shards)
                start = pl.multiple_of(shard * cols, HD)
                copies.append((ref, outs[1].at[0, :, pl.ds(start, cols)]))
            run_all(copies, sems)

        return call(
            place_kernel,
            "place",
            (jax.ShapeDtypeStruct((1, rows, full), kind),) * 2,
            (*blocks, cross_own, *cross_back),
            hbm,
            scratch=[pltpu.SemaphoreType.DMA((len(spots) + shards,))],
        )

    token = P(("group", "cfg"), ("patch", "head"), None)
    stale = P(("group", "cfg"), "patch", "head")
    text = P(("group", "cfg"), None, "head")
    return jax.shard_map(
        per_device,
        mesh=mesh,
        in_specs=(token, token, token, stale, stale, token, text, text, P(("group", "cfg"), None)),
        out_specs=(token, token),
        check_vma=False,
    )
```

```python
import math

import jax
import jax.numpy as jnp
from jax import lax
from jax.experimental import pallas as pl
from jax.experimental.pallas import tpu as pltpu
from jax.sharding import PartitionSpec as P

HD = 128
SCALE = 1.0 / math.sqrt(HD)
QUERY, KEY, VALUE, CROSS = range(4)


def scores_of(queries, keys):
    return lax.dot_general(
        queries, keys, (((1,), (1,)), ((), ())), preferred_element_type=jnp.float32
    ) * SCALE


def weighted(weights, values):
    return lax.dot_general(
        weights, values, (((1,), (0,)), ((), ())), preferred_element_type=jnp.float32
    )


def softmax_parts(scores):
    weights = jnp.exp(scores - jnp.max(scores, axis=-1, keepdims=True))
    totals = jnp.sum(weights, axis=-1, keepdims=True)
    shares = jnp.broadcast_to(1.0 / totals, (scores.shape[0], HD))
    return weights.astype(jnp.bfloat16), shares


def columns_of(ref, owner, cols):
    return ref.at[0, :, pl.ds(pl.multiple_of(owner * cols, HD), cols)]


def run_all(copies):
    for copy in copies:
        copy.start()
    for copy in copies:
        copy.wait()


def pack_kernel(shards, *refs):
    sources, targets, sems = refs[:4], refs[4:-1], refs[-1]
    cols = targets[0].shape[-1]
    me = lax.axis_index("head")
    copies = []
    for shift, target in enumerate(targets):
        owner = lax.rem(me + shift, shards)
        for index, source in enumerate(sources):
            copies.append(
                pltpu.make_async_copy(
                    columns_of(source, owner, cols), target.at[index], sems.at[shift, index]
                )
            )
    run_all(copies)


def load_kernel(*refs):
    count = (len(refs) - 1) // 2
    run_all(
        [
            pltpu.make_async_copy(refs[index], refs[index - count - 1], refs[-1].at[index])
            for index in range(count)
        ]
    )


def place_kernel(shards, own_ref, *refs):
    arrived, target, sems = refs[:-2], refs[-2], refs[-1]
    cols = own_ref.shape[-1]
    me = lax.axis_index("head")
    run_all(
        [
            pltpu.make_async_copy(
                ref, columns_of(target, lax.rem(me + shift, shards), cols), sems.at[shift]
            )
            for shift, ref in enumerate((own_ref, *arrived))
        ]
    )


def rows_of(own, arrived, index, lanes):
    return [ref[index, :, lanes] for ref in (own, *arrived)]


def cross_kernel(shards, own, *refs):
    arrived = refs[: shards - 1]
    key_ref, value_ref, mask_ref = refs[shards - 1 : shards + 2]
    targets = refs[shards + 2 : 2 * shards + 2]
    weights_ref, shares_ref = refs[2 * shards + 2 :]
    rows, cols = targets[0].shape
    usable = mask_ref[...] > 0
    for head in range(cols // HD):
        lanes = slice(head * HD, (head + 1) * HD)
        queries = jnp.concatenate(rows_of(own, arrived, CROSS, lanes), axis=0)
        scores = jnp.where(usable, scores_of(queries, key_ref[0, :, lanes]), -jnp.inf)
        weights_ref[head], shares_ref[head] = softmax_parts(scores)
    for head in range(cols // HD):
        lanes = slice(head * HD, (head + 1) * HD)
        mixed = weighted(weights_ref[head], value_ref[0, :, lanes]) * shares_ref[head]
        for place, target in enumerate(targets):
            target[:, lanes] = mixed[place * rows : (place + 1) * rows].astype(target.dtype)


def weights_kernel(shards, pieces, own, *refs):
    arrived = refs[: shards - 1]
    keys = refs[shards - 1 : shards - 1 + pieces]
    targets = refs[shards - 1 + pieces :]
    rows, cols = own.shape[1:]
    for head in range(cols // HD):
        lanes = slice(head * HD, (head + 1) * HD)
        queries = jnp.concatenate(rows_of(own, arrived, QUERY, lanes), axis=0)
        head_keys = rows_of(own, arrived, KEY, lanes) + [ref[0, :, lanes] for ref in keys]
        weights, shares = softmax_parts(scores_of(queries, jnp.concatenate(head_keys, axis=0)))
        for place in range(shards):
            targets[2 * place][head] = weights[place * rows : (place + 1) * rows]
            targets[2 * place + 1][head] = shares[place * rows : (place + 1) * rows]


def mix_kernel(shards, weights_ref, shares_ref, own, *refs):
    arrived, values, target = refs[: shards - 1], refs[shards - 1 : -1], refs[-1]
    for head in range(target.shape[-1] // HD):
        lanes = slice(head * HD, (head + 1) * HD)
        head_values = rows_of(own, arrived, VALUE, lanes) + [ref[0, :, lanes] for ref in values]
        mixed = weighted(weights_ref[head], jnp.concatenate(head_values, axis=0))
        target[:, lanes] = (mixed * shares_ref[head]).astype(target.dtype)


def solution(mesh):
    shards = mesh.shape["head"]
    patches = mesh.shape["patch"]
    ring = list(range(0, patches, 2)) + list(range(1, patches, 2))[::-1]
    ring_pairs = list(zip(ring, ring[1:] + ring[:1]))
    vmem = pl.BlockSpec(memory_space=pltpu.VMEM)
    hbm = pl.BlockSpec(memory_space=pltpu.HBM)
    anywhere = pl.BlockSpec(memory_space=pl.ANY)
    params = pltpu.CompilerParams(vmem_limit_bytes=32 * 1024 * 1024)

    def over_head(array, shift):
        pairs = [(i, (i + shift) % shards) for i in range(shards)]
        return lax.ppermute(array, "head", pairs)

    def onward(array):
        return lax.ppermute(array, "patch", ring_pairs)

    def in_hbm(*arrays):
        return [pltpu.with_memory_space_constraint(a, pltpu.HBM) for a in arrays]

    def per_device(
        fresh_query,
        fresh_key,
        fresh_value,
        stale_key,
        stale_value,
        cross_query,
        text_key,
        text_value,
        text_mask,
    ):
        rows, width = fresh_query.shape[1:]
        text_rows = text_key.shape[1]
        cols = width // shards
        heads = cols // HD
        kind = fresh_query.dtype
        everyone = rows * shards
        block = jax.ShapeDtypeStruct((rows, cols), kind)

        own, *away = pl.pallas_call(
            lambda *refs: pack_kernel(shards, *refs),
            out_shape=[pltpu.VMEM((4, rows, cols), kind)] * shards,
            in_specs=[hbm] * 4,
            out_specs=[vmem] * shards,
            scratch_shapes=[pltpu.SemaphoreType.DMA((shards, 4))],
            compiler_params=params,
            name="pack",
        )(*in_hbm(fresh_query, fresh_key, fresh_value, cross_query))
        arrived = [over_head(a, s + 1) for s, a in enumerate(away)]

        loads = [text_key, text_value, text_mask, stale_value]
        *text, first_value = pl.pallas_call(
            load_kernel,
            out_shape=[pltpu.VMEM(a.shape, a.dtype) for a in loads],
            in_specs=[hbm] * len(loads) + [anywhere],
            out_specs=[vmem] * len(loads),
            scratch_shapes=[pltpu.SemaphoreType.DMA((len(loads),))],
            compiler_params=params,
            name="load",
        )(*in_hbm(*loads), own)

        keys, values = [stale_key], [first_value]
        for _ in range(patches - 1):
            keys.append(onward(keys[-1]))
            values.append(onward(values[-1]))

        cross_own, *cross_away = pl.pallas_call(
            lambda *refs: cross_kernel(shards, *refs),
            out_shape=[block] * shards,
            in_specs=[vmem] * (shards + 3),
            out_specs=[vmem] * shards,
            scratch_shapes=[
                pltpu.VMEM((heads, everyone, text_rows), kind),
                pltpu.VMEM((heads, everyone, HD), jnp.float32),
            ],
            compiler_params=params,
            name="cross",
        )(own, *arrived, *text)
        cross_back = [over_head(a, -s - 1) for s, a in enumerate(cross_away)]

        place = pl.pallas_call(
            lambda *refs: place_kernel(shards, *refs),
            out_shape=jax.ShapeDtypeStruct((1, rows, width), kind),
            in_specs=[vmem] * shards,
            out_specs=hbm,
            scratch_shapes=[pltpu.SemaphoreType.DMA((shards,))],
            compiler_params=params,
            name="place",
        )
        cross_mixed = place(cross_own, *cross_back)

        pieces = patches - 1
        seen = everyone * patches
        parts = pl.pallas_call(
            lambda *refs: weights_kernel(shards, pieces, *refs),
            out_shape=[
                jax.ShapeDtypeStruct((heads, rows, seen), kind),
                jax.ShapeDtypeStruct((heads, rows, HD), jnp.float32),
            ]
            * shards,
            in_specs=[vmem] * (shards + pieces),
            out_specs=[vmem] * (2 * shards),
            compiler_params=params,
            name="weights",
        )(own, *arrived, *keys[1:])
        mix = pl.pallas_call(
            lambda *refs: mix_kernel(shards, *refs),
            out_shape=block,
            in_specs=[vmem] * (2 + shards + pieces),
            out_specs=vmem,
            compiler_params=params,
            name="mix",
        )
        self_back = [
            over_head(mix(*parts[2 * s : 2 * s + 2], own, *arrived, *values[1:]), -s)
            for s in range(1, shards)
        ]
        self_own = mix(*parts[:2], own, *arrived, *values[1:])
        return (place(self_own, *self_back), cross_mixed)

    token = P(("group", "cfg"), ("patch", "head"), None)
    stale = P(("group", "cfg"), "patch", "head")
    text = P(("group", "cfg"), None, "head")
    return jax.shard_map(
        per_device,
        mesh=mesh,
        in_specs=(token, token, token, stale, stale, token, text, text, P(("group", "cfg"), None)),
        out_specs=(token, token),
        check_vma=False,
    )
```

```python
import math

import jax
import jax.numpy as jnp
from jax import lax
from jax.experimental import pallas as pl
from jax.experimental.pallas import tpu as pltpu
from jax.sharding import PartitionSpec as P

HD = 128
SCALE = 1.0 / math.sqrt(HD)


def scores_of(queries, keys):
    return lax.dot_general(
        queries, keys, (((1,), (1,)), ((), ())), preferred_element_type=jnp.float32
    ) * SCALE


def weighted(weights, values):
    return lax.dot_general(
        weights, values, (((1,), (0,)), ((), ())), preferred_element_type=jnp.float32
    )


def softmax_parts(scores):
    weights = jnp.exp(scores - jnp.max(scores, axis=-1, keepdims=True))
    totals = jnp.sum(weights, axis=-1, keepdims=True)
    shares = jnp.broadcast_to(1.0 / totals, (scores.shape[0], HD))
    return weights.astype(jnp.bfloat16), shares


def run_all(copies, sems):
    started = []
    for index, (source, target) in enumerate(copies):
        started.append(pltpu.make_async_copy(source, target, sems.at[index]))
        started[-1].start()
    for copy in started:
        copy.wait()


def load_kernel(*refs):
    half = len(refs) // 2
    run_all(zip(refs[:half], refs[half:-1]), refs[-1])


def gate_kernel(*refs):
    pass


def head_lanes(head):
    return slice(head * HD, (head + 1) * HD)


def cross_kernel(shards, *refs):
    queries, (key_ref, value_ref, mask_ref) = refs[:shards], refs[shards : shards + 3]
    targets, (weights_ref, shares_ref) = refs[2 * shards + 2 : -2], refs[-2:]
    rows, cols = targets[0].shape
    usable = mask_ref[...] > 0
    for head in range(cols // HD):
        lanes = head_lanes(head)
        scores = scores_of(
            jnp.concatenate([ref[:, lanes] for ref in queries], axis=0), key_ref[0, :, lanes]
        )
        weights_ref[head], shares_ref[head] = softmax_parts(jnp.where(usable, scores, -jnp.inf))
    for head in range(cols // HD):
        lanes = head_lanes(head)
        mixed = weighted(weights_ref[head], value_ref[0, :, lanes]) * shares_ref[head]
        for place, target in enumerate(targets):
            target[:, lanes] = mixed[place * rows : (place + 1) * rows].astype(target.dtype)


def solution(mesh):
    shards = mesh.shape["head"]
    patches = mesh.shape["patch"]
    axes = ("patch", "head")
    vmem = pl.BlockSpec(memory_space=pltpu.VMEM)
    hbm = pl.BlockSpec(memory_space=pltpu.HBM)
    anywhere = pl.BlockSpec(memory_space=pl.ANY)
    params = pltpu.CompilerParams(vmem_limit_bytes=32 * 1024 * 1024)

    def call(kernel, name, out_shape, operands, out_spec=vmem, in_spec=vmem, scratch=(), **more):
        return pl.pallas_call(
            kernel,
            out_shape=out_shape,
            in_specs=[in_spec] * len(operands),
            out_specs=jax.tree.map(lambda _: out_spec, out_shape),
            scratch_shapes=scratch,
            compiler_params=params,
            name=name,
            **more,
        )(*operands)

    def in_hbm(*arrays):
        return [pltpu.with_memory_space_constraint(a, pltpu.HBM) for a in arrays]

    def handed_on(arrays):
        return call(
            gate_kernel,
            "gate",
            [jax.ShapeDtypeStruct(a.shape, a.dtype) for a in arrays],
            arrays,
            anywhere,
            anywhere,
            input_output_aliases={i: i for i in range(len(arrays))},
            cost_estimate=pl.CostEstimate(flops=500000000, bytes_accessed=1800000, transcendentals=0),
        )

    def per_device(
        fresh_query,
        fresh_key,
        fresh_value,
        stale_key,
        stale_value,
        cross_query,
        text_key,
        text_value,
        text_mask,
    ):
        rows, full = fresh_query.shape[1:]
        patch_rows = stale_key.shape[1]
        text_rows = text_key.shape[1]
        kind = fresh_query.dtype
        cols = full // shards
        heads = cols // HD
        share = math.gcd(patches, heads)
        teams = patches // share
        width = cols // share
        share_heads = heads // share
        mates = [(j, s) for j in range(share) for s in range(shards) if (j, s) != (0, 0)]

        ring = list(range(0, teams, 2)) + list(range(1, teams, 2))[::-1]
        ring_next = dict(zip(ring, ring[1:] + ring[:1]))

        def moved(array, step, shift, turn):
            pairs = []
            for patch in range(patches):
                team, member = divmod(patch, share)
                team = ring_next[team] if step else team
                target = team * share + (member + shift) % share
                for shard in range(shards):
                    pairs.append(
                        (patch * shards + shard, target * shards + (shard + turn) % shards)
                    )
            return lax.ppermute(array, axes, pairs)

        def place_of(shift, turn, ref, size):
            shard = lax.rem(lax.axis_index("head") + turn, shards)
            member = lax.rem(lax.axis_index("patch") + shift, share)
            start = pl.multiple_of(shard * cols + member * width, HD)
            return ref.at[0, :, pl.ds(start, size)]

        stale_rows = 2 * patch_rows

        def fresh_start(shift, turn):
            return stale_rows if turn == 0 and shift != 0 else 0

        def message_rows(shift, turn):
            return fresh_start(shift, turn) + 3 * rows

        def pack_kernel(query, key, value, old_key, old_value, cross, *refs):
            stale, own, refs = refs[:share], refs[share], refs[share + 1 :]
            crosses, messages = refs[:shards], refs[shards:-1]
            me = lax.rem(lax.axis_index("patch"), share)
            copies = []

            def stale_copies(shift, target):
                part = lax.rem(me + shift, share)
                lanes = pl.ds(pl.multiple_of(part * width, HD), width)
                for index, source in enumerate((old_key, old_value)):
                    block = pl.ds(index * patch_rows, patch_rows)
                    copies.append((source.at[0, :, lanes], target.at[block]))

            def fresh_copies(shift, turn, target, first):
                for index, source in enumerate((query, key, value)):
                    block = pl.ds(first + index * rows, rows)
                    copies.append((place_of(shift, turn, source, width), target.at[block]))

            for (shift, turn), message in zip(mates, messages):
                first = fresh_start(shift, turn)
                if first:
                    stale_copies(shift, message)
                fresh_copies(shift, turn, message, first)
            for shift in range(share):
                stale_copies(shift, stale[shift])
            fresh_copies(0, 0, own, 0)
            for turn, target in enumerate(crosses):
                shard = lax.rem(lax.axis_index("head") + turn, shards)
                lanes = pl.ds(pl.multiple_of(shard * cols, HD), cols)
                copies.append((cross.at[0, :, lanes], target))
            run_all(copies, refs[-1])

        packed_shapes = (
            [(stale_rows, width)] * share
            + [(3 * rows, width)]
            + [(rows, cols)] * shards
            + [(message_rows(*mate), width) for mate in mates]
        )
        copy_count = 2 * share + 3 + shards + sum(
            3 + (2 if fresh_start(*mate) else 0) for mate in mates
        )
        packed = call(
            pack_kernel,
            "pack",
            [pltpu.VMEM(shape, kind) for shape in packed_shapes],
            in_hbm(fresh_query, fresh_key, fresh_value, stale_key, stale_value, cross_query),
            in_spec=hbm,
            scratch=[pltpu.SemaphoreType.DMA((copy_count,))],
        )
        stale, own, packed = packed[:share], packed[share], packed[share + 1 :]
        crosses, messages = packed[:shards], packed[shards:]
        arrived = [
            moved(message, 0, *mate) for mate, message in zip(mates, messages)
        ]
        crosses = [crosses[0]] + [moved(a, 0, 0, turn) for turn, a in enumerate(crosses) if turn]

        pieces = []
        if teams > 1:
            latest = [moved(stale[shift], 1, shift, 0) for shift in range(share)]
            pieces += latest
            for _ in range(teams - 2):
                latest = [moved(piece, 1, 0, 0) for piece in latest]
                pieces += latest

        pieces = handed_on(pieces) if pieces else pieces

        text = [text_key, text_value, text_mask]
        text = call(
            load_kernel,
            "load",
            [pltpu.VMEM(a.shape, a.dtype) for a in text],
            in_hbm(*text),
            in_spec=hbm,
            scratch=[pltpu.SemaphoreType.DMA((len(text),))],
        )

        from_shards = [a for (shift, _), a in zip(mates, arrived) if shift == 0]
        cross_own, *cross_away = call(
            lambda *refs: cross_kernel(shards, *refs),
            "cross",
            [pltpu.VMEM((rows, cols), kind)] * shards,
            (*crosses, *text, *from_shards),
            scratch=[
                pltpu.VMEM((heads, shards * rows, text_rows), kind),
                pltpu.VMEM((heads, shards * rows, HD), jnp.float32),
            ],
        )
        cross_back = [moved(a, 0, 0, -turn - 1) for turn, a in enumerate(cross_away)]

        def place_kernel(spots, size, *refs):
            run_all(
                [
                    (ref, place_of(shift, turn, refs[-2], size))
                    for (shift, turn), ref in zip(spots, refs[:-2])
                ],
                refs[-1],
            )

        def cross_place_kernel(*refs):
            copies = []
            for turn, ref in enumerate(refs[:-2]):
                shard = lax.rem(lax.axis_index("head") + turn, shards)
                start = pl.multiple_of(shard * cols, HD)
                copies.append((ref, refs[-2].at[0, :, pl.ds(start, cols)]))
            run_all(copies, refs[-1])

        whole = jax.ShapeDtypeStruct((1, rows, full), kind)
        cross_mixed = call(
            cross_place_kernel,
            "place_cross",
            whole,
            (cross_own, *cross_back),
            hbm,
            scratch=[pltpu.SemaphoreType.DMA((shards,))],
        )

        spots = [(0, 0)] + mates
        tokens = [own, *arrived]
        first_row = dict(zip(spots, [0] + [fresh_start(*mate) for mate in mates]))

        def token_rows(refs, shift, index, lanes):
            found = []
            for spot, ref in zip(spots, refs):
                if spot[0] == shift:
                    start = first_row[spot] + index * rows
                    found.append(ref[start : start + rows, lanes])
            return found

        def stale_of(refs, shift, index, lanes):
            own_stale, *others = refs[len(spots) :]
            found = []
            if shift != 0:
                found.append(own_stale)
            found += [
                ref for (other, turn), ref in zip(spots, refs) if turn == 0 and other not in (0, shift)
            ]
            block = slice(index * patch_rows, (index + 1) * patch_rows)
            return [ref[block, lanes] for ref in found + others]

        def weights_kernel(*refs):
            sources, targets = refs[: -2 * len(spots)], refs[-2 * len(spots) :]
            for head in range(share_heads):
                lanes = head_lanes(head)
                for shift in range(share):
                    queries = token_rows(sources, shift, 0, lanes)
                    keys = token_rows(sources, shift, 1, lanes) + stale_of(sources, shift, 0, lanes)
                    weights, shares = softmax_parts(
                        scores_of(jnp.concatenate(queries, axis=0), jnp.concatenate(keys, axis=0))
                    )
                    for turn in range(shards):
                        spot = spots.index((shift, turn))
                        block = slice(turn * rows, (turn + 1) * rows)
                        targets[2 * spot][head] = weights[block]
                        targets[2 * spot + 1][head] = shares[block]

        def mix_kernel(shift, weights_ref, shares_ref, *refs):
            sources, target = refs[:-1], refs[-1]
            for head in range(share_heads):
                lanes = head_lanes(head)
                values = token_rows(sources, shift, 2, lanes) + stale_of(sources, shift, 1, lanes)
                mixed = weighted(weights_ref[head], jnp.concatenate(values, axis=0))
                target[:, lanes] = (mixed * shares_ref[head]).astype(target.dtype)

        sources = (*tokens, stale[0], *pieces)
        parts = call(
            weights_kernel,
            "weights",
            [
                pltpu.VMEM((share_heads, rows, patch_rows * patches), kind),
                pltpu.VMEM((share_heads, rows, HD), jnp.float32),
            ]
            * len(spots),
            sources,
        )

        def mixed(spot):
            return call(
                lambda *refs: mix_kernel(spots[spot][0], *refs),
                "mix",
                pltpu.VMEM((rows, width), kind),
                (*parts[2 * spot : 2 * spot + 2], *sources),
            )

        back = [
            moved(mixed(index), 0, -shift, -turn)
            for index, (shift, turn) in enumerate(spots)
            if index > 0
        ]
        self_mixed = call(
            lambda *refs: place_kernel(spots, width, *refs),
            "place_self",
            whole,
            (mixed(0), *back),
            hbm,
            scratch=[pltpu.SemaphoreType.DMA((len(spots),))],
        )
        return (self_mixed, cross_mixed)

    token = P(("group", "cfg"), ("patch", "head"), None)
    stale = P(("group", "cfg"), "patch", "head")
    text = P(("group", "cfg"), None, "head")
    return jax.shard_map(
        per_device,
        mesh=mesh,
        in_specs=(token, token, token, stale, stale, token, text, text, P(("group", "cfg"), None)),
        out_specs=(token, token),
        check_vma=False,
    )
```

```python
import math

import jax
import jax.numpy as jnp
from jax import lax
from jax.experimental import pallas as pl
from jax.experimental.pallas import tpu as pltpu
from jax.sharding import PartitionSpec as P

HD = 128
SCALE = 1.0 / math.sqrt(HD)
TERMS = 3


def scores_of(queries, keys):
    return lax.dot_general(
        queries, keys, (((1,), (1,)), ((), ())), preferred_element_type=jnp.float32
    ) * SCALE


def weighted(weights, values):
    return lax.dot_general(
        weights, values, (((1,), (0,)), ((), ())), preferred_element_type=jnp.float32
    )


def softmax_parts(scores):
    tops = jnp.max(scores, axis=-1, keepdims=True)
    weights = jnp.exp(scores - tops)
    totals = jnp.sum(weights, axis=-1, keepdims=True)
    shape = (scores.shape[0], HD)
    shares = jnp.broadcast_to(1.0 / totals, shape)
    logs = jnp.broadcast_to(tops + jnp.log(totals), shape)
    return weights.astype(jnp.bfloat16), shares, logs


def lanes_of_logs(logs):
    lane = lax.broadcasted_iota(jnp.int32, logs[0].shape, 1)
    block = jnp.zeros(logs[0].shape, jnp.float32)
    for head, rest in enumerate(logs):
        for term in range(TERMS):
            part = rest.astype(jnp.bfloat16).astype(jnp.float32)
            block = jnp.where(lane == TERMS * head + term, part, block)
            rest = rest - part
    return block.astype(jnp.bfloat16)


def logs_of_lanes(block, head):
    lane = lax.broadcasted_iota(jnp.int32, (HD, HD), 0)
    picked = (lane >= TERMS * head) & (lane < TERMS * (head + 1))
    return weighted(block, jnp.where(picked, 1.0, 0.0).astype(block.dtype))


def run_all(copies, sems):
    started = []
    for index, (source, target) in enumerate(copies):
        started.append(pltpu.make_async_copy(source, target, sems.at[index]))
        started[-1].start()
    for copy in started:
        copy.wait()


def load_kernel(*refs):
    half = len(refs) // 2
    run_all(zip(refs[:half], refs[half:-1]), refs[-1])


def gate_kernel(*refs):
    pass


def head_lanes(head):
    return slice(head * HD, (head + 1) * HD)


def cross_kernel(shards, *refs):
    queries, (key_ref, value_ref, mask_ref) = refs[:shards], refs[shards : shards + 3]
    targets, (weights_ref, shares_ref) = refs[2 * shards + 2 : -2], refs[-2:]
    rows, cols = targets[0].shape
    usable = mask_ref[...] > 0
    for head in range(cols // HD):
        lanes = head_lanes(head)
        scores = scores_of(
            jnp.concatenate([ref[:, lanes] for ref in queries], axis=0), key_ref[0, :, lanes]
        )
        weights_ref[head], shares_ref[head], _ = softmax_parts(
            jnp.where(usable, scores, -jnp.inf)
        )
    for head in range(cols // HD):
        lanes = head_lanes(head)
        mixed = weighted(weights_ref[head], value_ref[0, :, lanes]) * shares_ref[head]
        for place, target in enumerate(targets):
            target[:, lanes] = mixed[place * rows : (place + 1) * rows].astype(target.dtype)


def solution(mesh):
    shards = mesh.shape["head"]
    patches = mesh.shape["patch"]
    axes = ("patch", "head")
    vmem = pl.BlockSpec(memory_space=pltpu.VMEM)
    hbm = pl.BlockSpec(memory_space=pltpu.HBM)
    anywhere = pl.BlockSpec(memory_space=pl.ANY)
    params = pltpu.CompilerParams(vmem_limit_bytes=32 * 1024 * 1024)

    def call(kernel, name, out_shape, operands, out_spec=vmem, in_spec=vmem, scratch=(), **more):
        return pl.pallas_call(
            kernel,
            out_shape=out_shape,
            in_specs=[in_spec] * len(operands),
            out_specs=jax.tree.map(lambda _: out_spec, out_shape),
            scratch_shapes=scratch,
            compiler_params=params,
            name=name,
            **more,
        )(*operands)

    def in_hbm(*arrays):
        return [pltpu.with_memory_space_constraint(a, pltpu.HBM) for a in arrays]

    def handed_on(arrays):
        return call(
            gate_kernel,
            "gate",
            [jax.ShapeDtypeStruct(a.shape, a.dtype) for a in arrays],
            arrays,
            anywhere,
            anywhere,
            input_output_aliases={i: i for i in range(len(arrays))},
            cost_estimate=pl.CostEstimate(flops=500000000, bytes_accessed=1800000, transcendentals=0),
        )

    def per_device(
        fresh_query,
        fresh_key,
        fresh_value,
        stale_key,
        stale_value,
        cross_query,
        text_key,
        text_value,
        text_mask,
    ):
        rows, full = fresh_query.shape[1:]
        patch_rows = stale_key.shape[1]
        text_rows = text_key.shape[1]
        kind = fresh_query.dtype
        cols = full // shards
        heads = cols // HD
        share = math.gcd(patches, heads)
        teams = patches // share
        width = cols // share
        share_heads = heads // share
        mates = [(j, s) for j in range(share) for s in range(shards) if (j, s) != (0, 0)]

        ring = list(range(0, teams, 2)) + list(range(1, teams, 2))[::-1]
        ring_next = dict(zip(ring, ring[1:] + ring[:1]))

        def moved(array, step, shift, turn):
            pairs = []
            for patch in range(patches):
                team, member = divmod(patch, share)
                team = ring_next[team] if step else team
                target = team * share + (member + shift) % share
                for shard in range(shards):
                    pairs.append(
                        (patch * shards + shard, target * shards + (shard + turn) % shards)
                    )
            return lax.ppermute(array, axes, pairs)

        def place_of(shift, turn, ref, size):
            shard = lax.rem(lax.axis_index("head") + turn, shards)
            member = lax.rem(lax.axis_index("patch") + shift, share)
            start = pl.multiple_of(shard * cols + member * width, HD)
            return ref.at[0, :, pl.ds(start, size)]

        over_patch = [mate for mate in mates if mate[0] != 0]
        near_blocks = [(turn, shift) for turn in range(shards) for shift in range(1, share)]
        near_width = len(near_blocks) * width
        stale_rows = 2 * patch_rows

        def fresh_start(shift, turn):
            return stale_rows if turn == 0 and shift != 0 else 0

        def message_rows(shift, turn):
            return fresh_start(shift, turn) + (3 if shift == 0 else 1) * rows

        def pack_kernel(query, key, value, old_key, old_value, cross, *refs):
            stale, own, refs = refs[:share], refs[share], refs[share + 1 :]
            crosses, messages = refs[:shards], refs[shards : shards + len(mates)]
            nears = refs[shards + len(mates) : -1]
            me = lax.rem(lax.axis_index("patch"), share)
            copies = []

            def stale_copies(shift, target):
                part = lax.rem(me + shift, share)
                lanes = pl.ds(pl.multiple_of(part * width, HD), width)
                for index, source in enumerate((old_key, old_value)):
                    block = pl.ds(index * patch_rows, patch_rows)
                    copies.append((source.at[0, :, lanes], target.at[block]))

            def fresh_copies(shift, turn, target, first):
                for index, source in enumerate((query, key, value)[: 3 if shift == 0 else 1]):
                    block = pl.ds(first + index * rows, rows)
                    copies.append((place_of(shift, turn, source, width), target.at[block]))

            for (shift, turn), message in zip(mates, messages):
                first = fresh_start(shift, turn)
                if first:
                    stale_copies(shift, message)
                fresh_copies(shift, turn, message, first)
            for shift in range(share):
                stale_copies(shift, stale[shift])
            fresh_copies(0, 0, own, 0)
            for turn, target in enumerate(crosses):
                shard = lax.rem(lax.axis_index("head") + turn, shards)
                lanes = pl.ds(pl.multiple_of(shard * cols, HD), cols)
                copies.append((cross.at[0, :, lanes], target))
            for turn, target in enumerate(nears):
                for index, source in enumerate((query, key, value)[0 if turn == 0 else 1 :]):
                    for place, (other, shift) in enumerate(near_blocks):
                        block = target.at[pl.ds(index * rows, rows), pl.ds(place * width, width)]
                        copies.append((place_of(shift, turn + other, source, width), block))
            run_all(copies, refs[-1])

        packed_shapes = (
            [(stale_rows, width)] * share
            + [(3 * rows, width)]
            + [(rows, cols)] * shards
            + [(message_rows(*mate), width) for mate in mates]
        )
        if near_blocks:
            packed_shapes += [(3 * rows, near_width)] + [(2 * rows, near_width)] * (shards - 1)
        copy_count = 2 * share + 3 + shards + sum(
            (3 if mate[0] == 0 else 1) + (2 if fresh_start(*mate) else 0) for mate in mates
        )
        copy_count += len(near_blocks) * (2 * shards + 1)
        packed = call(
            pack_kernel,
            "pack",
            [pltpu.VMEM(shape, kind) for shape in packed_shapes],
            in_hbm(fresh_query, fresh_key, fresh_value, stale_key, stale_value, cross_query),
            in_spec=hbm,
            scratch=[pltpu.SemaphoreType.DMA((copy_count,))],
        )
        stale, own, packed = packed[:share], packed[share], packed[share + 1 :]
        crosses, messages = packed[:shards], packed[shards : shards + len(mates)]
        nears = packed[shards + len(mates) :]
        nears = [a if turn == 0 else moved(a, 0, 0, turn) for turn, a in enumerate(nears)]
        arrived = [
            moved(message, 0, *mate) for mate, message in zip(mates, messages)
        ]
        crosses = [crosses[0]] + [moved(a, 0, 0, turn) for turn, a in enumerate(crosses) if turn]

        pieces = []
        if teams > 1:
            latest = [moved(stale[shift], 1, shift, 0) for shift in range(share)]
            pieces += latest
            for _ in range(teams - 2):
                latest = [moved(piece, 1, 0, 0) for piece in latest]
                pieces += latest

        pieces = handed_on(pieces) if pieces else pieces

        text = [text_key, text_value, text_mask]
        text = call(
            load_kernel,
            "load",
            [pltpu.VMEM(a.shape, a.dtype) for a in text],
            in_hbm(*text),
            in_spec=hbm,
            scratch=[pltpu.SemaphoreType.DMA((len(text),))],
        )

        from_shards = [a for (shift, _), a in zip(mates, arrived) if shift == 0]
        cross_own, *cross_away = call(
            lambda *refs: cross_kernel(shards, *refs),
            "cross",
            [pltpu.VMEM((rows, cols), kind)] * shards,
            (*crosses, *text, *from_shards),
            scratch=[
                pltpu.VMEM((heads, shards * rows, text_rows), kind),
                pltpu.VMEM((heads, shards * rows, HD), jnp.float32),
            ],
        )
        cross_back = [moved(a, 0, 0, -turn - 1) for turn, a in enumerate(cross_away)]

        def place_kernel(spots, size, *refs):
            run_all(
                [
                    (ref, place_of(shift, turn, refs[-2], size))
                    for (shift, turn), ref in zip(spots, refs[:-2])
                ],
                refs[-1],
            )

        def cross_place_kernel(*refs):
            copies = []
            for turn, ref in enumerate(refs[:-2]):
                shard = lax.rem(lax.axis_index("head") + turn, shards)
                start = pl.multiple_of(shard * cols, HD)
                copies.append((ref, refs[-2].at[0, :, pl.ds(start, cols)]))
            run_all(copies, refs[-1])

        whole = jax.ShapeDtypeStruct((1, rows, full), kind)
        cross_mixed = call(
            cross_place_kernel,
            "place_cross",
            whole,
            (cross_own, *cross_back),
            hbm,
            scratch=[pltpu.SemaphoreType.DMA((shards,))],
        )

        def near_kernel(*refs):
            own_ref, others, (sums_ref, logs_ref) = refs[0], refs[1:-2], refs[-2:]
            for index in range(near_width // HD):
                lanes = head_lanes(index)
                keys = [own_ref[rows : 2 * rows, lanes]] + [ref[:rows, lanes] for ref in others]
                values = [own_ref[2 * rows :, lanes]] + [ref[rows:, lanes] for ref in others]
                scores = scores_of(own_ref[:rows, lanes], jnp.concatenate(keys, axis=0))
                weights, shares, logs_ref[index] = softmax_parts(scores)
                sums_ref[:, lanes] = weighted(weights, jnp.concatenate(values, axis=0)) * shares

        near = []
        if near_blocks:
            near = call(
                near_kernel,
                "near",
                [
                    pltpu.VMEM((rows, near_width), jnp.float32),
                    pltpu.VMEM((near_width // HD, rows, HD), jnp.float32),
                ],
                nears,
            )

        spots = [(0, 0)] + mates
        tokens = [own, *arrived]
        first_row = dict(zip(spots, [0] + [fresh_start(*mate) for mate in mates]))

        def token_rows(refs, shift, index, lanes):
            found = []
            for spot, ref in zip(spots, refs):
                if spot[0] == shift:
                    start = first_row[spot] + index * rows
                    found.append(ref[start : start + rows, lanes])
            return found

        def stale_of(refs, shift, index, lanes):
            own_stale, *others = refs[len(spots) :]
            found = []
            if shift != 0:
                found.append(own_stale)
            found += [
                ref for (other, turn), ref in zip(spots, refs) if turn == 0 and other not in (0, shift)
            ]
            block = slice(index * patch_rows, (index + 1) * patch_rows)
            return [ref[block, lanes] for ref in found + others]

        def weights_kernel(*refs):
            count = len(spots) + 1 + len(pieces)
            sources, targets, logs_of = refs[:count], refs[count:], {}
            for head in range(share_heads):
                lanes = head_lanes(head)
                for shift in range(share):
                    queries = token_rows(sources, shift, 0, lanes)
                    keys = stale_of(sources, shift, 0, lanes)
                    if shift == 0:
                        keys = token_rows(sources, shift, 1, lanes) + keys
                    weights, shares, logs = softmax_parts(
                        scores_of(jnp.concatenate(queries, axis=0), jnp.concatenate(keys, axis=0))
                    )
                    for turn in range(shards):
                        spot = spots.index((shift, turn))
                        block = slice(turn * rows, (turn + 1) * rows)
                        targets[2 * spot][head] = weights[block]
                        targets[2 * spot + 1][head] = shares[block]
                        logs_of.setdefault(spot, []).append(logs[block])
            for place, mate in enumerate(over_patch):
                targets[2 * len(spots) + place][...] = lanes_of_logs(logs_of[spots.index(mate)])

        def mix_kernel(shift, weights_ref, shares_ref, *refs):
            sources, target = refs[:-1], refs[-1]
            for head in range(share_heads):
                lanes = head_lanes(head)
                values = stale_of(sources, shift, 1, lanes)
                if shift == 0:
                    values = token_rows(sources, shift, 2, lanes) + values
                mixed = weighted(weights_ref[head], jnp.concatenate(values, axis=0))
                target[:, lanes] = (mixed * shares_ref[head]).astype(target.dtype)

        def mate_mix_kernel(shift, weights_ref, shares_ref, logs_ref, *refs):
            mix_kernel(shift, weights_ref, shares_ref, *refs[:-1], refs[-1].at[:, pl.ds(0, width)])
            refs[-1][:, width:] = logs_ref[...]

        def merge_kernel(*refs):
            (sums_ref, logs_ref), refs = refs[:2], refs[2:]
            for (shift, turn), far, target in zip(over_patch, refs, refs[len(over_patch) :]):
                first = near_blocks.index((turn, shift)) * share_heads
                for head in range(share_heads):
                    lanes = head_lanes(head)
                    far_logs, near_logs = logs_of_lanes(far[:, width:], head), logs_ref[first + head]
                    tops = jnp.maximum(far_logs, near_logs)
                    far_part, near_part = jnp.exp(far_logs - tops), jnp.exp(near_logs - tops)
                    mixed = far[:, lanes].astype(jnp.float32) * far_part
                    mixed += sums_ref[:, head_lanes(first + head)] * near_part
                    target[:, lanes] = (mixed / (far_part + near_part)).astype(target.dtype)

        sources = (*tokens, stale[0], *pieces)
        part_shapes = []
        for shift, _ in spots:
            seen = patch_rows * (patches if shift == 0 else patches - 1)
            part_shapes += [
                pltpu.VMEM((share_heads, rows, seen), kind),
                pltpu.VMEM((share_heads, rows, HD), jnp.float32),
            ]
        parts = call(
            weights_kernel,
            "weights",
            part_shapes + [pltpu.VMEM((rows, HD), kind)] * len(over_patch),
            sources,
        )

        def mixed(spot):
            pair, shift = parts[2 * spot : 2 * spot + 2], spots[spot][0]
            if shift == 0:
                kernel, shape = mix_kernel, (rows, width)
            else:
                kernel, shape = mate_mix_kernel, (rows, width + HD)
                pair = (*pair, parts[2 * len(spots) + over_patch.index(spots[spot])])
            return call(
                lambda *refs: kernel(shift, *refs), "mix", pltpu.VMEM(shape, kind), (*pair, *sources)
            )

        back = [
            moved(mixed(index), 0, -shift, -turn)
            for index, (shift, turn) in enumerate(spots)
            if index > 0
        ]
        if over_patch:
            back[shards - 1 :] = call(
                merge_kernel,
                "merge",
                [pltpu.VMEM((rows, width), kind)] * len(over_patch),
                (*near, *back[shards - 1 :]),
            )
        self_mixed = call(
            lambda *refs: place_kernel(spots, width, *refs),
            "place_self",
            whole,
            (mixed(0), *back),
            hbm,
            scratch=[pltpu.SemaphoreType.DMA((len(spots),))],
        )
        return (self_mixed, cross_mixed)

    token = P(("group", "cfg"), ("patch", "head"), None)
    stale = P(("group", "cfg"), "patch", "head")
    text = P(("group", "cfg"), None, "head")
    return jax.shard_map(
        per_device,
        mesh=mesh,
        in_specs=(token, token, token, stale, stale, token, text, text, P(("group", "cfg"), None)),
        out_specs=(token, token),
        check_vma=False,
    )
```

```python
import math

import jax
import jax.numpy as jnp
from jax import lax
from jax.experimental import pallas as pl
from jax.experimental.pallas import tpu as pltpu
from jax.sharding import PartitionSpec as P

HD = 128
SCALE = 1.0 / math.sqrt(HD)
TERMS = 3


def scores_of(queries, keys):
    return lax.dot_general(
        queries, keys, (((1,), (1,)), ((), ())), preferred_element_type=jnp.float32
    ) * SCALE


def weighted(weights, values):
    return lax.dot_general(
        weights, values, (((1,), (0,)), ((), ())), preferred_element_type=jnp.float32
    )


def softmax_parts(scores):
    tops = jnp.max(scores, axis=-1, keepdims=True)
    weights = jnp.exp(scores - tops)
    totals = jnp.sum(weights, axis=-1, keepdims=True)
    shape = (scores.shape[0], HD)
    shares = jnp.broadcast_to(1.0 / totals, shape)
    logs = jnp.broadcast_to(tops + jnp.log(totals), shape)
    return weights.astype(jnp.bfloat16), shares, logs


def lanes_of_logs(logs):
    lane = lax.broadcasted_iota(jnp.int32, logs[0].shape, 1)
    block = jnp.zeros(logs[0].shape, jnp.float32)
    for head, rest in enumerate(logs):
        for term in range(TERMS):
            part = rest.astype(jnp.bfloat16).astype(jnp.float32)
            block = jnp.where(lane == TERMS * head + term, part, block)
            rest = rest - part
    return block.astype(jnp.bfloat16)


def logs_of_lanes(block, head):
    lane = lax.broadcasted_iota(jnp.int32, (HD, HD), 0)
    picked = (lane >= TERMS * head) & (lane < TERMS * (head + 1))
    return weighted(block, jnp.where(picked, 1.0, 0.0).astype(block.dtype))


def run_all(copies, sems):
    started = []
    for index, (source, target) in enumerate(copies):
        started.append(pltpu.make_async_copy(source, target, sems.at[index]))
        started[-1].start()
    for copy in started:
        copy.wait()


def load_kernel(*refs):
    half = len(refs) // 2
    run_all(zip(refs[:half], refs[half:-1]), refs[-1])


def gate_kernel(*refs):
    pass


def head_lanes(head):
    return slice(head * HD, (head + 1) * HD)


def cross_kernel(shards, *refs):
    queries, (key_ref, value_ref, mask_ref) = refs[:shards], refs[shards : shards + 3]
    targets, (weights_ref, shares_ref) = refs[2 * shards + 2 : -2], refs[-2:]
    rows, cols = targets[0].shape
    usable = mask_ref[...] > 0
    for head in range(cols // HD):
        lanes = head_lanes(head)
        scores = scores_of(
            jnp.concatenate([ref[:, lanes] for ref in queries], axis=0), key_ref[0, :, lanes]
        )
        weights_ref[head], shares_ref[head], _ = softmax_parts(
            jnp.where(usable, scores, -jnp.inf)
        )
    for head in range(cols // HD):
        lanes = head_lanes(head)
        mixed = weighted(weights_ref[head], value_ref[0, :, lanes]) * shares_ref[head]
        for place, target in enumerate(targets):
            target[:, lanes] = mixed[place * rows : (place + 1) * rows].astype(target.dtype)


def solution(mesh):
    shards = mesh.shape["head"]
    patches = mesh.shape["patch"]
    axes = ("patch", "head")
    vmem = pl.BlockSpec(memory_space=pltpu.VMEM)
    hbm = pl.BlockSpec(memory_space=pltpu.HBM)
    anywhere = pl.BlockSpec(memory_space=pl.ANY)
    params = pltpu.CompilerParams(vmem_limit_bytes=32 * 1024 * 1024)

    def call(kernel, name, out_shape, operands, out_spec=vmem, in_spec=vmem, scratch=(), **more):
        return pl.pallas_call(
            kernel,
            out_shape=out_shape,
            in_specs=[in_spec] * len(operands),
            out_specs=jax.tree.map(lambda _: out_spec, out_shape),
            scratch_shapes=scratch,
            compiler_params=params,
            name=name,
            **more,
        )(*operands)

    def in_hbm(*arrays):
        return [pltpu.with_memory_space_constraint(a, pltpu.HBM) for a in arrays]

    def handed_on(arrays):
        return call(
            gate_kernel,
            "gate",
            [jax.ShapeDtypeStruct(a.shape, a.dtype) for a in arrays],
            arrays,
            anywhere,
            anywhere,
            input_output_aliases={i: i for i in range(len(arrays))},
            cost_estimate=pl.CostEstimate(flops=500000000, bytes_accessed=1800000, transcendentals=0),
        )

    def per_device(
        fresh_query,
        fresh_key,
        fresh_value,
        stale_key,
        stale_value,
        cross_query,
        text_key,
        text_value,
        text_mask,
    ):
        rows, full = fresh_query.shape[1:]
        everyone = rows * shards
        patch_rows = stale_key.shape[1]
        text_rows = text_key.shape[1]
        kind = fresh_query.dtype
        cols = full // shards
        heads = cols // HD
        share = math.gcd(patches, heads)
        teams = patches // share
        width = cols // share
        share_heads = heads // share
        mates = [(j, s) for j in range(share) for s in range(shards) if (j, s) != (0, 0)]

        ring = list(range(0, teams, 2)) + list(range(1, teams, 2))[::-1]
        ring_next = dict(zip(ring, ring[1:] + ring[:1]))

        def moved(array, step, shift, turn):
            pairs = []
            for patch in range(patches):
                team, member = divmod(patch, share)
                team = ring_next[team] if step else team
                target = team * share + (member + shift) % share
                for shard in range(shards):
                    pairs.append(
                        (patch * shards + shard, target * shards + (shard + turn) % shards)
                    )
            return lax.ppermute(array, axes, pairs)

        def place_of(shift, turn, ref, size):
            shard = lax.rem(lax.axis_index("head") + turn, shards)
            member = lax.rem(lax.axis_index("patch") + shift, share)
            start = pl.multiple_of(shard * cols + member * width, HD)
            return ref.at[0, :, pl.ds(start, size)]

        over_patch = [mate for mate in mates if mate[0] != 0]
        near_blocks = [(turn, shift) for turn in range(shards) for shift in range(1, share)]
        near_width = len(near_blocks) * width
        stale_rows = 2 * patch_rows

        def fresh_start(shift, turn):
            return stale_rows if turn == 0 and shift != 0 else 0

        def message_rows(shift, turn):
            return fresh_start(shift, turn) + (3 if shift == 0 else 1) * rows

        def pack_kernel(query, key, value, old_key, old_value, cross, *refs):
            stale, own, refs = refs[:share], refs[share], refs[share + 1 :]
            crosses, messages = refs[:shards], refs[shards : shards + len(mates)]
            nears = refs[shards + len(mates) : -1]
            me = lax.rem(lax.axis_index("patch"), share)
            copies = []

            def stale_copies(shift, target):
                part = lax.rem(me + shift, share)
                lanes = pl.ds(pl.multiple_of(part * width, HD), width)
                for index, source in enumerate((old_key, old_value)):
                    block = pl.ds(index * patch_rows, patch_rows)
                    copies.append((source.at[0, :, lanes], target.at[block]))

            def fresh_copies(shift, turn, target, first):
                for index, source in enumerate((query, key, value)[: 3 if shift == 0 else 1]):
                    block = pl.ds(first + index * rows, rows)
                    copies.append((place_of(shift, turn, source, width), target.at[block]))

            for (shift, turn), message in zip(mates, messages):
                first = fresh_start(shift, turn)
                if first:
                    stale_copies(shift, message)
                fresh_copies(shift, turn, message, first)
            for shift in range(share):
                stale_copies(shift, stale[shift])
            fresh_copies(0, 0, own, 0)
            for turn, target in enumerate(crosses):
                shard = lax.rem(lax.axis_index("head") + turn, shards)
                lanes = pl.ds(pl.multiple_of(shard * cols, HD), cols)
                copies.append((cross.at[0, :, lanes], target))
            for turn, target in enumerate(nears):
                for index, source in enumerate((query, key, value)[0 if turn == 0 else 1 :]):
                    for place, (other, shift) in enumerate(near_blocks):
                        block = target.at[pl.ds(index * rows, rows), pl.ds(place * width, width)]
                        copies.append((place_of(shift, turn + other, source, width), block))
            run_all(copies, refs[-1])

        packed_shapes = (
            [(stale_rows, width)] * share
            + [(3 * rows, width)]
            + [(rows, cols)] * shards
            + [(message_rows(*mate), width) for mate in mates]
        )
        if near_blocks:
            packed_shapes += [(3 * rows, near_width)] + [(2 * rows, near_width)] * (shards - 1)
        copy_count = 2 * share + 3 + shards + sum(
            (3 if mate[0] == 0 else 1) + (2 if fresh_start(*mate) else 0) for mate in mates
        )
        copy_count += len(near_blocks) * (2 * shards + 1)
        packed = call(
            pack_kernel,
            "pack",
            [pltpu.VMEM(shape, kind) for shape in packed_shapes],
            in_hbm(fresh_query, fresh_key, fresh_value, stale_key, stale_value, cross_query),
            in_spec=hbm,
            scratch=[pltpu.SemaphoreType.DMA((copy_count,))],
        )
        stale, own, packed = packed[:share], packed[share], packed[share + 1 :]
        crosses, messages = packed[:shards], packed[shards : shards + len(mates)]
        nears = packed[shards + len(mates) :]
        nears = [a if turn == 0 else moved(a, 0, 0, turn) for turn, a in enumerate(nears)]
        arrived = [
            moved(message, 0, *mate) for mate, message in zip(mates, messages)
        ]
        crosses = [crosses[0]] + [moved(a, 0, 0, turn) for turn, a in enumerate(crosses) if turn]

        pieces = []
        if teams > 1:
            latest = [moved(stale[shift], 1, shift, 0) for shift in range(share)]
            pieces += latest
            for _ in range(teams - 2):
                latest = [moved(piece, 1, 0, 0) for piece in latest]
                pieces += latest

        pieces = handed_on(pieces) if pieces else pieces

        text = [text_key, text_value, text_mask]
        text = call(
            load_kernel,
            "load",
            [pltpu.VMEM(a.shape, a.dtype) for a in text],
            in_hbm(*text),
            in_spec=hbm,
            scratch=[pltpu.SemaphoreType.DMA((len(text),))],
        )

        from_shards = [a for (shift, _), a in zip(mates, arrived) if shift == 0]
        cross_own, *cross_away = call(
            lambda *refs: cross_kernel(shards, *refs),
            "cross",
            [pltpu.VMEM((rows, cols), kind)] * shards,
            (*crosses, *text, *from_shards),
            scratch=[
                pltpu.VMEM((heads, shards * rows, text_rows), kind),
                pltpu.VMEM((heads, shards * rows, HD), jnp.float32),
            ],
        )
        cross_back = [moved(a, 0, 0, -turn - 1) for turn, a in enumerate(cross_away)]

        def place_kernel(spots, size, *refs):
            run_all(
                [
                    (ref, place_of(shift, turn, refs[-2], size))
                    for (shift, turn), ref in zip(spots, refs[:-2])
                ],
                refs[-1],
            )

        def cross_place_kernel(*refs):
            copies = []
            for turn, ref in enumerate(refs[:-2]):
                shard = lax.rem(lax.axis_index("head") + turn, shards)
                start = pl.multiple_of(shard * cols, HD)
                copies.append((ref, refs[-2].at[0, :, pl.ds(start, cols)]))
            run_all(copies, refs[-1])

        whole = jax.ShapeDtypeStruct((1, rows, full), kind)
        cross_mixed = call(
            cross_place_kernel,
            "place_cross",
            whole,
            (cross_own, *cross_back),
            hbm,
            scratch=[pltpu.SemaphoreType.DMA((shards,))],
        )

        def near_kernel(*refs):
            own_ref, others, (sums_ref, logs_ref, weights_ref, shares_ref) = refs[0], refs[1:-4], refs[-4:]
            for index in range(near_width // HD):
                lanes = head_lanes(index)
                keys = [own_ref[rows : 2 * rows, lanes]] + [ref[:rows, lanes] for ref in others]
                scores = scores_of(own_ref[:rows, lanes], jnp.concatenate(keys, axis=0))
                weights_ref[index], shares_ref[index], logs_ref[index] = softmax_parts(scores)
            for index in range(near_width // HD):
                lanes = head_lanes(index)
                values = [own_ref[2 * rows :, lanes]] + [ref[rows:, lanes] for ref in others]
                sums = weighted(weights_ref[index], jnp.concatenate(values, axis=0))
                sums_ref[:, lanes] = sums * shares_ref[index]

        near = []
        if near_blocks:
            near = call(
                near_kernel,
                "near",
                [
                    pltpu.VMEM((rows, near_width), jnp.float32),
                    pltpu.VMEM((near_width // HD, rows, HD), jnp.float32),
                ],
                nears,
                scratch=[
                    pltpu.VMEM((near_width // HD, rows, everyone), kind),
                    pltpu.VMEM((near_width // HD, rows, HD), jnp.float32),
                ],
            )

        spots = [(0, 0)] + mates
        tokens = [own, *arrived]
        first_row = dict(zip(spots, [0] + [fresh_start(*mate) for mate in mates]))

        def token_rows(refs, shift, index, lanes):
            found = []
            for spot, ref in zip(spots, refs):
                if spot[0] == shift:
                    start = first_row[spot] + index * rows
                    found.append(ref[start : start + rows, lanes])
            return found

        def stale_of(refs, shift, index, lanes):
            own_stale, *others = refs[len(spots) :]
            found = []
            if shift != 0:
                found.append(own_stale)
            found += [
                ref for (other, turn), ref in zip(spots, refs) if turn == 0 and other not in (0, shift)
            ]
            block = slice(index * patch_rows, (index + 1) * patch_rows)
            return [ref[block, lanes] for ref in found + others]

        def weights_kernel(*refs):
            count = len(spots) + 1 + len(pieces)
            sources, targets, logs_of = refs[:count], refs[count:], {}
            for head in range(share_heads):
                lanes = head_lanes(head)
                for shift in range(share):
                    queries = token_rows(sources, shift, 0, lanes)
                    keys = stale_of(sources, shift, 0, lanes)
                    if shift == 0:
                        keys = token_rows(sources, shift, 1, lanes) + keys
                    weights, shares, logs = softmax_parts(
                        scores_of(jnp.concatenate(queries, axis=0), jnp.concatenate(keys, axis=0))
                    )
                    for turn in range(shards):
                        spot = spots.index((shift, turn))
                        block = slice(turn * rows, (turn + 1) * rows)
                        targets[2 * spot][head] = weights[block]
                        targets[2 * spot + 1][head] = shares[block]
                        logs_of.setdefault(spot, []).append(logs[block])
            for place, mate in enumerate(over_patch):
                targets[2 * len(spots) + place][...] = lanes_of_logs(logs_of[spots.index(mate)])

        def mix_kernel(shift, weights_ref, shares_ref, *refs):
            sources, target = refs[:-1], refs[-1]
            for head in range(share_heads):
                lanes = head_lanes(head)
                values = stale_of(sources, shift, 1, lanes)
                if shift == 0:
                    values = token_rows(sources, shift, 2, lanes) + values
                mixed = weighted(weights_ref[head], jnp.concatenate(values, axis=0))
                target[:, lanes] = (mixed * shares_ref[head]).astype(target.dtype)

        def mate_mix_kernel(shift, weights_ref, shares_ref, logs_ref, *refs):
            mix_kernel(shift, weights_ref, shares_ref, *refs[:-1], refs[-1].at[:, pl.ds(0, width)])
            refs[-1][:, width:] = logs_ref[...]

        def merge_kernel(*refs):
            (sums_ref, logs_ref), refs = refs[:2], refs[2:]
            for (shift, turn), far, target in zip(over_patch, refs, refs[len(over_patch) :]):
                first = near_blocks.index((turn, shift)) * share_heads
                for head in range(share_heads):
                    lanes = head_lanes(head)
                    far_logs, near_logs = logs_of_lanes(far[:, width:], head), logs_ref[first + head]
                    tops = jnp.maximum(far_logs, near_logs)
                    far_part, near_part = jnp.exp(far_logs - tops), jnp.exp(near_logs - tops)
                    mixed = far[:, lanes].astype(jnp.float32) * far_part
                    mixed += sums_ref[:, head_lanes(first + head)] * near_part
                    target[:, lanes] = (mixed / (far_part + near_part)).astype(target.dtype)

        sources = (*tokens, stale[0], *pieces)
        part_shapes = []
        for shift, _ in spots:
            seen = patch_rows * (patches if shift == 0 else patches - 1)
            part_shapes += [
                pltpu.VMEM((share_heads, rows, seen), kind),
                pltpu.VMEM((share_heads, rows, HD), jnp.float32),
            ]
        parts = call(
            weights_kernel,
            "weights",
            part_shapes + [pltpu.VMEM((rows, HD), kind)] * len(over_patch),
            sources,
        )

        def mixed(spot):
            pair, shift = parts[2 * spot : 2 * spot + 2], spots[spot][0]
            if shift == 0:
                kernel, shape = mix_kernel, (rows, width)
            else:
                kernel, shape = mate_mix_kernel, (rows, width + HD)
                pair = (*pair, parts[2 * len(spots) + over_patch.index(spots[spot])])
            return call(
                lambda *refs: kernel(shift, *refs), "mix", pltpu.VMEM(shape, kind), (*pair, *sources)
            )

        back = [
            moved(mixed(index), 0, -shift, -turn)
            for index, (shift, turn) in enumerate(spots)
            if index > 0
        ]
        if over_patch:
            back[shards - 1 :] = call(
                merge_kernel,
                "merge",
                [pltpu.VMEM((rows, width), kind)] * len(over_patch),
                (*near, *back[shards - 1 :]),
            )
        self_mixed = call(
            lambda *refs: place_kernel(spots, width, *refs),
            "place_self",
            whole,
            (mixed(0), *back),
            hbm,
            scratch=[pltpu.SemaphoreType.DMA((len(spots),))],
        )
        return (self_mixed, cross_mixed)

    token = P(("group", "cfg"), ("patch", "head"), None)
    stale = P(("group", "cfg"), "patch", "head")
    text = P(("group", "cfg"), None, "head")
    return jax.shard_map(
        per_device,
        mesh=mesh,
        in_specs=(token, token, token, stale, stale, token, text, text, P(("group", "cfg"), None)),
        out_specs=(token, token),
        check_vma=False,
    )
```

```python
import math

import jax
import jax.numpy as jnp
from jax import lax
from jax.experimental import pallas as pl
from jax.experimental.pallas import tpu as pltpu
from jax.sharding import PartitionSpec as P

HD = 128
SCALE = 1.0 / math.sqrt(HD)
TERMS = 3


def scores_of(queries, keys):
    return lax.dot_general(
        queries, keys, (((1,), (1,)), ((), ())), preferred_element_type=jnp.float32
    ) * SCALE


def weighted(weights, values):
    return lax.dot_general(
        weights, values, (((1,), (0,)), ((), ())), preferred_element_type=jnp.float32
    )


def softmax_parts(scores):
    tops = jnp.max(scores, axis=-1, keepdims=True)
    weights = jnp.exp(scores - tops)
    totals = jnp.sum(weights, axis=-1, keepdims=True)
    shape = (scores.shape[0], HD)
    shares = jnp.broadcast_to(1.0 / totals, shape)
    logs = jnp.broadcast_to(tops + jnp.log(totals), shape)
    return weights.astype(jnp.bfloat16), shares, logs


def lanes_of_logs(logs):
    lane = lax.broadcasted_iota(jnp.int32, logs[0].shape, 1)
    block = jnp.zeros(logs[0].shape, jnp.float32)
    for head, rest in enumerate(logs):
        for term in range(TERMS):
            part = rest.astype(jnp.bfloat16).astype(jnp.float32)
            block = jnp.where(lane == TERMS * head + term, part, block)
            rest = rest - part
    return block.astype(jnp.bfloat16)


def logs_of_lanes(block, head):
    lane = lax.broadcasted_iota(jnp.int32, (HD, HD), 0)
    picked = (lane >= TERMS * head) & (lane < TERMS * (head + 1))
    return weighted(block, jnp.where(picked, 1.0, 0.0).astype(block.dtype))


def run_all(copies, sems):
    started = []
    for index, (source, target) in enumerate(copies):
        started.append(pltpu.make_async_copy(source, target, sems.at[index]))
        started[-1].start()
    for copy in started:
        copy.wait()


def load_kernel(*refs):
    half = len(refs) // 2
    run_all(zip(refs[:half], refs[half:-1]), refs[-1])


def gate_kernel(*refs):
    pass


def head_lanes(head):
    return slice(head * HD, (head + 1) * HD)


def cross_kernel(shards, *refs):
    queries, (key_ref, value_ref, mask_ref) = refs[:shards], refs[shards : shards + 3]
    targets, (weights_ref, shares_ref) = refs[2 * shards + 2 : -2], refs[-2:]
    rows, cols = targets[0].shape
    usable = mask_ref[...] > 0
    for head in range(cols // HD):
        lanes = head_lanes(head)
        scores = scores_of(
            jnp.concatenate([ref[:, lanes] for ref in queries], axis=0), key_ref[0, :, lanes]
        )
        weights_ref[head], shares_ref[head], _ = softmax_parts(
            jnp.where(usable, scores, -jnp.inf)
        )
    for head in range(cols // HD):
        lanes = head_lanes(head)
        mixed = weighted(weights_ref[head], value_ref[0, :, lanes]) * shares_ref[head]
        for place, target in enumerate(targets):
            target[:, lanes] = mixed[place * rows : (place + 1) * rows].astype(target.dtype)


def solution(mesh):
    shards = mesh.shape["head"]
    patches = mesh.shape["patch"]
    axes = ("patch", "head")
    vmem = pl.BlockSpec(memory_space=pltpu.VMEM)
    hbm = pl.BlockSpec(memory_space=pltpu.HBM)
    anywhere = pl.BlockSpec(memory_space=pl.ANY)
    params = pltpu.CompilerParams(vmem_limit_bytes=32 * 1024 * 1024)

    def call(kernel, name, out_shape, operands, out_spec=vmem, in_spec=vmem, scratch=(), **more):
        return pl.pallas_call(
            kernel,
            out_shape=out_shape,
            in_specs=[in_spec] * len(operands),
            out_specs=jax.tree.map(lambda _: out_spec, out_shape),
            scratch_shapes=scratch,
            compiler_params=params,
            name=name,
            **more,
        )(*operands)

    def in_hbm(*arrays):
        return [pltpu.with_memory_space_constraint(a, pltpu.HBM) for a in arrays]

    def handed_on(arrays, others=(), **more):
        return call(
            gate_kernel,
            "gate",
            [jax.ShapeDtypeStruct(a.shape, a.dtype) for a in arrays],
            (*arrays, *others),
            anywhere,
            anywhere,
            input_output_aliases={i: i for i in range(len(arrays))},
            **more,
        )

    def per_device(
        fresh_query,
        fresh_key,
        fresh_value,
        stale_key,
        stale_value,
        cross_query,
        text_key,
        text_value,
        text_mask,
    ):
        rows, full = fresh_query.shape[1:]
        everyone = rows * shards
        patch_rows = stale_key.shape[1]
        text_rows = text_key.shape[1]
        kind = fresh_query.dtype
        cols = full // shards
        heads = cols // HD
        share = math.gcd(patches, heads)
        teams = patches // share
        width = cols // share
        share_heads = heads // share
        mates = [(j, s) for j in range(share) for s in range(shards) if (j, s) != (0, 0)]

        ring = list(range(0, teams, 2)) + list(range(1, teams, 2))[::-1]
        ring_next = dict(zip(ring, ring[1:] + ring[:1]))

        def moved(array, step, shift, turn):
            pairs = []
            for patch in range(patches):
                team, member = divmod(patch, share)
                team = ring_next[team] if step else team
                target = team * share + (member + shift) % share
                for shard in range(shards):
                    pairs.append(
                        (patch * shards + shard, target * shards + (shard + turn) % shards)
                    )
            return lax.ppermute(array, axes, pairs)

        def place_of(shift, turn, ref, size):
            shard = lax.rem(lax.axis_index("head") + turn, shards)
            member = lax.rem(lax.axis_index("patch") + shift, share)
            start = pl.multiple_of(shard * cols + member * width, HD)
            return ref.at[0, :, pl.ds(start, size)]

        over_patch = [mate for mate in mates if mate[0] != 0]
        near_blocks = [(turn, shift) for turn in range(shards) for shift in range(1, share)]
        near_width = len(near_blocks) * width
        stale_rows = 2 * patch_rows

        def fresh_start(shift, turn):
            return stale_rows if turn == 0 and shift != 0 else 0

        def message_rows(shift, turn):
            return fresh_start(shift, turn) + (3 if shift == 0 else 1) * rows

        def pack_kernel(query, key, value, old_key, old_value, cross, *refs):
            stale, own, refs = refs[:share], refs[share], refs[share + 1 :]
            crosses, messages = refs[:shards], refs[shards : shards + len(mates)]
            nears = refs[shards + len(mates) : -1]
            me = lax.rem(lax.axis_index("patch"), share)
            copies = []

            def stale_copies(shift, target):
                part = lax.rem(me + shift, share)
                lanes = pl.ds(pl.multiple_of(part * width, HD), width)
                for index, source in enumerate((old_key, old_value)):
                    block = pl.ds(index * patch_rows, patch_rows)
                    copies.append((source.at[0, :, lanes], target.at[block]))

            def fresh_copies(shift, turn, target, first):
                for index, source in enumerate((query, key, value)[: 3 if shift == 0 else 1]):
                    block = pl.ds(first + index * rows, rows)
                    copies.append((place_of(shift, turn, source, width), target.at[block]))

            for (shift, turn), message in zip(mates, messages):
                first = fresh_start(shift, turn)
                if first:
                    stale_copies(shift, message)
                fresh_copies(shift, turn, message, first)
            for shift in range(share):
                stale_copies(shift, stale[shift])
            fresh_copies(0, 0, own, 0)
            for turn, target in enumerate(crosses):
                shard = lax.rem(lax.axis_index("head") + turn, shards)
                lanes = pl.ds(pl.multiple_of(shard * cols, HD), cols)
                copies.append((cross.at[0, :, lanes], target))
            for turn, target in enumerate(nears):
                for index, source in enumerate((query, key, value)[0 if turn == 0 else 1 :]):
                    for place, (other, shift) in enumerate(near_blocks):
                        block = target.at[pl.ds(index * rows, rows), pl.ds(place * width, width)]
                        copies.append((place_of(shift, turn + other, source, width), block))
            run_all(copies, refs[-1])

        packed_shapes = (
            [(stale_rows, width)] * share
            + [(3 * rows, width)]
            + [(rows, cols)] * shards
            + [(message_rows(*mate), width) for mate in mates]
        )
        if near_blocks:
            packed_shapes += [(3 * rows, near_width)] + [(2 * rows, near_width)] * (shards - 1)
        copy_count = 2 * share + 3 + shards + sum(
            (3 if mate[0] == 0 else 1) + (2 if fresh_start(*mate) else 0) for mate in mates
        )
        copy_count += len(near_blocks) * (2 * shards + 1)
        packed = call(
            pack_kernel,
            "pack",
            [pltpu.VMEM(shape, kind) for shape in packed_shapes],
            in_hbm(fresh_query, fresh_key, fresh_value, stale_key, stale_value, cross_query),
            in_spec=hbm,
            scratch=[pltpu.SemaphoreType.DMA((copy_count,))],
        )
        stale, own, packed = packed[:share], packed[share], packed[share + 1 :]
        crosses, messages = packed[:shards], packed[shards : shards + len(mates)]
        nears = packed[shards + len(mates) :]
        text = [text_key, text_value, text_mask]
        text = call(
            load_kernel,
            "load",
            [pltpu.VMEM(a.shape, a.dtype) for a in text],
            in_hbm(*text),
            in_spec=hbm,
            scratch=[pltpu.SemaphoreType.DMA((len(text),))],
        )

        nears = [
            moved(handed_on([a], text[-1:])[0], 0, 0, turn) if turn else a
            for turn, a in enumerate(nears)
        ]
        arrived = [
            moved(message, 0, *mate) for mate, message in zip(mates, messages)
        ]
        crosses = [crosses[0]] + [moved(a, 0, 0, turn) for turn, a in enumerate(crosses) if turn]

        pieces = []
        if teams > 1:
            latest = [moved(stale[shift], 1, shift, 0) for shift in range(share)]
            pieces += latest
            for _ in range(teams - 2):
                latest = [moved(piece, 1, 0, 0) for piece in latest]
                pieces += latest

        cost = pl.CostEstimate(flops=500000000, bytes_accessed=1800000, transcendentals=0)
        pieces = handed_on(pieces, cost_estimate=cost) if pieces else pieces

        from_shards = [a for (shift, _), a in zip(mates, arrived) if shift == 0]
        cross_own, *cross_away = call(
            lambda *refs: cross_kernel(shards, *refs),
            "cross",
            [pltpu.VMEM((rows, cols), kind)] * shards,
            (*crosses, *text, *from_shards),
            scratch=[
                pltpu.VMEM((heads, shards * rows, text_rows), kind),
                pltpu.VMEM((heads, shards * rows, HD), jnp.float32),
            ],
        )
        cross_back = [moved(a, 0, 0, -turn - 1) for turn, a in enumerate(cross_away)]

        def place_kernel(spots, size, *refs):
            run_all(
                [
                    (ref, place_of(shift, turn, refs[-2], size))
                    for (shift, turn), ref in zip(spots, refs[:-2])
                ],
                refs[-1],
            )

        def cross_place_kernel(*refs):
            copies = []
            for turn, ref in enumerate(refs[:-2]):
                shard = lax.rem(lax.axis_index("head") + turn, shards)
                start = pl.multiple_of(shard * cols, HD)
                copies.append((ref, refs[-2].at[0, :, pl.ds(start, cols)]))
            run_all(copies, refs[-1])

        whole = jax.ShapeDtypeStruct((1, rows, full), kind)
        cross_mixed = call(
            cross_place_kernel,
            "place_cross",
            whole,
            (cross_own, *cross_back),
            hbm,
            scratch=[pltpu.SemaphoreType.DMA((shards,))],
        )

        def near_kernel(*refs):
            own_ref, others, (sums_ref, logs_ref, weights_ref, shares_ref) = refs[0], refs[1:-4], refs[-4:]
            for index in range(near_width // HD):
                lanes = head_lanes(index)
                keys = [own_ref[rows : 2 * rows, lanes]] + [ref[:rows, lanes] for ref in others]
                scores = scores_of(own_ref[:rows, lanes], jnp.concatenate(keys, axis=0))
                weights_ref[index], shares_ref[index], logs_ref[index] = softmax_parts(scores)
            for index in range(near_width // HD):
                lanes = head_lanes(index)
                values = [own_ref[2 * rows :, lanes]] + [ref[rows:, lanes] for ref in others]
                sums = weighted(weights_ref[index], jnp.concatenate(values, axis=0))
                sums_ref[:, lanes] = sums * shares_ref[index]

        near = []
        if near_blocks:
            near = call(
                near_kernel,
                "near",
                [
                    pltpu.VMEM((rows, near_width), jnp.float32),
                    pltpu.VMEM((near_width // HD, rows, HD), jnp.float32),
                ],
                nears,
                scratch=[
                    pltpu.VMEM((near_width // HD, rows, everyone), kind),
                    pltpu.VMEM((near_width // HD, rows, HD), jnp.float32),
                ],
            )

        spots = [(0, 0)] + mates
        tokens = [own, *arrived]
        first_row = dict(zip(spots, [0] + [fresh_start(*mate) for mate in mates]))

        def token_rows(refs, shift, index, lanes):
            found = []
            for spot, ref in zip(spots, refs):
                if spot[0] == shift:
                    start = first_row[spot] + index * rows
                    found.append(ref[start : start + rows, lanes])
            return found

        def stale_of(refs, shift, index, lanes):
            own_stale, *others = refs[len(spots) :]
            found = []
            if shift != 0:
                found.append(own_stale)
            found += [
                ref for (other, turn), ref in zip(spots, refs) if turn == 0 and other not in (0, shift)
            ]
            block = slice(index * patch_rows, (index + 1) * patch_rows)
            return [ref[block, lanes] for ref in found + others]

        def weights_kernel(*refs):
            count = len(spots) + 1 + len(pieces)
            sources, targets, logs_of = refs[:count], refs[count:], {}
            for head in range(share_heads):
                lanes = head_lanes(head)
                for shift in range(share):
                    queries = token_rows(sources, shift, 0, lanes)
                    keys = stale_of(sources, shift, 0, lanes)
                    if shift == 0:
                        keys = token_rows(sources, shift, 1, lanes) + keys
                    weights, shares, logs = softmax_parts(
                        scores_of(jnp.concatenate(queries, axis=0), jnp.concatenate(keys, axis=0))
                    )
                    for turn in range(shards):
                        spot = spots.index((shift, turn))
                        block = slice(turn * rows, (turn + 1) * rows)
                        targets[2 * spot][head] = weights[block]
                        targets[2 * spot + 1][head] = shares[block]
                        logs_of.setdefault(spot, []).append(logs[block])
            for place, mate in enumerate(over_patch):
                targets[2 * len(spots) + place][...] = lanes_of_logs(logs_of[spots.index(mate)])

        def mix_kernel(shift, weights_ref, shares_ref, *refs):
            sources, target = refs[:-1], refs[-1]
            for head in range(share_heads):
                lanes = head_lanes(head)
                values = stale_of(sources, shift, 1, lanes)
                if shift == 0:
                    values = token_rows(sources, shift, 2, lanes) + values
                mixed = weighted(weights_ref[head], jnp.concatenate(values, axis=0))
                target[:, lanes] = (mixed * shares_ref[head]).astype(target.dtype)

        def mate_mix_kernel(shift, weights_ref, shares_ref, logs_ref, *refs):
            mix_kernel(shift, weights_ref, shares_ref, *refs[:-1], refs[-1].at[:, pl.ds(0, width)])
            refs[-1][:, width:] = logs_ref[...]

        def merge_kernel(*refs):
            (sums_ref, logs_ref), refs = refs[:2], refs[2:]
            for (shift, turn), far, target in zip(over_patch, refs, refs[len(over_patch) :]):
                first = near_blocks.index((turn, shift)) * share_heads
                for head in range(share_heads):
                    lanes = head_lanes(head)
                    far_logs, near_logs = logs_of_lanes(far[:, width:], head), logs_ref[first + head]
                    tops = jnp.maximum(far_logs, near_logs)
                    far_part, near_part = jnp.exp(far_logs - tops), jnp.exp(near_logs - tops)
                    mixed = far[:, lanes].astype(jnp.float32) * far_part
                    mixed += sums_ref[:, head_lanes(first + head)] * near_part
                    target[:, lanes] = (mixed / (far_part + near_part)).astype(target.dtype)

        sources = (*tokens, stale[0], *pieces)
        part_shapes = []
        for shift, _ in spots:
            seen = patch_rows * (patches if shift == 0 else patches - 1)
            part_shapes += [
                pltpu.VMEM((share_heads, rows, seen), kind),
                pltpu.VMEM((share_heads, rows, HD), jnp.float32),
            ]
        parts = call(
            weights_kernel,
            "weights",
            part_shapes + [pltpu.VMEM((rows, HD), kind)] * len(over_patch),
            sources,
        )

        def mixed(spot):
            pair, shift = parts[2 * spot : 2 * spot + 2], spots[spot][0]
            if shift == 0:
                kernel, shape = mix_kernel, (rows, width)
            else:
                kernel, shape = mate_mix_kernel, (rows, width + HD)
                pair = (*pair, parts[2 * len(spots) + over_patch.index(spots[spot])])
            return call(
                lambda *refs: kernel(shift, *refs), "mix", pltpu.VMEM(shape, kind), (*pair, *sources)
            )

        back = [
            moved(mixed(index), 0, -shift, -turn)
            for index, (shift, turn) in enumerate(spots)
            if index > 0
        ]
        if over_patch:
            back[shards - 1 :] = call(
                merge_kernel,
                "merge",
                [pltpu.VMEM((rows, width), kind)] * len(over_patch),
                (*near, *back[shards - 1 :]),
            )
        self_mixed = call(
            lambda *refs: place_kernel(spots, width, *refs),
            "place_self",
            whole,
            (mixed(0), *back),
            hbm,
            scratch=[pltpu.SemaphoreType.DMA((len(spots),))],
        )
        return (self_mixed, cross_mixed)

    token = P(("group", "cfg"), ("patch", "head"), None)
    stale = P(("group", "cfg"), "patch", "head")
    text = P(("group", "cfg"), None, "head")
    return jax.shard_map(
        per_device,
        mesh=mesh,
        in_specs=(token, token, token, stale, stale, token, text, text, P(("group", "cfg"), None)),
        out_specs=(token, token),
        check_vma=False,
    )
```

```python
import math

import jax
import jax.numpy as jnp
from jax import lax
from jax.experimental import pallas as pl
from jax.experimental.pallas import tpu as pltpu
from jax.sharding import PartitionSpec as P

HD = 128
SCALE = 1.0 / math.sqrt(HD)
TERMS = 3


def scores_of(queries, keys):
    return lax.dot_general(
        queries, keys, (((1,), (1,)), ((), ())), preferred_element_type=jnp.float32
    ) * SCALE


def weighted(weights, values):
    return lax.dot_general(
        weights, values, (((1,), (0,)), ((), ())), preferred_element_type=jnp.float32
    )


def softmax_parts(scores):
    tops = jnp.max(scores, axis=-1, keepdims=True)
    weights = jnp.exp(scores - tops)
    totals = jnp.sum(weights, axis=-1, keepdims=True)
    shape = (scores.shape[0], HD)
    shares = jnp.broadcast_to(1.0 / totals, shape)
    logs = jnp.broadcast_to(tops + jnp.log(totals), shape)
    return weights.astype(jnp.bfloat16), shares, logs


def lanes_of_logs(logs):
    lane = lax.broadcasted_iota(jnp.int32, logs[0].shape, 1)
    block = jnp.zeros(logs[0].shape, jnp.float32)
    for head, rest in enumerate(logs):
        for term in range(TERMS):
            part = rest.astype(jnp.bfloat16).astype(jnp.float32)
            block = jnp.where(lane == TERMS * head + term, part, block)
            rest = rest - part
    return block.astype(jnp.bfloat16)


def logs_of_lanes(block, head):
    lane = lax.broadcasted_iota(jnp.int32, (HD, HD), 0)
    picked = (lane >= TERMS * head) & (lane < TERMS * (head + 1))
    return weighted(block, jnp.where(picked, 1.0, 0.0).astype(block.dtype))


def run_all(copies, sems):
    started = []
    for index, (source, target) in enumerate(copies):
        started.append(pltpu.make_async_copy(source, target, sems.at[index]))
        started[-1].start()
    for copy in started:
        copy.wait()


def load_kernel(*refs):
    half = len(refs) // 2
    run_all(zip(refs[:half], refs[half:-1]), refs[-1])


def gate_kernel(*refs):
    pass


def head_lanes(head):
    return slice(head * HD, (head + 1) * HD)


def cross_kernel(shards, nears, *refs):
    queries, (key_ref, value_ref, mask_ref) = refs[:shards], refs[shards : shards + 3]
    own, away, (weights_ref, shares_ref) = refs[-2 - shards], refs[-1 - shards : -2], refs[-2:]
    rows, cols = own.shape
    usable = mask_ref[...] > 0
    for head in range(cols // HD):
        lanes = head_lanes(head)
        scores = scores_of(
            jnp.concatenate([ref[:, lanes] for ref in queries], axis=0), key_ref[0, :, lanes]
        )
        weights_ref[head], shares_ref[head], _ = softmax_parts(
            jnp.where(usable, scores, -jnp.inf)
        )
    for source, target in zip(refs[shards + 3 : shards + 3 + nears], away):
        target[target.shape[0] - source.shape[0] :, :] = source[...]
    for head in range(cols // HD):
        lanes = head_lanes(head)
        mixed = weighted(weights_ref[head], value_ref[0, :, lanes]) * shares_ref[head]
        own[:, lanes] = mixed[:rows].astype(own.dtype)
        for turn, target in enumerate(away, 1):
            part, inner = divmod(head * HD, target.shape[1])
            block = slice(part * rows, (part + 1) * rows)
            mine = mixed[turn * rows : (turn + 1) * rows].astype(target.dtype)
            target[block, inner : inner + HD] = mine


def solution(mesh):
    shards = mesh.shape["head"]
    patches = mesh.shape["patch"]
    axes = ("patch", "head")
    vmem = pl.BlockSpec(memory_space=pltpu.VMEM)
    hbm = pl.BlockSpec(memory_space=pltpu.HBM)
    anywhere = pl.BlockSpec(memory_space=pl.ANY)
    params = pltpu.CompilerParams(vmem_limit_bytes=32 * 1024 * 1024)

    def call(kernel, name, out_shape, operands, out_spec=vmem, in_spec=vmem, scratch=(), **more):
        return pl.pallas_call(
            kernel,
            out_shape=out_shape,
            in_specs=[in_spec] * len(operands),
            out_specs=jax.tree.map(lambda _: out_spec, out_shape),
            scratch_shapes=scratch,
            compiler_params=params,
            name=name,
            **more,
        )(*operands)

    def in_hbm(*arrays):
        return [pltpu.with_memory_space_constraint(a, pltpu.HBM) for a in arrays]

    def handed_on(arrays, **more):
        return call(
            gate_kernel,
            "gate",
            [jax.ShapeDtypeStruct(a.shape, a.dtype) for a in arrays],
            arrays,
            anywhere,
            anywhere,
            input_output_aliases={i: i for i in range(len(arrays))},
            **more,
        )

    def per_device(
        fresh_query,
        fresh_key,
        fresh_value,
        stale_key,
        stale_value,
        cross_query,
        text_key,
        text_value,
        text_mask,
    ):
        rows, full = fresh_query.shape[1:]
        everyone = rows * shards
        patch_rows = stale_key.shape[1]
        text_rows = text_key.shape[1]
        kind = fresh_query.dtype
        cols = full // shards
        heads = cols // HD
        share = math.gcd(patches, heads)
        teams = patches // share
        width = cols // share
        share_heads = heads // share
        mates = [(j, s) for j in range(share) for s in range(shards) if (j, s) != (0, 0)]

        ring = list(range(0, teams, 2)) + list(range(1, teams, 2))[::-1]
        ring_next = dict(zip(ring, ring[1:] + ring[:1]))

        def moved(array, step, shift, turn):
            pairs = []
            for patch in range(patches):
                team, member = divmod(patch, share)
                team = ring_next[team] if step else team
                target = team * share + (member + shift) % share
                for shard in range(shards):
                    pairs.append(
                        (patch * shards + shard, target * shards + (shard + turn) % shards)
                    )
            return lax.ppermute(array, axes, pairs)

        def place_of(shift, turn, ref, size):
            shard = lax.rem(lax.axis_index("head") + turn, shards)
            member = lax.rem(lax.axis_index("patch") + shift, share)
            start = pl.multiple_of(shard * cols + member * width, HD)
            return ref.at[0, :, pl.ds(start, size)]

        over_patch = [mate for mate in mates if mate[0] != 0]
        near_blocks = [(turn, shift) for turn in range(shards) for shift in range(1, share)]
        near_width = len(near_blocks) * width
        back_rows = (share + 2 * len(near_blocks)) * rows
        stale_rows = 2 * patch_rows

        def fresh_start(shift, turn):
            return stale_rows if turn == 0 and shift != 0 else 0

        def message_rows(shift, turn):
            return fresh_start(shift, turn) + (3 if shift == 0 else 1) * rows

        def pack_kernel(query, key, value, old_key, old_value, cross, *refs):
            stale, own, refs = refs[:share], refs[share], refs[share + 1 :]
            crosses, messages = refs[:shards], refs[shards : shards + len(mates)]
            nears = refs[shards + len(mates) : -1]
            me = lax.rem(lax.axis_index("patch"), share)
            copies = []

            def stale_copies(shift, target):
                part = lax.rem(me + shift, share)
                lanes = pl.ds(pl.multiple_of(part * width, HD), width)
                for index, source in enumerate((old_key, old_value)):
                    block = pl.ds(index * patch_rows, patch_rows)
                    copies.append((source.at[0, :, lanes], target.at[block]))

            def fresh_copies(shift, turn, target, first):
                for index, source in enumerate((query, key, value)[: 3 if shift == 0 else 1]):
                    block = pl.ds(first + index * rows, rows)
                    copies.append((place_of(shift, turn, source, width), target.at[block]))

            for (shift, turn), message in zip(mates, messages):
                first = fresh_start(shift, turn)
                if first:
                    stale_copies(shift, message)
                fresh_copies(shift, turn, message, first)
            for shift in range(share):
                stale_copies(shift, stale[shift])
            fresh_copies(0, 0, own, 0)
            for turn, target in enumerate(crosses):
                shard = lax.rem(lax.axis_index("head") + turn, shards)
                lanes = pl.ds(pl.multiple_of(shard * cols, HD), cols)
                copies.append((cross.at[0, :, lanes], target))
            for turn, target in enumerate(nears):
                for place, (other, shift) in enumerate(near_blocks):
                    for index, source in enumerate((query, key, value)):
                        if turn == 0:
                            block = pl.ds((3 * place + index) * rows, rows)
                        elif index > 0:
                            block = pl.ds((2 * place + index - 1) * rows, rows)
                        else:
                            continue
                        spot = place_of(shift, other + shards - turn, source, width)
                        copies.append((spot, target.at[block]))
            run_all(copies, refs[-1])

        packed_shapes = (
            [(stale_rows, width)] * share
            + [(3 * rows, width)]
            + [(rows, cols)] * shards
            + [(message_rows(*mate), width) for mate in mates]
        )
        if near_blocks:
            near_rows = [3 * rows * len(near_blocks)] + [2 * rows * len(near_blocks)] * (shards - 1)
            packed_shapes += [(height, width) for height in near_rows]
        copy_count = 2 * share + 3 + shards + sum(
            (3 if mate[0] == 0 else 1) + (2 if fresh_start(*mate) else 0) for mate in mates
        )
        copy_count += len(near_blocks) * (2 * shards + 1)
        packed = call(
            pack_kernel,
            "pack",
            [pltpu.VMEM(shape, kind) for shape in packed_shapes],
            in_hbm(fresh_query, fresh_key, fresh_value, stale_key, stale_value, cross_query),
            in_spec=hbm,
            scratch=[pltpu.SemaphoreType.DMA((copy_count,))],
        )
        stale, own, packed = packed[:share], packed[share], packed[share + 1 :]
        crosses, messages = packed[:shards], packed[shards : shards + len(mates)]
        nears = packed[shards + len(mates) :]
        text = [text_key, text_value, text_mask]
        text = call(
            load_kernel,
            "load",
            [pltpu.VMEM(a.shape, a.dtype) for a in text],
            in_hbm(*text),
            in_spec=hbm,
            scratch=[pltpu.SemaphoreType.DMA((len(text),))],
        )


        arrived = [
            moved(message, 0, *mate) for mate, message in zip(mates, messages)
        ]
        crosses = [crosses[0]] + [moved(a, 0, 0, turn) for turn, a in enumerate(crosses) if turn]

        pieces = []
        if teams > 1:
            latest = [moved(stale[shift], 1, shift, 0) for shift in range(share)]
            pieces += latest
            for _ in range(teams - 2):
                latest = [moved(piece, 1, 0, 0) for piece in latest]
                pieces += latest

        if teams * share > 1:
            first = len(mates) - len(over_patch)
            cost = pl.CostEstimate(flops=3000000000, bytes_accessed=10800000, transcendentals=0)
            found = list(handed_on([*arrived[first:], *pieces], cost_estimate=cost))
            arrived[first:], pieces = found[: len(over_patch)], found[len(over_patch) :]

        from_shards = [a for (shift, _), a in zip(mates, arrived) if shift == 0]
        cross_own, *cross_away = call(
            lambda *refs: cross_kernel(shards, len(nears[1:]), *refs),
            "cross",
            [pltpu.VMEM((rows, cols), kind)]
            + [pltpu.VMEM((back_rows, width), kind)] * (shards - 1),
            (*crosses, *text, *nears[1:], *from_shards),
            scratch=[
                pltpu.VMEM((heads, shards * rows, text_rows), kind),
                pltpu.VMEM((heads, shards * rows, HD), jnp.float32),
            ],
        )
        cross_back = [moved(a, 0, 0, -turn - 1) for turn, a in enumerate(cross_away)]

        def place_kernel(spots, size, *refs):
            run_all(
                [
                    (ref, place_of(shift, turn, refs[-2], size))
                    for (shift, turn), ref in zip(spots, refs[:-2])
                ],
                refs[-1],
            )

        def cross_place_kernel(*refs):
            copies = []
            for turn, ref in enumerate(refs[:-2]):
                shard = lax.rem(lax.axis_index("head") + turn, shards)
                if turn == 0:
                    start = pl.multiple_of(shard * cols, HD)
                    copies.append((ref, refs[-2].at[0, :, pl.ds(start, cols)]))
                    continue
                for part in range(share):
                    start = pl.multiple_of(shard * cols + part * width, HD)
                    block = ref.at[pl.ds(part * rows, rows)]
                    copies.append((block, refs[-2].at[0, :, pl.ds(start, width)]))
            run_all(copies, refs[-1])

        whole = jax.ShapeDtypeStruct((1, rows, full), kind)
        cross_mixed = call(
            cross_place_kernel,
            "place_cross",
            whole,
            (cross_own, *cross_back),
            hbm,
            scratch=[pltpu.SemaphoreType.DMA((1 + (shards - 1) * share,))],
        )

        def near_kernel(*refs):
            own_ref, others, (sums_ref, logs_ref, weights_ref, shares_ref) = refs[0], refs[1:-4], refs[-4:]

            def rows_of(index, head):
                place, head = divmod(head, share_heads)
                lanes = head_lanes(head)
                start = (3 * place + index) * rows
                found = [own_ref[start : start + rows, lanes]]
                start = (share + 2 * place + index - 1) * rows
                for ref in others if index > 0 else ():
                    found.append(ref[start : start + rows, lanes])
                return jnp.concatenate(found, axis=0)

            for head in range(near_width // HD):
                scores = scores_of(rows_of(0, head), rows_of(1, head))
                weights_ref[head], shares_ref[head], logs_ref[head] = softmax_parts(scores)
            for head in range(near_width // HD):
                sums = weighted(weights_ref[head], rows_of(2, head))
                sums_ref[:, head_lanes(head)] = sums * shares_ref[head]

        near = []
        if near_blocks:
            near = call(
                near_kernel,
                "near",
                [
                    pltpu.VMEM((rows, near_width), jnp.float32),
                    pltpu.VMEM((near_width // HD, rows, HD), jnp.float32),
                ],
                (nears[0], *cross_back),
                scratch=[
                    pltpu.VMEM((near_width // HD, rows, everyone), kind),
                    pltpu.VMEM((near_width // HD, rows, HD), jnp.float32),
                ],
            )

        spots = [(0, 0)] + mates
        tokens = [own, *arrived]
        first_row = dict(zip(spots, [0] + [fresh_start(*mate) for mate in mates]))

        def token_rows(refs, shift, index, lanes):
            found = []
            for spot, ref in zip(spots, refs):
                if spot[0] == shift:
                    start = first_row[spot] + index * rows
                    found.append(ref[start : start + rows, lanes])
            return found

        def stale_of(refs, shift, index, lanes):
            own_stale, *others = refs[len(spots) :]
            found = []
            if shift != 0:
                found.append(own_stale)
            found += [
                ref for (other, turn), ref in zip(spots, refs) if turn == 0 and other not in (0, shift)
            ]
            block = slice(index * patch_rows, (index + 1) * patch_rows)
            return [ref[block, lanes] for ref in found + others]

        def weights_kernel(*refs):
            count = len(spots) + 1 + len(pieces)
            sources, targets, logs_of = refs[:count], refs[count:], {}
            for head in range(share_heads):
                lanes = head_lanes(head)
                for shift in range(share):
                    queries = token_rows(sources, shift, 0, lanes)
                    keys = stale_of(sources, shift, 0, lanes)
                    if shift == 0:
                        keys = token_rows(sources, shift, 1, lanes) + keys
                    weights, shares, logs = softmax_parts(
                        scores_of(jnp.concatenate(queries, axis=0), jnp.concatenate(keys, axis=0))
                    )
                    for turn in range(shards):
                        spot = spots.index((shift, turn))
                        block = slice(turn * rows, (turn + 1) * rows)
                        targets[2 * spot][head] = weights[block]
                        targets[2 * spot + 1][head] = shares[block]
                        logs_of.setdefault(spot, []).append(logs[block])
            for place, mate in enumerate(over_patch):
                targets[2 * len(spots) + place][...] = lanes_of_logs(logs_of[spots.index(mate)])

        def mix_kernel(shift, weights_ref, shares_ref, *refs):
            sources, target = refs[:-1], refs[-1]
            for head in range(share_heads):
                lanes = head_lanes(head)
                values = stale_of(sources, shift, 1, lanes)
                if shift == 0:
                    values = token_rows(sources, shift, 2, lanes) + values
                mixed = weighted(weights_ref[head], jnp.concatenate(values, axis=0))
                target[:, lanes] = (mixed * shares_ref[head]).astype(target.dtype)

        def mate_mix_kernel(shift, weights_ref, shares_ref, logs_ref, *refs):
            mix_kernel(shift, weights_ref, shares_ref, *refs[:-1], refs[-1].at[:, pl.ds(0, width)])
            refs[-1][:, width:] = logs_ref[...]

        def merge_kernel(*refs):
            (sums_ref, logs_ref), refs = refs[:2], refs[2:]
            for (shift, turn), far, target in zip(over_patch, refs, refs[len(over_patch) :]):
                first = near_blocks.index((turn, shift)) * share_heads
                for head in range(share_heads):
                    lanes = head_lanes(head)
                    far_logs, near_logs = logs_of_lanes(far[:, width:], head), logs_ref[first + head]
                    tops = jnp.maximum(far_logs, near_logs)
                    far_part, near_part = jnp.exp(far_logs - tops), jnp.exp(near_logs - tops)
                    mixed = far[:, lanes].astype(jnp.float32) * far_part
                    mixed += sums_ref[:, head_lanes(first + head)] * near_part
                    target[:, lanes] = (mixed / (far_part + near_part)).astype(target.dtype)

        sources = (*tokens, stale[0], *pieces)
        part_shapes = []
        for shift, _ in spots:
            seen = patch_rows * (patches if shift == 0 else patches - 1)
            part_shapes += [
                pltpu.VMEM((share_heads, rows, seen), kind),
                pltpu.VMEM((share_heads, rows, HD), jnp.float32),
            ]
        parts = call(
            weights_kernel,
            "weights",
            part_shapes + [pltpu.VMEM((rows, HD), kind)] * len(over_patch),
            sources,
        )

        def mixed(spot):
            pair, shift = parts[2 * spot : 2 * spot + 2], spots[spot][0]
            if shift == 0:
                kernel, shape = mix_kernel, (rows, width)
            else:
                kernel, shape = mate_mix_kernel, (rows, width + HD)
                pair = (*pair, parts[2 * len(spots) + over_patch.index(spots[spot])])
            return call(
                lambda *refs: kernel(shift, *refs), "mix", pltpu.VMEM(shape, kind), (*pair, *sources)
            )

        back = [
            moved(mixed(index), 0, -shift, -turn)
            for index, (shift, turn) in enumerate(spots)
            if index > 0
        ]
        if over_patch:
            back[shards - 1 :] = call(
                merge_kernel,
                "merge",
                [pltpu.VMEM((rows, width), kind)] * len(over_patch),
                (*near, *back[shards - 1 :]),
            )
        self_mixed = call(
            lambda *refs: place_kernel(spots, width, *refs),
            "place_self",
            whole,
            (mixed(0), *back),
            hbm,
            scratch=[pltpu.SemaphoreType.DMA((len(spots),))],
        )
        return (self_mixed, cross_mixed)

    token = P(("group", "cfg"), ("patch", "head"), None)
    stale = P(("group", "cfg"), "patch", "head")
    text = P(("group", "cfg"), None, "head")
    return jax.shard_map(
        per_device,
        mesh=mesh,
        in_specs=(token, token, token, stale, stale, token, text, text, P(("group", "cfg"), None)),
        out_specs=(token, token),
        check_vma=False,
    )
```

```python
import math

import jax
import jax.numpy as jnp
from jax import lax
from jax.experimental import pallas as pl
from jax.experimental.pallas import tpu as pltpu
from jax.sharding import PartitionSpec as P

HD = 128
SCALE = 1.0 / math.sqrt(HD)
TERMS = 3


def scores_of(queries, keys):
    return lax.dot_general(
        queries, keys, (((1,), (1,)), ((), ())), preferred_element_type=jnp.float32
    ) * SCALE


def weighted(weights, values):
    return lax.dot_general(
        weights, values, (((1,), (0,)), ((), ())), preferred_element_type=jnp.float32
    )


def softmax_parts(scores):
    tops = jnp.max(scores, axis=-1, keepdims=True)
    weights = jnp.exp(scores - tops)
    totals = jnp.sum(weights, axis=-1, keepdims=True)
    shape = (scores.shape[0], HD)
    shares = jnp.broadcast_to(1.0 / totals, shape)
    logs = jnp.broadcast_to(tops + jnp.log(totals), shape)
    return weights.astype(jnp.bfloat16), shares, logs


def lanes_of_logs(logs):
    lane = lax.broadcasted_iota(jnp.int32, logs[0].shape, 1)
    block = jnp.zeros(logs[0].shape, jnp.float32)
    for head, rest in enumerate(logs):
        for term in range(TERMS):
            part = rest.astype(jnp.bfloat16).astype(jnp.float32)
            block = jnp.where(lane == TERMS * head + term, part, block)
            rest = rest - part
    return block.astype(jnp.bfloat16)


def logs_of_lanes(block, head):
    lane = lax.broadcasted_iota(jnp.int32, (HD, HD), 0)
    picked = (lane >= TERMS * head) & (lane < TERMS * (head + 1))
    return weighted(block, jnp.where(picked, 1.0, 0.0).astype(block.dtype))


def run_all(copies, sems):
    started = []
    for index, (source, target) in enumerate(copies):
        started.append(pltpu.make_async_copy(source, target, sems.at[index]))
        started[-1].start()
    for copy in started:
        copy.wait()


def load_kernel(*refs):
    half = len(refs) // 2
    run_all(zip(refs[:half], refs[half:-1]), refs[-1])


def gate_kernel(*refs):
    pass


def head_lanes(head):
    return slice(head * HD, (head + 1) * HD)


def cross_kernel(shards, nears, *refs):
    queries, (key_ref, value_ref, mask_ref) = refs[:shards], refs[shards : shards + 3]
    own, away, (weights_ref, shares_ref) = refs[-2 - shards], refs[-1 - shards : -2], refs[-2:]
    rows, cols = own.shape
    usable = mask_ref[...] > 0
    for head in range(cols // HD):
        lanes = head_lanes(head)
        scores = scores_of(
            jnp.concatenate([ref[:, lanes] for ref in queries], axis=0), key_ref[0, :, lanes]
        )
        weights_ref[head], shares_ref[head], _ = softmax_parts(
            jnp.where(usable, scores, -jnp.inf)
        )
    for source, target in zip(refs[shards + 3 : shards + 3 + nears], away):
        target[target.shape[0] - source.shape[0] :, :] = source[...]
    for head in range(cols // HD):
        lanes = head_lanes(head)
        mixed = weighted(weights_ref[head], value_ref[0, :, lanes]) * shares_ref[head]
        own[:, lanes] = mixed[:rows].astype(own.dtype)
        for turn, target in enumerate(away, 1):
            part, inner = divmod(head * HD, target.shape[1])
            block = slice(part * rows, (part + 1) * rows)
            mine = mixed[turn * rows : (turn + 1) * rows].astype(target.dtype)
            target[block, inner : inner + HD] = mine


def solution(mesh):
    shards = mesh.shape["head"]
    patches = mesh.shape["patch"]
    axes = ("patch", "head")
    vmem = pl.BlockSpec(memory_space=pltpu.VMEM)
    hbm = pl.BlockSpec(memory_space=pltpu.HBM)
    anywhere = pl.BlockSpec(memory_space=pl.ANY)
    params = pltpu.CompilerParams(vmem_limit_bytes=32 * 1024 * 1024)

    def call(kernel, name, out_shape, operands, out_spec=vmem, in_spec=vmem, scratch=(), **more):
        return pl.pallas_call(
            kernel,
            out_shape=out_shape,
            in_specs=[in_spec] * len(operands),
            out_specs=jax.tree.map(lambda _: out_spec, out_shape),
            scratch_shapes=scratch,
            compiler_params=params,
            name=name,
            **more,
        )(*operands)

    def in_hbm(*arrays):
        return [pltpu.with_memory_space_constraint(a, pltpu.HBM) for a in arrays]

    def handed_on(arrays, **more):
        return call(
            gate_kernel,
            "gate",
            [jax.ShapeDtypeStruct(a.shape, a.dtype) for a in arrays],
            arrays,
            anywhere,
            anywhere,
            input_output_aliases={i: i for i in range(len(arrays))},
            **more,
        )

    def per_device(
        fresh_query,
        fresh_key,
        fresh_value,
        stale_key,
        stale_value,
        cross_query,
        text_key,
        text_value,
        text_mask,
    ):
        rows, full = fresh_query.shape[1:]
        everyone = rows * shards
        patch_rows = stale_key.shape[1]
        text_rows = text_key.shape[1]
        kind = fresh_query.dtype
        cols = full // shards
        heads = cols // HD
        share = math.gcd(patches, heads)
        teams = patches // share
        width = cols // share
        share_heads = heads // share
        mates = [(j, s) for j in range(share) for s in range(shards) if (j, s) != (0, 0)]

        ring = list(range(0, teams, 2)) + list(range(1, teams, 2))[::-1]
        ring_next = dict(zip(ring, ring[1:] + ring[:1]))

        def moved(array, step, shift, turn):
            pairs = []
            for patch in range(patches):
                team, member = divmod(patch, share)
                team = ring_next[team] if step else team
                target = team * share + (member + shift) % share
                for shard in range(shards):
                    pairs.append(
                        (patch * shards + shard, target * shards + (shard + turn) % shards)
                    )
            return lax.ppermute(array, axes, pairs)

        def place_of(shift, turn, ref, size):
            shard = lax.rem(lax.axis_index("head") + turn, shards)
            member = lax.rem(lax.axis_index("patch") + shift, share)
            start = pl.multiple_of(shard * cols + member * width, HD)
            return ref.at[0, :, pl.ds(start, size)]

        over_patch = [mate for mate in mates if mate[0] != 0]
        near_blocks = [(turn, shift) for turn in range(shards) for shift in range(1, share)]
        near_width = len(near_blocks) * width
        back_rows = (share + 2 * len(near_blocks)) * rows
        stale_rows = 2 * patch_rows

        def fresh_start(shift, turn):
            return stale_rows if turn == 0 and shift != 0 else 0

        def message_rows(shift, turn):
            return fresh_start(shift, turn) + (3 if shift == 0 else 1) * rows

        def pack_kernel(query, key, value, old_key, old_value, cross, *refs):
            stale, own, refs = refs[:share], refs[share], refs[share + 1 :]
            crosses, messages = refs[:shards], refs[shards : shards + len(mates)]
            nears = refs[shards + len(mates) : -1]
            me = lax.rem(lax.axis_index("patch"), share)
            copies = []

            def stale_copies(shift, target):
                part = lax.rem(me + shift, share)
                lanes = pl.ds(pl.multiple_of(part * width, HD), width)
                for index, source in enumerate((old_key, old_value)):
                    block = pl.ds(index * patch_rows, patch_rows)
                    copies.append((source.at[0, :, lanes], target.at[block]))

            def fresh_copies(shift, turn, target, first):
                for index, source in enumerate((query, key, value)[: 3 if shift == 0 else 1]):
                    block = pl.ds(first + index * rows, rows)
                    copies.append((place_of(shift, turn, source, width), target.at[block]))

            for (shift, turn), message in zip(mates, messages):
                first = fresh_start(shift, turn)
                if first:
                    stale_copies(shift, message)
                fresh_copies(shift, turn, message, first)
            for shift in range(share):
                stale_copies(shift, stale[shift])
            fresh_copies(0, 0, own, 0)
            for turn, target in enumerate(crosses):
                shard = lax.rem(lax.axis_index("head") + turn, shards)
                lanes = pl.ds(pl.multiple_of(shard * cols, HD), cols)
                copies.append((cross.at[0, :, lanes], target))
            for turn, target in enumerate(nears):
                for place, (other, shift) in enumerate(near_blocks):
                    for index, source in enumerate((query, key, value)):
                        if turn == 0:
                            block = pl.ds((3 * place + index) * rows, rows)
                        elif index > 0:
                            block = pl.ds((2 * place + index - 1) * rows, rows)
                        else:
                            continue
                        spot = place_of(shift, other + shards - turn, source, width)
                        copies.append((spot, target.at[block]))
            run_all(copies, refs[-1])

        packed_shapes = (
            [(stale_rows, width)] * share
            + [(3 * rows, width)]
            + [(rows, cols)] * shards
            + [(message_rows(*mate), width) for mate in mates]
        )
        if near_blocks:
            near_rows = [3 * rows * len(near_blocks)] + [2 * rows * len(near_blocks)] * (shards - 1)
            packed_shapes += [(height, width) for height in near_rows]
        copy_count = 2 * share + 3 + shards + sum(
            (3 if mate[0] == 0 else 1) + (2 if fresh_start(*mate) else 0) for mate in mates
        )
        copy_count += len(near_blocks) * (2 * shards + 1)
        packed = call(
            pack_kernel,
            "pack",
            [pltpu.VMEM(shape, kind) for shape in packed_shapes],
            in_hbm(fresh_query, fresh_key, fresh_value, stale_key, stale_value, cross_query),
            in_spec=hbm,
            scratch=[pltpu.SemaphoreType.DMA((copy_count,))],
        )
        stale, own, packed = packed[:share], packed[share], packed[share + 1 :]
        crosses, messages = packed[:shards], packed[shards : shards + len(mates)]
        nears = packed[shards + len(mates) :]
        text = [text_key, text_value, text_mask]
        text = call(
            load_kernel,
            "load",
            [pltpu.VMEM(a.shape, a.dtype) for a in text],
            in_hbm(*text),
            in_spec=hbm,
            scratch=[pltpu.SemaphoreType.DMA((len(text),))],
        )


        arrived = [
            moved(message, 0, *mate) for mate, message in zip(mates, messages)
        ]
        crosses = [crosses[0]] + [moved(a, 0, 0, turn) for turn, a in enumerate(crosses) if turn]

        pieces = []
        if teams > 1:
            latest = [moved(stale[shift], 1, shift, 0) for shift in range(share)]
            pieces += latest
            for _ in range(teams - 2):
                latest = [moved(piece, 1, 0, 0) for piece in latest]
                pieces += latest

        cost = pl.CostEstimate(flops=500000000, bytes_accessed=1800000, transcendentals=0)
        pieces = handed_on(pieces, cost_estimate=cost) if pieces else pieces

        from_shards = [a for (shift, _), a in zip(mates, arrived) if shift == 0]
        cross_own, *cross_away = call(
            lambda *refs: cross_kernel(shards, len(nears[1:]), *refs),
            "cross",
            [pltpu.VMEM((rows, cols), kind)]
            + [pltpu.VMEM((back_rows, width), kind)] * (shards - 1),
            (*crosses, *text, *nears[1:], *from_shards),
            scratch=[
                pltpu.VMEM((heads, shards * rows, text_rows), kind),
                pltpu.VMEM((heads, shards * rows, HD), jnp.float32),
            ],
        )
        cross_back = [moved(a, 0, 0, -turn - 1) for turn, a in enumerate(cross_away)]

        def place_kernel(spots, size, *refs):
            run_all(
                [
                    (ref, place_of(shift, turn, refs[-2], size))
                    for (shift, turn), ref in zip(spots, refs[:-2])
                ],
                refs[-1],
            )

        def cross_place_kernel(*refs):
            copies = []
            for turn, ref in enumerate(refs[:-2]):
                shard = lax.rem(lax.axis_index("head") + turn, shards)
                if turn == 0:
                    start = pl.multiple_of(shard * cols, HD)
                    copies.append((ref, refs[-2].at[0, :, pl.ds(start, cols)]))
                    continue
                for part in range(share):
                    start = pl.multiple_of(shard * cols + part * width, HD)
                    block = ref.at[pl.ds(part * rows, rows)]
                    copies.append((block, refs[-2].at[0, :, pl.ds(start, width)]))
            run_all(copies, refs[-1])

        whole = jax.ShapeDtypeStruct((1, rows, full), kind)
        cross_mixed = call(
            cross_place_kernel,
            "place_cross",
            whole,
            (cross_own, *cross_back),
            hbm,
            scratch=[pltpu.SemaphoreType.DMA((1 + (shards - 1) * share,))],
        )

        def near_kernel(*refs):
            own_ref, others, (sums_ref, logs_ref, weights_ref, shares_ref) = refs[0], refs[1:-4], refs[-4:]

            def rows_of(index, head):
                place, head = divmod(head, share_heads)
                lanes = head_lanes(head)
                start = (3 * place + index) * rows
                found = [own_ref[start : start + rows, lanes]]
                start = (share + 2 * place + index - 1) * rows
                for ref in others if index > 0 else ():
                    found.append(ref[start : start + rows, lanes])
                return jnp.concatenate(found, axis=0)

            for head in range(near_width // HD):
                scores = scores_of(rows_of(0, head), rows_of(1, head))
                weights_ref[head], shares_ref[head], logs_ref[head] = softmax_parts(scores)
            for head in range(near_width // HD):
                sums = weighted(weights_ref[head], rows_of(2, head))
                sums_ref[:, head_lanes(head)] = sums * shares_ref[head]

        near = []
        if near_blocks:
            near = call(
                near_kernel,
                "near",
                [
                    pltpu.VMEM((rows, near_width), jnp.float32),
                    pltpu.VMEM((near_width // HD, rows, HD), jnp.float32),
                ],
                (nears[0], *cross_back),
                scratch=[
                    pltpu.VMEM((near_width // HD, rows, everyone), kind),
                    pltpu.VMEM((near_width // HD, rows, HD), jnp.float32),
                ],
            )

        spots = [(0, 0)] + mates
        tokens = [own, *arrived]
        first_row = dict(zip(spots, [0] + [fresh_start(*mate) for mate in mates]))

        def token_rows(refs, shift, index, lanes):
            found = []
            for spot, ref in zip(spots, refs):
                if spot[0] == shift:
                    start = first_row[spot] + index * rows
                    found.append(ref[start : start + rows, lanes])
            return found

        def stale_of(refs, shift, index, lanes):
            own_stale, *others = refs[len(spots) :]
            found = []
            if shift != 0:
                found.append(own_stale)
            found += [
                ref for (other, turn), ref in zip(spots, refs) if turn == 0 and other not in (0, shift)
            ]
            block = slice(index * patch_rows, (index + 1) * patch_rows)
            return [ref[block, lanes] for ref in found + others]

        def weights_kernel(*refs):
            count = len(spots) + 1 + len(pieces)
            sources, targets, logs_of = refs[:count], refs[count:], {}
            for head in range(share_heads):
                lanes = head_lanes(head)
                for shift in range(share):
                    queries = token_rows(sources, shift, 0, lanes)
                    keys = stale_of(sources, shift, 0, lanes)
                    if shift == 0:
                        keys = token_rows(sources, shift, 1, lanes) + keys
                    weights, shares, logs = softmax_parts(
                        scores_of(jnp.concatenate(queries, axis=0), jnp.concatenate(keys, axis=0))
                    )
                    for turn in range(shards):
                        spot = spots.index((shift, turn))
                        block = slice(turn * rows, (turn + 1) * rows)
                        targets[2 * spot][head] = weights[block]
                        targets[2 * spot + 1][head] = shares[block]
                        logs_of.setdefault(spot, []).append(logs[block])
            for place, mate in enumerate(over_patch):
                targets[2 * len(spots) + place][...] = lanes_of_logs(logs_of[spots.index(mate)])

        def mix_kernel(shift, weights_ref, shares_ref, *refs):
            sources, target = refs[:-1], refs[-1]
            for head in range(share_heads):
                lanes = head_lanes(head)
                values = stale_of(sources, shift, 1, lanes)
                if shift == 0:
                    values = token_rows(sources, shift, 2, lanes) + values
                mixed = weighted(weights_ref[head], jnp.concatenate(values, axis=0))
                target[:, lanes] = (mixed * shares_ref[head]).astype(target.dtype)

        def mate_mix_kernel(shift, weights_ref, shares_ref, logs_ref, *refs):
            mix_kernel(shift, weights_ref, shares_ref, *refs[:-1], refs[-1].at[:, pl.ds(0, width)])
            refs[-1][:, width:] = logs_ref[...]

        def merge_kernel(*refs):
            (sums_ref, logs_ref), refs = refs[:2], refs[2:]
            for (shift, turn), far, target in zip(over_patch, refs, refs[len(over_patch) :]):
                first = near_blocks.index((turn, shift)) * share_heads
                for head in range(share_heads):
                    lanes = head_lanes(head)
                    far_logs, near_logs = logs_of_lanes(far[:, width:], head), logs_ref[first + head]
                    tops = jnp.maximum(far_logs, near_logs)
                    far_part, near_part = jnp.exp(far_logs - tops), jnp.exp(near_logs - tops)
                    mixed = far[:, lanes].astype(jnp.float32) * far_part
                    mixed += sums_ref[:, head_lanes(first + head)] * near_part
                    target[:, lanes] = (mixed / (far_part + near_part)).astype(target.dtype)

        sources = (*tokens, stale[0], *pieces)
        part_shapes = []
        for shift, _ in spots:
            seen = patch_rows * (patches if shift == 0 else patches - 1)
            part_shapes += [
                pltpu.VMEM((share_heads, rows, seen), kind),
                pltpu.VMEM((share_heads, rows, HD), jnp.float32),
            ]
        parts = call(
            weights_kernel,
            "weights",
            part_shapes + [pltpu.VMEM((rows, HD), kind)] * len(over_patch),
            sources,
            cost_estimate=pl.CostEstimate(flops=2000000000, bytes_accessed=7200000, transcendentals=0),
        )

        def mixed(spot):
            pair, shift = parts[2 * spot : 2 * spot + 2], spots[spot][0]
            if shift == 0:
                kernel, shape = mix_kernel, (rows, width)
            else:
                kernel, shape = mate_mix_kernel, (rows, width + HD)
                pair = (*pair, parts[2 * len(spots) + over_patch.index(spots[spot])])
            return call(
                lambda *refs: kernel(shift, *refs), "mix", pltpu.VMEM(shape, kind), (*pair, *sources)
            )

        back = [
            moved(mixed(index), 0, -shift, -turn)
            for index, (shift, turn) in enumerate(spots)
            if index > 0
        ]
        if over_patch:
            back[shards - 1 :] = call(
                merge_kernel,
                "merge",
                [pltpu.VMEM((rows, width), kind)] * len(over_patch),
                (*near, *back[shards - 1 :]),
            )
        self_mixed = call(
            lambda *refs: place_kernel(spots, width, *refs),
            "place_self",
            whole,
            (mixed(0), *back),
            hbm,
            scratch=[pltpu.SemaphoreType.DMA((len(spots),))],
        )
        return (self_mixed, cross_mixed)

    token = P(("group", "cfg"), ("patch", "head"), None)
    stale = P(("group", "cfg"), "patch", "head")
    text = P(("group", "cfg"), None, "head")
    return jax.shard_map(
        per_device,
        mesh=mesh,
        in_specs=(token, token, token, stale, stale, token, text, text, P(("group", "cfg"), None)),
        out_specs=(token, token),
        check_vma=False,
    )
```

```python
import math

import jax
import jax.numpy as jnp
from jax import lax
from jax.experimental import pallas as pl
from jax.experimental.pallas import tpu as pltpu
from jax.sharding import PartitionSpec as P

HD = 128
SCALE = 1.0 / math.sqrt(HD)
TERMS = 3


def scores_of(queries, keys):
    return lax.dot_general(
        queries, keys, (((1,), (1,)), ((), ())), preferred_element_type=jnp.float32
    ) * SCALE


def weighted(weights, values):
    return lax.dot_general(
        weights, values, (((1,), (0,)), ((), ())), preferred_element_type=jnp.float32
    )


def softmax_parts(scores):
    tops = jnp.max(scores, axis=-1, keepdims=True)
    weights = jnp.exp(scores - tops)
    totals = jnp.sum(weights, axis=-1, keepdims=True)
    shape = (scores.shape[0], HD)
    shares = jnp.broadcast_to(1.0 / totals, shape)
    logs = jnp.broadcast_to(tops + jnp.log(totals), shape)
    return weights.astype(jnp.bfloat16), shares, logs


def lanes_of_logs(logs):
    lane = lax.broadcasted_iota(jnp.int32, logs[0].shape, 1)
    block = jnp.zeros(logs[0].shape, jnp.float32)
    for head, rest in enumerate(logs):
        for term in range(TERMS):
            part = rest.astype(jnp.bfloat16).astype(jnp.float32)
            block = jnp.where(lane == TERMS * head + term, part, block)
            rest = rest - part
    return block.astype(jnp.bfloat16)


def logs_of_lanes(block, head):
    lane = lax.broadcasted_iota(jnp.int32, (HD, HD), 0)
    picked = (lane >= TERMS * head) & (lane < TERMS * (head + 1))
    return weighted(block, jnp.where(picked, 1.0, 0.0).astype(block.dtype))


def run_all(copies, sems):
    started = []
    for index, (source, target) in enumerate(copies):
        started.append(pltpu.make_async_copy(source, target, sems.at[index]))
        started[-1].start()
    for copy in started:
        copy.wait()


def load_kernel(*refs):
    half = len(refs) // 2
    run_all(zip(refs[:half], refs[half:-1]), refs[-1])


def gate_kernel(*refs):
    pass


def head_lanes(head):
    return slice(head * HD, (head + 1) * HD)


def cross_kernel(shards, nears, *refs):
    queries, (key_ref, value_ref, mask_ref) = refs[:shards], refs[shards : shards + 3]
    own, away, (weights_ref, shares_ref) = refs[-2 - shards], refs[-1 - shards : -2], refs[-2:]
    rows, cols = own.shape
    usable = mask_ref[...] > 0
    for head in range(cols // HD):
        lanes = head_lanes(head)
        scores = scores_of(
            jnp.concatenate([ref[:, lanes] for ref in queries], axis=0), key_ref[0, :, lanes]
        )
        weights_ref[head], shares_ref[head], _ = softmax_parts(
            jnp.where(usable, scores, -jnp.inf)
        )
    for source, target in zip(refs[shards + 3 : shards + 3 + nears], away):
        target[target.shape[0] - source.shape[0] :, :] = source[...]
    for head in range(cols // HD):
        lanes = head_lanes(head)
        mixed = weighted(weights_ref[head], value_ref[0, :, lanes]) * shares_ref[head]
        own[:, lanes] = mixed[:rows].astype(own.dtype)
        for turn, target in enumerate(away, 1):
            part, inner = divmod(head * HD, target.shape[1])
            block = slice(part * rows, (part + 1) * rows)
            mine = mixed[turn * rows : (turn + 1) * rows].astype(target.dtype)
            target[block, inner : inner + HD] = mine


def solution(mesh):
    shards = mesh.shape["head"]
    patches = mesh.shape["patch"]
    axes = ("patch", "head")
    vmem = pl.BlockSpec(memory_space=pltpu.VMEM)
    hbm = pl.BlockSpec(memory_space=pltpu.HBM)
    anywhere = pl.BlockSpec(memory_space=pl.ANY)
    params = pltpu.CompilerParams(vmem_limit_bytes=32 * 1024 * 1024)

    def call(kernel, name, out_shape, operands, out_spec=vmem, in_spec=vmem, scratch=(), **more):
        return pl.pallas_call(
            kernel,
            out_shape=out_shape,
            in_specs=[in_spec] * len(operands),
            out_specs=jax.tree.map(lambda _: out_spec, out_shape),
            scratch_shapes=scratch,
            compiler_params=params,
            name=name,
            **more,
        )(*operands)

    def in_hbm(*arrays):
        return [pltpu.with_memory_space_constraint(a, pltpu.HBM) for a in arrays]

    def handed_on(arrays, **more):
        return call(
            gate_kernel,
            "gate",
            [jax.ShapeDtypeStruct(a.shape, a.dtype) for a in arrays],
            arrays,
            anywhere,
            anywhere,
            input_output_aliases={i: i for i in range(len(arrays))},
            **more,
        )

    def per_device(
        fresh_query,
        fresh_key,
        fresh_value,
        stale_key,
        stale_value,
        cross_query,
        text_key,
        text_value,
        text_mask,
    ):
        rows, full = fresh_query.shape[1:]
        everyone = rows * shards
        patch_rows = stale_key.shape[1]
        text_rows = text_key.shape[1]
        kind = fresh_query.dtype
        cols = full // shards
        heads = cols // HD
        share = math.gcd(patches, heads)
        teams = patches // share
        width = cols // share
        share_heads = heads // share
        mates = [(j, s) for j in range(share) for s in range(shards) if (j, s) != (0, 0)]

        ring = list(range(0, teams, 2)) + list(range(1, teams, 2))[::-1]
        ring_next = dict(zip(ring, ring[1:] + ring[:1]))

        def moved(array, step, shift, turn):
            pairs = []
            for patch in range(patches):
                team, member = divmod(patch, share)
                team = ring_next[team] if step else team
                target = team * share + (member + shift) % share
                for shard in range(shards):
                    pairs.append(
                        (patch * shards + shard, target * shards + (shard + turn) % shards)
                    )
            return lax.ppermute(array, axes, pairs)

        def place_of(shift, turn, ref, size):
            shard = lax.rem(lax.axis_index("head") + turn, shards)
            member = lax.rem(lax.axis_index("patch") + shift, share)
            start = pl.multiple_of(shard * cols + member * width, HD)
            return ref.at[0, :, pl.ds(start, size)]

        over_patch = [mate for mate in mates if mate[0] != 0]
        near_blocks = [(turn, shift) for turn in range(shards) for shift in range(1, share)]
        near_width = len(near_blocks) * width
        back_rows = (share + 2 * len(near_blocks)) * rows
        stale_rows = 2 * patch_rows

        def fresh_start(shift, turn):
            return stale_rows if turn == 0 and shift != 0 else 0

        def message_rows(shift, turn):
            return fresh_start(shift, turn) + (3 if shift == 0 else 1) * rows

        def pack_kernel(query, key, value, old_key, old_value, cross, *refs):
            stale, own, refs = refs[:share], refs[share], refs[share + 1 :]
            crosses, messages = refs[:shards], refs[shards : shards + len(mates)]
            nears = refs[shards + len(mates) : -1]
            me = lax.rem(lax.axis_index("patch"), share)
            copies = []

            def stale_copies(shift, target):
                part = lax.rem(me + shift, share)
                lanes = pl.ds(pl.multiple_of(part * width, HD), width)
                for index, source in enumerate((old_key, old_value)):
                    block = pl.ds(index * patch_rows, patch_rows)
                    copies.append((source.at[0, :, lanes], target.at[block]))

            def fresh_copies(shift, turn, target, first):
                for index, source in enumerate((query, key, value)[: 3 if shift == 0 else 1]):
                    block = pl.ds(first + index * rows, rows)
                    copies.append((place_of(shift, turn, source, width), target.at[block]))

            for (shift, turn), message in zip(mates, messages):
                first = fresh_start(shift, turn)
                if first:
                    stale_copies(shift, message)
                fresh_copies(shift, turn, message, first)
            for shift in range(share):
                stale_copies(shift, stale[shift])
            fresh_copies(0, 0, own, 0)
            for turn, target in enumerate(crosses):
                shard = lax.rem(lax.axis_index("head") + turn, shards)
                lanes = pl.ds(pl.multiple_of(shard * cols, HD), cols)
                copies.append((cross.at[0, :, lanes], target))
            for turn, target in enumerate(nears):
                for place, (other, shift) in enumerate(near_blocks):
                    for index, source in enumerate((query, key, value)):
                        if turn == 0:
                            block = pl.ds((3 * place + index) * rows, rows)
                        elif index > 0:
                            block = pl.ds((2 * place + index - 1) * rows, rows)
                        else:
                            continue
                        spot = place_of(shift, other + shards - turn, source, width)
                        copies.append((spot, target.at[block]))
            run_all(copies, refs[-1])

        packed_shapes = (
            [(stale_rows, width)] * share
            + [(3 * rows, width)]
            + [(rows, cols)] * shards
            + [(message_rows(*mate), width) for mate in mates]
        )
        if near_blocks:
            near_rows = [3 * rows * len(near_blocks)] + [2 * rows * len(near_blocks)] * (shards - 1)
            packed_shapes += [(height, width) for height in near_rows]
        copy_count = 2 * share + 3 + shards + sum(
            (3 if mate[0] == 0 else 1) + (2 if fresh_start(*mate) else 0) for mate in mates
        )
        copy_count += len(near_blocks) * (2 * shards + 1)
        packed = call(
            pack_kernel,
            "pack",
            [pltpu.VMEM(shape, kind) for shape in packed_shapes],
            in_hbm(fresh_query, fresh_key, fresh_value, stale_key, stale_value, cross_query),
            in_spec=hbm,
            scratch=[pltpu.SemaphoreType.DMA((copy_count,))],
        )
        stale, own, packed = packed[:share], packed[share], packed[share + 1 :]
        crosses, messages = packed[:shards], packed[shards : shards + len(mates)]
        nears = packed[shards + len(mates) :]
        text = [text_key, text_value, text_mask]
        text = call(
            load_kernel,
            "load",
            [pltpu.VMEM(a.shape, a.dtype) for a in text],
            in_hbm(*text),
            in_spec=hbm,
            scratch=[pltpu.SemaphoreType.DMA((len(text),))],
        )


        arrived = [
            moved(message, 0, *mate) for mate, message in zip(mates, messages)
        ]
        crosses = [crosses[0]] + [moved(a, 0, 0, turn) for turn, a in enumerate(crosses) if turn]

        pieces = []
        if teams > 1:
            latest = [moved(stale[shift], 1, shift, 0) for shift in range(share)]
            pieces += latest
            for _ in range(teams - 2):
                latest = [moved(piece, 1, 0, 0) for piece in latest]
                pieces += latest

        cost = pl.CostEstimate(flops=500000000, bytes_accessed=1800000, transcendentals=0)
        pieces = handed_on(pieces, cost_estimate=cost) if pieces else pieces
        cost = pl.CostEstimate(flops=1000000000, bytes_accessed=3600000, transcendentals=0)
        for index, (shift, turn) in enumerate(mates):
            if shift and turn:
                arrived[index] = handed_on([arrived[index]], cost_estimate=cost)[0]

        from_shards = [a for (shift, _), a in zip(mates, arrived) if shift == 0]
        cross_own, *cross_away = call(
            lambda *refs: cross_kernel(shards, len(nears[1:]), *refs),
            "cross",
            [pltpu.VMEM((rows, cols), kind)]
            + [pltpu.VMEM((back_rows, width), kind)] * (shards - 1),
            (*crosses, *text, *nears[1:], *from_shards),
            scratch=[
                pltpu.VMEM((heads, shards * rows, text_rows), kind),
                pltpu.VMEM((heads, shards * rows, HD), jnp.float32),
            ],
        )
        cross_back = [moved(a, 0, 0, -turn - 1) for turn, a in enumerate(cross_away)]

        def place_kernel(spots, size, *refs):
            run_all(
                [
                    (ref, place_of(shift, turn, refs[-2], size))
                    for (shift, turn), ref in zip(spots, refs[:-2])
                ],
                refs[-1],
            )

        def cross_place_kernel(*refs):
            copies = []
            for turn, ref in enumerate(refs[:-2]):
                shard = lax.rem(lax.axis_index("head") + turn, shards)
                if turn == 0:
                    start = pl.multiple_of(shard * cols, HD)
                    copies.append((ref, refs[-2].at[0, :, pl.ds(start, cols)]))
                    continue
                for part in range(share):
                    start = pl.multiple_of(shard * cols + part * width, HD)
                    block = ref.at[pl.ds(part * rows, rows)]
                    copies.append((block, refs[-2].at[0, :, pl.ds(start, width)]))
            run_all(copies, refs[-1])

        whole = jax.ShapeDtypeStruct((1, rows, full), kind)
        cross_mixed = call(
            cross_place_kernel,
            "place_cross",
            whole,
            (cross_own, *cross_back),
            hbm,
            scratch=[pltpu.SemaphoreType.DMA((1 + (shards - 1) * share,))],
        )

        def near_kernel(*refs):
            own_ref, others, (sums_ref, logs_ref, weights_ref, shares_ref) = refs[0], refs[1:-4], refs[-4:]

            def rows_of(index, head):
                place, head = divmod(head, share_heads)
                lanes = head_lanes(head)
                start = (3 * place + index) * rows
                found = [own_ref[start : start + rows, lanes]]
                start = (share + 2 * place + index - 1) * rows
                for ref in others if index > 0 else ():
                    found.append(ref[start : start + rows, lanes])
                return jnp.concatenate(found, axis=0)

            for head in range(near_width // HD):
                scores = scores_of(rows_of(0, head), rows_of(1, head))
                weights_ref[head], shares_ref[head], logs_ref[head] = softmax_parts(scores)
            for head in range(near_width // HD):
                sums = weighted(weights_ref[head], rows_of(2, head))
                sums_ref[:, head_lanes(head)] = sums * shares_ref[head]

        near = []
        if near_blocks:
            near = call(
                near_kernel,
                "near",
                [
                    pltpu.VMEM((rows, near_width), jnp.float32),
                    pltpu.VMEM((near_width // HD, rows, HD), jnp.float32),
                ],
                (nears[0], *cross_back),
                scratch=[
                    pltpu.VMEM((near_width // HD, rows, everyone), kind),
                    pltpu.VMEM((near_width // HD, rows, HD), jnp.float32),
                ],
            )

        spots = [(0, 0)] + mates
        tokens = [own, *arrived]
        first_row = dict(zip(spots, [0] + [fresh_start(*mate) for mate in mates]))

        def token_rows(refs, shift, index, lanes):
            found = []
            for spot, ref in zip(spots, refs):
                if spot[0] == shift:
                    start = first_row[spot] + index * rows
                    found.append(ref[start : start + rows, lanes])
            return found

        def stale_of(refs, shift, index, lanes):
            own_stale, *others = refs[len(spots) :]
            found = []
            if shift != 0:
                found.append(own_stale)
            found += [
                ref for (other, turn), ref in zip(spots, refs) if turn == 0 and other not in (0, shift)
            ]
            block = slice(index * patch_rows, (index + 1) * patch_rows)
            return [ref[block, lanes] for ref in found + others]

        def weights_kernel(*refs):
            count = len(spots) + 1 + len(pieces)
            sources, targets, logs_of = refs[:count], refs[count:], {}
            for head in range(share_heads):
                lanes = head_lanes(head)
                for shift in range(share):
                    queries = token_rows(sources, shift, 0, lanes)
                    keys = stale_of(sources, shift, 0, lanes)
                    if shift == 0:
                        keys = token_rows(sources, shift, 1, lanes) + keys
                    weights, shares, logs = softmax_parts(
                        scores_of(jnp.concatenate(queries, axis=0), jnp.concatenate(keys, axis=0))
                    )
                    for turn in range(shards):
                        spot = spots.index((shift, turn))
                        block = slice(turn * rows, (turn + 1) * rows)
                        targets[2 * spot][head] = weights[block]
                        targets[2 * spot + 1][head] = shares[block]
                        logs_of.setdefault(spot, []).append(logs[block])
            for place, mate in enumerate(over_patch):
                targets[2 * len(spots) + place][...] = lanes_of_logs(logs_of[spots.index(mate)])

        def mix_kernel(shift, weights_ref, shares_ref, *refs):
            sources, target = refs[:-1], refs[-1]
            for head in range(share_heads):
                lanes = head_lanes(head)
                values = stale_of(sources, shift, 1, lanes)
                if shift == 0:
                    values = token_rows(sources, shift, 2, lanes) + values
                mixed = weighted(weights_ref[head], jnp.concatenate(values, axis=0))
                target[:, lanes] = (mixed * shares_ref[head]).astype(target.dtype)

        def mate_mix_kernel(shift, weights_ref, shares_ref, logs_ref, *refs):
            mix_kernel(shift, weights_ref, shares_ref, *refs[:-1], refs[-1].at[:, pl.ds(0, width)])
            refs[-1][:, width:] = logs_ref[...]

        def merge_kernel(*refs):
            (sums_ref, logs_ref), refs = refs[:2], refs[2:]
            for (shift, turn), far, target in zip(over_patch, refs, refs[len(over_patch) :]):
                first = near_blocks.index((turn, shift)) * share_heads
                for head in range(share_heads):
                    lanes = head_lanes(head)
                    far_logs, near_logs = logs_of_lanes(far[:, width:], head), logs_ref[first + head]
                    tops = jnp.maximum(far_logs, near_logs)
                    far_part, near_part = jnp.exp(far_logs - tops), jnp.exp(near_logs - tops)
                    mixed = far[:, lanes].astype(jnp.float32) * far_part
                    mixed += sums_ref[:, head_lanes(first + head)] * near_part
                    target[:, lanes] = (mixed / (far_part + near_part)).astype(target.dtype)

        sources = (*tokens, stale[0], *pieces)
        part_shapes = []
        for shift, _ in spots:
            seen = patch_rows * (patches if shift == 0 else patches - 1)
            part_shapes += [
                pltpu.VMEM((share_heads, rows, seen), kind),
                pltpu.VMEM((share_heads, rows, HD), jnp.float32),
            ]
        parts = call(
            weights_kernel,
            "weights",
            part_shapes + [pltpu.VMEM((rows, HD), kind)] * len(over_patch),
            sources,
            cost_estimate=pl.CostEstimate(flops=2000000000, bytes_accessed=7200000, transcendentals=0),
        )

        def mixed(spot):
            pair, shift = parts[2 * spot : 2 * spot + 2], spots[spot][0]
            if shift == 0:
                kernel, shape = mix_kernel, (rows, width)
            else:
                kernel, shape = mate_mix_kernel, (rows, width + HD)
                pair = (*pair, parts[2 * len(spots) + over_patch.index(spots[spot])])
            return call(
                lambda *refs: kernel(shift, *refs), "mix", pltpu.VMEM(shape, kind), (*pair, *sources)
            )

        back = [
            moved(mixed(index), 0, -shift, -turn)
            for index, (shift, turn) in enumerate(spots)
            if index > 0
        ]
        if over_patch:
            back[shards - 1 :] = call(
                merge_kernel,
                "merge",
                [pltpu.VMEM((rows, width), kind)] * len(over_patch),
                (*near, *back[shards - 1 :]),
            )
        self_mixed = call(
            lambda *refs: place_kernel(spots, width, *refs),
            "place_self",
            whole,
            (mixed(0), *back),
            hbm,
            scratch=[pltpu.SemaphoreType.DMA((len(spots),))],
        )
        return (self_mixed, cross_mixed)

    token = P(("group", "cfg"), ("patch", "head"), None)
    stale = P(("group", "cfg"), "patch", "head")
    text = P(("group", "cfg"), None, "head")
    return jax.shard_map(
        per_device,
        mesh=mesh,
        in_specs=(token, token, token, stale, stale, token, text, text, P(("group", "cfg"), None)),
        out_specs=(token, token),
        check_vma=False,
    )
```

```python
import math

import jax
import jax.numpy as jnp
from jax import lax
from jax.experimental import pallas as pl
from jax.experimental.pallas import tpu as pltpu
from jax.sharding import PartitionSpec as P

HD = 128
SCALE = 1.0 / math.sqrt(HD)
TERMS = 3


def scores_of(queries, keys):
    return lax.dot_general(
        queries, keys, (((1,), (1,)), ((), ())), preferred_element_type=jnp.float32
    ) * SCALE


def weighted(weights, values):
    return lax.dot_general(
        weights, values, (((1,), (0,)), ((), ())), preferred_element_type=jnp.float32
    )


def softmax_parts(scores):
    tops = jnp.max(scores, axis=-1, keepdims=True)
    weights = jnp.exp(scores - tops)
    totals = jnp.sum(weights, axis=-1, keepdims=True)
    shape = (scores.shape[0], HD)
    shares = jnp.broadcast_to(1.0 / totals, shape)
    logs = jnp.broadcast_to(tops + jnp.log(totals), shape)
    return weights.astype(jnp.bfloat16), shares, logs


def lanes_of_logs(logs):
    lane = lax.broadcasted_iota(jnp.int32, logs[0].shape, 1)
    block = jnp.zeros(logs[0].shape, jnp.float32)
    for head, rest in enumerate(logs):
        for term in range(TERMS):
            part = rest.astype(jnp.bfloat16).astype(jnp.float32)
            block = jnp.where(lane == TERMS * head + term, part, block)
            rest = rest - part
    return block.astype(jnp.bfloat16)


def logs_of_lanes(block, head):
    lane = lax.broadcasted_iota(jnp.int32, (HD, HD), 0)
    picked = (lane >= TERMS * head) & (lane < TERMS * (head + 1))
    return weighted(block, jnp.where(picked, 1.0, 0.0).astype(block.dtype))


def run_all(copies, sems):
    started = []
    for index, (source, target) in enumerate(copies):
        started.append(pltpu.make_async_copy(source, target, sems.at[index]))
        started[-1].start()
    for copy in started:
        copy.wait()


def load_kernel(*refs):
    half = len(refs) // 2
    run_all(zip(refs[:half], refs[half:-1]), refs[-1])


def gate_kernel(*refs):
    pass


def head_lanes(head):
    return slice(head * HD, (head + 1) * HD)


def cross_kernel(shards, nears, *refs):
    queries, (key_ref, value_ref, mask_ref) = refs[:shards], refs[shards : shards + 3]
    own, away, (weights_ref, shares_ref) = refs[-2 - shards], refs[-1 - shards : -2], refs[-2:]
    rows, cols = own.shape
    usable = mask_ref[...] > 0
    for head in range(cols // HD):
        lanes = head_lanes(head)
        scores = scores_of(
            jnp.concatenate([ref[:, lanes] for ref in queries], axis=0), key_ref[0, :, lanes]
        )
        weights_ref[head], shares_ref[head], _ = softmax_parts(
            jnp.where(usable, scores, -jnp.inf)
        )
    for source, target in zip(refs[shards + 3 : shards + 3 + nears], away):
        target[target.shape[0] - source.shape[0] :, :] = source[...]
    for head in range(cols // HD):
        lanes = head_lanes(head)
        mixed = weighted(weights_ref[head], value_ref[0, :, lanes]) * shares_ref[head]
        own[:, lanes] = mixed[:rows].astype(own.dtype)
        for turn, target in enumerate(away, 1):
            part, inner = divmod(head * HD, target.shape[1])
            block = slice(part * rows, (part + 1) * rows)
            mine = mixed[turn * rows : (turn + 1) * rows].astype(target.dtype)
            target[block, inner : inner + HD] = mine


def solution(mesh):
    shards = mesh.shape["head"]
    patches = mesh.shape["patch"]
    axes = ("patch", "head")
    vmem = pl.BlockSpec(memory_space=pltpu.VMEM)
    hbm = pl.BlockSpec(memory_space=pltpu.HBM)
    anywhere = pl.BlockSpec(memory_space=pl.ANY)
    params = pltpu.CompilerParams(vmem_limit_bytes=32 * 1024 * 1024)

    def call(kernel, name, out_shape, operands, out_spec=vmem, in_spec=vmem, scratch=(), **more):
        return pl.pallas_call(
            kernel,
            out_shape=out_shape,
            in_specs=[in_spec] * len(operands),
            out_specs=jax.tree.map(lambda _: out_spec, out_shape),
            scratch_shapes=scratch,
            compiler_params=params,
            name=name,
            **more,
        )(*operands)

    def in_hbm(*arrays):
        return [pltpu.with_memory_space_constraint(a, pltpu.HBM) for a in arrays]

    def handed_on(arrays, **more):
        return call(
            gate_kernel,
            "gate",
            [jax.ShapeDtypeStruct(a.shape, a.dtype) for a in arrays],
            arrays,
            anywhere,
            anywhere,
            input_output_aliases={i: i for i in range(len(arrays))},
            **more,
        )

    def per_device(
        fresh_query,
        fresh_key,
        fresh_value,
        stale_key,
        stale_value,
        cross_query,
        text_key,
        text_value,
        text_mask,
    ):
        rows, full = fresh_query.shape[1:]
        everyone = rows * shards
        patch_rows = stale_key.shape[1]
        text_rows = text_key.shape[1]
        kind = fresh_query.dtype
        cols = full // shards
        heads = cols // HD
        share = math.gcd(patches, heads)
        teams = patches // share
        width = cols // share
        share_heads = heads // share
        mates = [(j, s) for j in range(share) for s in range(shards) if (j, s) != (0, 0)]

        ring = list(range(0, teams, 2)) + list(range(1, teams, 2))[::-1]
        ring_next = dict(zip(ring, ring[1:] + ring[:1]))

        def moved(array, step, shift, turn):
            pairs = []
            for patch in range(patches):
                team, member = divmod(patch, share)
                team = ring_next[team] if step else team
                target = team * share + (member + shift) % share
                for shard in range(shards):
                    pairs.append(
                        (patch * shards + shard, target * shards + (shard + turn) % shards)
                    )
            return lax.ppermute(array, axes, pairs)

        def place_of(shift, turn, ref, size):
            shard = lax.rem(lax.axis_index("head") + turn, shards)
            member = lax.rem(lax.axis_index("patch") + shift, share)
            start = pl.multiple_of(shard * cols + member * width, HD)
            return ref.at[0, :, pl.ds(start, size)]

        over_patch = [mate for mate in mates if mate[0] != 0]
        near_blocks = [(turn, shift) for turn in range(shards) for shift in range(1, share)]
        near_width = len(near_blocks) * width
        back_rows = (share + 2 * len(near_blocks)) * rows
        stale_rows = 2 * patch_rows

        def fresh_start(shift, turn):
            return stale_rows if turn == 0 and shift != 0 else 0

        def message_rows(shift, turn):
            return fresh_start(shift, turn) + (3 if shift == 0 else 1) * rows

        def pack_kernel(query, key, value, old_key, old_value, cross, *refs):
            stale, own, refs = refs[:share], refs[share], refs[share + 1 :]
            crosses, messages = refs[:shards], refs[shards : shards + len(mates)]
            nears = refs[shards + len(mates) : -1]
            me = lax.rem(lax.axis_index("patch"), share)
            copies = []

            def stale_copies(shift, target):
                part = lax.rem(me + shift, share)
                lanes = pl.ds(pl.multiple_of(part * width, HD), width)
                for index, source in enumerate((old_key, old_value)):
                    block = pl.ds(index * patch_rows, patch_rows)
                    copies.append((source.at[0, :, lanes], target.at[block]))

            def fresh_copies(shift, turn, target, first):
                for index, source in enumerate((query, key, value)[: 3 if shift == 0 else 1]):
                    block = pl.ds(first + index * rows, rows)
                    copies.append((place_of(shift, turn, source, width), target.at[block]))

            for (shift, turn), message in zip(mates, messages):
                first = fresh_start(shift, turn)
                if first:
                    stale_copies(shift, message)
                fresh_copies(shift, turn, message, first)
            for shift in range(share):
                stale_copies(shift, stale[shift])
            fresh_copies(0, 0, own, 0)
            for turn, target in enumerate(crosses):
                shard = lax.rem(lax.axis_index("head") + turn, shards)
                lanes = pl.ds(pl.multiple_of(shard * cols, HD), cols)
                copies.append((cross.at[0, :, lanes], target))
            for turn, target in enumerate(nears):
                for place, (other, shift) in enumerate(near_blocks):
                    for index, source in enumerate((query, key, value)):
                        if turn == 0:
                            block = pl.ds((3 * place + index) * rows, rows)
                        elif index > 0:
                            block = pl.ds((2 * place + index - 1) * rows, rows)
                        else:
                            continue
                        spot = place_of(shift, other + shards - turn, source, width)
                        copies.append((spot, target.at[block]))
            run_all(copies, refs[-1])

        packed_shapes = (
            [(stale_rows, width)] * share
            + [(3 * rows, width)]
            + [(rows, cols)] * shards
            + [(message_rows(*mate), width) for mate in mates]
        )
        if near_blocks:
            near_rows = [3 * rows * len(near_blocks)] + [2 * rows * len(near_blocks)] * (shards - 1)
            packed_shapes += [(height, width) for height in near_rows]
        copy_count = 2 * share + 3 + shards + sum(
            (3 if mate[0] == 0 else 1) + (2 if fresh_start(*mate) else 0) for mate in mates
        )
        copy_count += len(near_blocks) * (2 * shards + 1)
        packed = call(
            pack_kernel,
            "pack",
            [pltpu.VMEM(shape, kind) for shape in packed_shapes],
            in_hbm(fresh_query, fresh_key, fresh_value, stale_key, stale_value, cross_query),
            in_spec=hbm,
            scratch=[pltpu.SemaphoreType.DMA((copy_count,))],
        )
        stale, own, packed = packed[:share], packed[share], packed[share + 1 :]
        crosses, messages = packed[:shards], packed[shards : shards + len(mates)]
        nears = packed[shards + len(mates) :]
        text = [text_key, text_value, text_mask]
        text = call(
            load_kernel,
            "load",
            [pltpu.VMEM(a.shape, a.dtype) for a in text],
            in_hbm(*text),
            in_spec=hbm,
            scratch=[pltpu.SemaphoreType.DMA((len(text),))],
        )


        arrived = [
            moved(message, 0, *mate) for mate, message in zip(mates, messages)
        ]
        crosses = [crosses[0]] + [moved(a, 0, 0, turn) for turn, a in enumerate(crosses) if turn]

        pieces = []
        if teams > 1:
            latest = [moved(stale[shift], 1, shift, 0) for shift in range(share)]
            pieces += latest
            for _ in range(teams - 2):
                latest = [moved(piece, 1, 0, 0) for piece in latest]
                pieces += latest

        cost = pl.CostEstimate(flops=500000000, bytes_accessed=1800000, transcendentals=0)
        pieces = handed_on(pieces, cost_estimate=cost) if pieces else pieces

        from_shards = [a for (shift, _), a in zip(mates, arrived) if shift == 0]
        cross_own, *cross_away = call(
            lambda *refs: cross_kernel(shards, len(nears[1:]), *refs),
            "cross",
            [pltpu.VMEM((rows, cols), kind)]
            + [pltpu.VMEM((back_rows, width), kind)] * (shards - 1),
            (*crosses, *text, *nears[1:], *from_shards),
            scratch=[
                pltpu.VMEM((heads, shards * rows, text_rows), kind),
                pltpu.VMEM((heads, shards * rows, HD), jnp.float32),
            ],
        )
        cross_back = [moved(a, 0, 0, -turn - 1) for turn, a in enumerate(cross_away)]

        def place_kernel(spots, size, *refs):
            run_all(
                [
                    (ref, place_of(shift, turn, refs[-2], size))
                    for (shift, turn), ref in zip(spots, refs[:-2])
                ],
                refs[-1],
            )

        def cross_place_kernel(*refs):
            copies = []
            for turn, ref in enumerate(refs[:-2]):
                shard = lax.rem(lax.axis_index("head") + turn, shards)
                if turn == 0:
                    start = pl.multiple_of(shard * cols, HD)
                    copies.append((ref, refs[-2].at[0, :, pl.ds(start, cols)]))
                    continue
                for part in range(share):
                    start = pl.multiple_of(shard * cols + part * width, HD)
                    block = ref.at[pl.ds(part * rows, rows)]
                    copies.append((block, refs[-2].at[0, :, pl.ds(start, width)]))
            run_all(copies, refs[-1])

        whole = jax.ShapeDtypeStruct((1, rows, full), kind)
        cross_mixed = call(
            cross_place_kernel,
            "place_cross",
            whole,
            (cross_own, *cross_back),
            hbm,
            scratch=[pltpu.SemaphoreType.DMA((1 + (shards - 1) * share,))],
        )

        def near_kernel(*refs):
            own_ref, others, (sums_ref, logs_ref, weights_ref, shares_ref) = refs[0], refs[1:-4], refs[-4:]

            def rows_of(index, head):
                place, head = divmod(head, share_heads)
                lanes = head_lanes(head)
                start = (3 * place + index) * rows
                found = [own_ref[start : start + rows, lanes]]
                start = (share + 2 * place + index - 1) * rows
                for ref in others if index > 0 else ():
                    found.append(ref[start : start + rows, lanes])
                return jnp.concatenate(found, axis=0)

            for head in range(near_width // HD):
                scores = scores_of(rows_of(0, head), rows_of(1, head))
                weights_ref[head], shares_ref[head], logs_ref[head] = softmax_parts(scores)
            for head in range(near_width // HD):
                sums = weighted(weights_ref[head], rows_of(2, head))
                sums_ref[:, head_lanes(head)] = sums * shares_ref[head]

        near = []
        if near_blocks:
            near = call(
                near_kernel,
                "near",
                [
                    pltpu.VMEM((rows, near_width), jnp.float32),
                    pltpu.VMEM((near_width // HD, rows, HD), jnp.float32),
                ],
                (nears[0], *cross_back),
                scratch=[
                    pltpu.VMEM((near_width // HD, rows, everyone), kind),
                    pltpu.VMEM((near_width // HD, rows, HD), jnp.float32),
                ],
            )

        spots = [(0, 0)] + mates
        tokens = [own, *arrived]
        first_row = dict(zip(spots, [0] + [fresh_start(*mate) for mate in mates]))

        def token_rows(refs, shift, index, lanes):
            found = []
            for spot, ref in zip(spots, refs):
                if spot[0] == shift:
                    start = first_row[spot] + index * rows
                    found.append(ref[start : start + rows, lanes])
            return found

        def stale_of(refs, shift, index, lanes):
            own_stale, *others = refs[len(spots) :]
            found = []
            if shift != 0:
                found.append(own_stale)
            found += [
                ref for (other, turn), ref in zip(spots, refs) if turn == 0 and other not in (0, shift)
            ]
            block = slice(index * patch_rows, (index + 1) * patch_rows)
            return [ref[block, lanes] for ref in found + others]

        def weights_kernel(group, *refs):
            count = len(spots) + 1 + len(pieces)
            sources, targets, logs_of = refs[:count], refs[-3 * len(group) :], {}
            for head in range(share_heads):
                lanes = head_lanes(head)
                for shift in sorted({spot[0] for spot in group}):
                    turns = [turn for other, turn in group if other == shift]
                    queries = token_rows(sources, shift, 0, lanes)
                    queries = jnp.concatenate([queries[turn] for turn in turns], axis=0)
                    keys = stale_of(sources, shift, 0, lanes)
                    if shift == 0:
                        keys = token_rows(sources, shift, 1, lanes) + keys
                    weights, shares, logs = softmax_parts(
                        scores_of(queries, jnp.concatenate(keys, axis=0))
                    )
                    for place, turn in enumerate(turns):
                        spot = group.index((shift, turn))
                        block = slice(place * rows, (place + 1) * rows)
                        targets[3 * spot][head] = weights[block]
                        targets[3 * spot + 1][head] = shares[block]
                        logs_of.setdefault(spot, []).append(logs[block])
            for spot in range(len(group)):
                targets[3 * spot + 2][...] = lanes_of_logs(logs_of[spot])

        def mix_kernel(shift, weights_ref, shares_ref, *refs):
            sources, target = refs[:-1], refs[-1]
            for head in range(share_heads):
                lanes = head_lanes(head)
                values = stale_of(sources, shift, 1, lanes)
                if shift == 0:
                    values = token_rows(sources, shift, 2, lanes) + values
                mixed = weighted(weights_ref[head], jnp.concatenate(values, axis=0))
                target[:, lanes] = (mixed * shares_ref[head]).astype(target.dtype)

        def mate_mix_kernel(shift, weights_ref, shares_ref, logs_ref, *refs):
            mix_kernel(shift, weights_ref, shares_ref, *refs[:-1], refs[-1].at[:, pl.ds(0, width)])
            refs[-1][:, width:] = logs_ref[...]

        def merge_kernel(*refs):
            (sums_ref, logs_ref), refs = refs[:2], refs[2:]
            for (shift, turn), far, target in zip(over_patch, refs, refs[len(over_patch) :]):
                first = near_blocks.index((turn, shift)) * share_heads
                for head in range(share_heads):
                    lanes = head_lanes(head)
                    far_logs, near_logs = logs_of_lanes(far[:, width:], head), logs_ref[first + head]
                    tops = jnp.maximum(far_logs, near_logs)
                    far_part, near_part = jnp.exp(far_logs - tops), jnp.exp(near_logs - tops)
                    mixed = far[:, lanes].astype(jnp.float32) * far_part
                    mixed += sums_ref[:, head_lanes(first + head)] * near_part
                    target[:, lanes] = (mixed / (far_part + near_part)).astype(target.dtype)

        sources = (*tokens, stale[0], *pieces)
        diagonal = [spot for spot in over_patch if spot[1]]
        prompt = [spot for spot in spots if spot not in diagonal]
        parts = {}

        def make_weights(group, *others, **more):
            shapes = []
            for shift, _ in group:
                seen = patch_rows * (patches if shift == 0 else patches - 1)
                shapes += [
                    pltpu.VMEM((share_heads, rows, seen), kind),
                    pltpu.VMEM((share_heads, rows, HD), jnp.float32),
                    pltpu.VMEM((rows, HD), kind),
                ]
            made = call(
                lambda *refs: weights_kernel(group, *refs),
                "weights",
                shapes,
                (*sources, *others),
                **more,
            )
            parts.update({spot: made[3 * i : 3 * i + 3] for i, spot in enumerate(group)})

        def mixed(spot):
            weights, shares, logs = parts[spot]
            if spot[0] == 0:
                kernel, shape, operands = mix_kernel, (rows, width), (weights, shares)
            else:
                kernel, shape, operands = mate_mix_kernel, (rows, width + HD), parts[spot]
            return call(
                lambda *refs: kernel(spot[0], *refs),
                "mix",
                pltpu.VMEM(shape, kind),
                (*operands, *sources),
            )

        now = sources
        absent = [sources[spots.index(spot)] for spot in diagonal]
        sources = tuple(own if any(a is late for late in absent) else a for a in now)
        make_weights(prompt, cost_estimate=pl.CostEstimate(flops=2000000000, bytes_accessed=7200000, transcendentals=0))
        ready = {spot: mixed(spot) for spot in prompt if spot != (0, 0)}
        sources = now
        if diagonal:
            make_weights(diagonal, *ready.values())
        ready.update({spot: mixed(spot) for spot in diagonal})
        back = [moved(ready[spot], 0, -spot[0], -spot[1]) for spot in spots[1:]]
        sources = tuple(own if any(a is late for late in absent) else a for a in now)
        if over_patch:
            back[shards - 1 :] = call(
                merge_kernel,
                "merge",
                [pltpu.VMEM((rows, width), kind)] * len(over_patch),
                (*near, *back[shards - 1 :]),
            )
        self_mixed = call(
            lambda *refs: place_kernel(spots, width, *refs),
            "place_self",
            whole,
            (mixed((0, 0)), *back),
            hbm,
            scratch=[pltpu.SemaphoreType.DMA((len(spots),))],
        )
        return (self_mixed, cross_mixed)

    token = P(("group", "cfg"), ("patch", "head"), None)
    stale = P(("group", "cfg"), "patch", "head")
    text = P(("group", "cfg"), None, "head")
    return jax.shard_map(
        per_device,
        mesh=mesh,
        in_specs=(token, token, token, stale, stale, token, text, text, P(("group", "cfg"), None)),
        out_specs=(token, token),
        check_vma=False,
    )
```

```python
import math

import jax
import jax.numpy as jnp
from jax import lax
from jax.experimental import pallas as pl
from jax.experimental.pallas import tpu as pltpu
from jax.sharding import PartitionSpec as P

HD = 128
SCALE = 1.0 / math.sqrt(HD)
TERMS = 3


def scores_of(queries, keys):
    return lax.dot_general(
        queries, keys, (((1,), (1,)), ((), ())), preferred_element_type=jnp.float32
    ) * SCALE


def weighted(weights, values):
    return lax.dot_general(
        weights, values, (((1,), (0,)), ((), ())), preferred_element_type=jnp.float32
    )


def softmax_parts(scores):
    tops = jnp.max(scores, axis=-1, keepdims=True)
    weights = jnp.exp(scores - tops)
    totals = jnp.sum(weights, axis=-1, keepdims=True)
    shape = (scores.shape[0], HD)
    shares = jnp.broadcast_to(1.0 / totals, shape)
    logs = jnp.broadcast_to(tops + jnp.log(totals), shape)
    return weights.astype(jnp.bfloat16), shares, logs


def lanes_of_logs(logs):
    lane = lax.broadcasted_iota(jnp.int32, logs[0].shape, 1)
    block = jnp.zeros(logs[0].shape, jnp.float32)
    for head, rest in enumerate(logs):
        for term in range(TERMS):
            part = rest.astype(jnp.bfloat16).astype(jnp.float32)
            block = jnp.where(lane == TERMS * head + term, part, block)
            rest = rest - part
    return block.astype(jnp.bfloat16)


def logs_of_lanes(block, head):
    lane = lax.broadcasted_iota(jnp.int32, (HD, HD), 0)
    picked = (lane >= TERMS * head) & (lane < TERMS * (head + 1))
    return weighted(block, jnp.where(picked, 1.0, 0.0).astype(block.dtype))


def run_all(copies, sems):
    started = []
    for index, (source, target) in enumerate(copies):
        started.append(pltpu.make_async_copy(source, target, sems.at[index]))
        started[-1].start()
    for copy in started:
        copy.wait()


def load_kernel(*refs):
    half = len(refs) // 2
    run_all(zip(refs[:half], refs[half:-1]), refs[-1])


def gate_kernel(*refs):
    pass


def head_lanes(head):
    return slice(head * HD, (head + 1) * HD)


def cross_kernel(shards, nears, *refs):
    queries, (key_ref, value_ref, mask_ref) = refs[:shards], refs[shards : shards + 3]
    own, away, (weights_ref, shares_ref) = refs[-2 - shards], refs[-1 - shards : -2], refs[-2:]
    rows, cols = own.shape
    usable = mask_ref[...] > 0
    for head in range(cols // HD):
        lanes = head_lanes(head)
        scores = scores_of(
            jnp.concatenate([ref[:, lanes] for ref in queries], axis=0), key_ref[0, :, lanes]
        )
        weights_ref[head], shares_ref[head], _ = softmax_parts(
            jnp.where(usable, scores, -jnp.inf)
        )
    for source, target in zip(refs[shards + 3 : shards + 3 + nears], away):
        target[target.shape[0] - source.shape[0] :, :] = source[...]
    for head in range(cols // HD):
        lanes = head_lanes(head)
        mixed = weighted(weights_ref[head], value_ref[0, :, lanes]) * shares_ref[head]
        own[:, lanes] = mixed[:rows].astype(own.dtype)
        for turn, target in enumerate(away, 1):
            part, inner = divmod(head * HD, target.shape[1])
            block = slice(part * rows, (part + 1) * rows)
            mine = mixed[turn * rows : (turn + 1) * rows].astype(target.dtype)
            target[block, inner : inner + HD] = mine


def solution(mesh):
    shards = mesh.shape["head"]
    patches = mesh.shape["patch"]
    axes = ("patch", "head")
    vmem = pl.BlockSpec(memory_space=pltpu.VMEM)
    hbm = pl.BlockSpec(memory_space=pltpu.HBM)
    anywhere = pl.BlockSpec(memory_space=pl.ANY)
    params = pltpu.CompilerParams(vmem_limit_bytes=32 * 1024 * 1024)

    def call(kernel, name, out_shape, operands, out_spec=vmem, in_spec=vmem, scratch=(), **more):
        return pl.pallas_call(
            kernel,
            out_shape=out_shape,
            in_specs=[in_spec] * len(operands),
            out_specs=jax.tree.map(lambda _: out_spec, out_shape),
            scratch_shapes=scratch,
            compiler_params=params,
            name=name,
            **more,
        )(*operands)

    def in_hbm(*arrays):
        return [pltpu.with_memory_space_constraint(a, pltpu.HBM) for a in arrays]

    def handed_on(arrays, **more):
        return call(
            gate_kernel,
            "gate",
            [jax.ShapeDtypeStruct(a.shape, a.dtype) for a in arrays],
            arrays,
            anywhere,
            anywhere,
            input_output_aliases={i: i for i in range(len(arrays))},
            **more,
        )

    def per_device(
        fresh_query,
        fresh_key,
        fresh_value,
        stale_key,
        stale_value,
        cross_query,
        text_key,
        text_value,
        text_mask,
    ):
        rows, full = fresh_query.shape[1:]
        everyone = rows * shards
        patch_rows = stale_key.shape[1]
        text_rows = text_key.shape[1]
        kind = fresh_query.dtype
        cols = full // shards
        heads = cols // HD
        share = math.gcd(patches, heads)
        teams = patches // share
        width = cols // share
        share_heads = heads // share
        mates = [(j, s) for j in range(share) for s in range(shards) if (j, s) != (0, 0)]

        ring = list(range(0, teams, 2)) + list(range(1, teams, 2))[::-1]
        ring_next = dict(zip(ring, ring[1:] + ring[:1]))

        def moved(array, step, shift, turn):
            pairs = []
            for patch in range(patches):
                team, member = divmod(patch, share)
                team = ring_next[team] if step else team
                target = team * share + (member + shift) % share
                for shard in range(shards):
                    pairs.append(
                        (patch * shards + shard, target * shards + (shard + turn) % shards)
                    )
            return lax.ppermute(array, axes, pairs)

        def place_of(shift, turn, ref, size):
            shard = lax.rem(lax.axis_index("head") + turn, shards)
            member = lax.rem(lax.axis_index("patch") + shift, share)
            start = pl.multiple_of(shard * cols + member * width, HD)
            return ref.at[0, :, pl.ds(start, size)]

        over_patch = [mate for mate in mates if mate[0] != 0]
        near_blocks = [(turn, shift) for turn in range(shards) for shift in range(1, share)]
        near_width = len(near_blocks) * width
        back_rows = (share + 2 * len(near_blocks)) * rows
        stale_rows = 2 * patch_rows

        def fresh_start(shift, turn):
            return stale_rows if turn == 0 and shift != 0 else 0

        def message_rows(shift, turn):
            return fresh_start(shift, turn) + (3 if shift == 0 else 1) * rows

        def pack_kernel(query, key, value, old_key, old_value, cross, *refs):
            stale, own, refs = refs[:share], refs[share], refs[share + 1 :]
            crosses, messages = refs[:shards], refs[shards : shards + len(mates)]
            nears = refs[shards + len(mates) : -1]
            me = lax.rem(lax.axis_index("patch"), share)
            copies = []

            def stale_copies(shift, target):
                part = lax.rem(me + shift, share)
                lanes = pl.ds(pl.multiple_of(part * width, HD), width)
                for index, source in enumerate((old_key, old_value)):
                    block = pl.ds(index * patch_rows, patch_rows)
                    copies.append((source.at[0, :, lanes], target.at[block]))

            def fresh_copies(shift, turn, target, first):
                for index, source in enumerate((query, key, value)[: 3 if shift == 0 else 1]):
                    block = pl.ds(first + index * rows, rows)
                    copies.append((place_of(shift, turn, source, width), target.at[block]))

            for (shift, turn), message in zip(mates, messages):
                first = fresh_start(shift, turn)
                if first:
                    stale_copies(shift, message)
                fresh_copies(shift, turn, message, first)
            for shift in range(share):
                stale_copies(shift, stale[shift])
            fresh_copies(0, 0, own, 0)
            for turn, target in enumerate(crosses):
                shard = lax.rem(lax.axis_index("head") + turn, shards)
                lanes = pl.ds(pl.multiple_of(shard * cols, HD), cols)
                copies.append((cross.at[0, :, lanes], target))
            for turn, target in enumerate(nears):
                for place, (other, shift) in enumerate(near_blocks):
                    for index, source in enumerate((query, key, value)):
                        if turn == 0:
                            block = pl.ds((3 * place + index) * rows, rows)
                        elif index > 0:
                            block = pl.ds((2 * place + index - 1) * rows, rows)
                        else:
                            continue
                        spot = place_of(shift, other + shards - turn, source, width)
                        copies.append((spot, target.at[block]))
            run_all(copies, refs[-1])

        packed_shapes = (
            [(stale_rows, width)] * share
            + [(3 * rows, width)]
            + [(rows, cols)] * shards
            + [(message_rows(*mate), width) for mate in mates]
        )
        if near_blocks:
            near_rows = [3 * rows * len(near_blocks)] + [2 * rows * len(near_blocks)] * (shards - 1)
            packed_shapes += [(height, width) for height in near_rows]
        copy_count = 2 * share + 3 + shards + sum(
            (3 if mate[0] == 0 else 1) + (2 if fresh_start(*mate) else 0) for mate in mates
        )
        copy_count += len(near_blocks) * (2 * shards + 1)
        packed = call(
            pack_kernel,
            "pack",
            [pltpu.VMEM(shape, kind) for shape in packed_shapes],
            in_hbm(fresh_query, fresh_key, fresh_value, stale_key, stale_value, cross_query),
            in_spec=hbm,
            scratch=[pltpu.SemaphoreType.DMA((copy_count,))],
        )
        stale, own, packed = packed[:share], packed[share], packed[share + 1 :]
        crosses, messages = packed[:shards], packed[shards : shards + len(mates)]
        nears = packed[shards + len(mates) :]
        text = [text_key, text_value, text_mask]
        text = call(
            load_kernel,
            "load",
            [pltpu.VMEM(a.shape, a.dtype) for a in text],
            in_hbm(*text),
            in_spec=hbm,
            scratch=[pltpu.SemaphoreType.DMA((len(text),))],
        )


        arrived = [
            moved(message, 0, *mate) for mate, message in zip(mates, messages)
        ]
        crosses = [crosses[0]] + [moved(a, 0, 0, turn) for turn, a in enumerate(crosses) if turn]

        pieces = []
        if teams > 1:
            latest = [moved(stale[shift], 1, shift, 0) for shift in range(share)]
            pieces += latest
            for _ in range(teams - 2):
                latest = [moved(piece, 1, 0, 0) for piece in latest]
                pieces += latest

        cost = pl.CostEstimate(flops=500000000, bytes_accessed=1800000, transcendentals=0)
        pieces = handed_on(pieces, cost_estimate=cost) if pieces else pieces

        from_shards = [a for (shift, _), a in zip(mates, arrived) if shift == 0]
        cross_own, *cross_away = call(
            lambda *refs: cross_kernel(shards, len(nears[1:]), *refs),
            "cross",
            [pltpu.VMEM((rows, cols), kind)]
            + [pltpu.VMEM((back_rows, width), kind)] * (shards - 1),
            (*crosses, *text, *nears[1:], *from_shards),
            scratch=[
                pltpu.VMEM((heads, shards * rows, text_rows), kind),
                pltpu.VMEM((heads, shards * rows, HD), jnp.float32),
            ],
        )
        cross_back = [moved(a, 0, 0, -turn - 1) for turn, a in enumerate(cross_away)]

        def place_kernel(spots, size, *refs):
            run_all(
                [
                    (ref, place_of(shift, turn, refs[-2], size))
                    for (shift, turn), ref in zip(spots, refs[:-2])
                ],
                refs[-1],
            )

        def cross_place_kernel(*refs):
            copies = []
            for turn, ref in enumerate(refs[:-2]):
                shard = lax.rem(lax.axis_index("head") + turn, shards)
                if turn == 0:
                    start = pl.multiple_of(shard * cols, HD)
                    copies.append((ref, refs[-2].at[0, :, pl.ds(start, cols)]))
                    continue
                for part in range(share):
                    start = pl.multiple_of(shard * cols + part * width, HD)
                    block = ref.at[pl.ds(part * rows, rows)]
                    copies.append((block, refs[-2].at[0, :, pl.ds(start, width)]))
            run_all(copies, refs[-1])

        whole = jax.ShapeDtypeStruct((1, rows, full), kind)
        cross_mixed = call(
            cross_place_kernel,
            "place_cross",
            whole,
            (cross_own, *cross_back),
            hbm,
            scratch=[pltpu.SemaphoreType.DMA((1 + (shards - 1) * share,))],
        )

        def near_kernel(*refs):
            own_ref, others, (sums_ref, logs_ref, weights_ref, shares_ref) = refs[0], refs[1:-4], refs[-4:]

            def rows_of(index, head):
                place, head = divmod(head, share_heads)
                lanes = head_lanes(head)
                start = (3 * place + index) * rows
                found = [own_ref[start : start + rows, lanes]]
                start = (share + 2 * place + index - 1) * rows
                for ref in others if index > 0 else ():
                    found.append(ref[start : start + rows, lanes])
                return jnp.concatenate(found, axis=0)

            for head in range(near_width // HD):
                scores = scores_of(rows_of(0, head), rows_of(1, head))
                weights_ref[head], shares_ref[head], logs_ref[head] = softmax_parts(scores)
            for head in range(near_width // HD):
                sums = weighted(weights_ref[head], rows_of(2, head))
                sums_ref[:, head_lanes(head)] = sums * shares_ref[head]

        near = []
        if near_blocks:
            near = call(
                near_kernel,
                "near",
                [
                    pltpu.VMEM((rows, near_width), jnp.float32),
                    pltpu.VMEM((near_width // HD, rows, HD), jnp.float32),
                ],
                (nears[0], *cross_back),
                scratch=[
                    pltpu.VMEM((near_width // HD, rows, everyone), kind),
                    pltpu.VMEM((near_width // HD, rows, HD), jnp.float32),
                ],
            )

        spots = [(0, 0)] + mates
        tokens = [own, *arrived]
        first_row = dict(zip(spots, [0] + [fresh_start(*mate) for mate in mates]))

        def token_rows(refs, shift, index, lanes):
            found = []
            for spot, ref in zip(spots, refs):
                if spot[0] == shift:
                    start = first_row[spot] + index * rows
                    found.append(ref[start : start + rows, lanes])
            return found

        def stale_of(refs, shift, index, lanes):
            own_stale, *others = refs[len(spots) :]
            found = []
            if shift != 0:
                found.append(own_stale)
            found += [
                ref for (other, turn), ref in zip(spots, refs) if turn == 0 and other not in (0, shift)
            ]
            block = slice(index * patch_rows, (index + 1) * patch_rows)
            return [ref[block, lanes] for ref in found + others]

        def weights_kernel(group, *refs):
            count = len(spots) + 1 + len(pieces)
            sources, targets, logs_of = refs[:count], refs[-3 * len(group) :], {}
            for head in range(share_heads):
                lanes = head_lanes(head)
                for shift in sorted({spot[0] for spot in group}):
                    turns = [turn for other, turn in group if other == shift]
                    queries = token_rows(sources, shift, 0, lanes)
                    queries = jnp.concatenate([queries[turn] for turn in turns], axis=0)
                    keys = stale_of(sources, shift, 0, lanes)
                    if shift == 0:
                        keys = token_rows(sources, shift, 1, lanes) + keys
                    weights, shares, logs = softmax_parts(
                        scores_of(queries, jnp.concatenate(keys, axis=0))
                    )
                    for place, turn in enumerate(turns):
                        spot = group.index((shift, turn))
                        block = slice(place * rows, (place + 1) * rows)
                        targets[3 * spot][head] = weights[block]
                        targets[3 * spot + 1][head] = shares[block]
                        if shift > 0:
                            logs_of.setdefault(spot, []).append(logs[block])
            for spot, (shift, _) in enumerate(group):
                if shift == 0:
                    targets[3 * spot + 2][...] = jnp.zeros_like(targets[3 * spot + 2])
            for spot, logs in logs_of.items():
                targets[3 * spot + 2][...] = lanes_of_logs(logs)

        def mix_kernel(shift, weights_ref, shares_ref, *refs):
            sources, target = refs[:-1], refs[-1]
            for head in range(share_heads):
                lanes = head_lanes(head)
                values = stale_of(sources, shift, 1, lanes)
                if shift == 0:
                    values = token_rows(sources, shift, 2, lanes) + values
                mixed = weighted(weights_ref[head], jnp.concatenate(values, axis=0))
                target[:, lanes] = (mixed * shares_ref[head]).astype(target.dtype)

        def mate_mix_kernel(shift, weights_ref, shares_ref, logs_ref, *refs):
            mix_kernel(shift, weights_ref, shares_ref, *refs[:-1], refs[-1].at[:, pl.ds(0, width)])
            refs[-1][:, width:] = logs_ref[...]

        def merge_kernel(*refs):
            (sums_ref, logs_ref), refs = refs[:2], refs[2:]
            for (shift, turn), far, target in zip(over_patch, refs, refs[len(over_patch) :]):
                first = near_blocks.index((turn, shift)) * share_heads
                for head in range(share_heads):
                    lanes = head_lanes(head)
                    far_logs, near_logs = logs_of_lanes(far[:, width:], head), logs_ref[first + head]
                    tops = jnp.maximum(far_logs, near_logs)
                    far_part, near_part = jnp.exp(far_logs - tops), jnp.exp(near_logs - tops)
                    mixed = far[:, lanes].astype(jnp.float32) * far_part
                    mixed += sums_ref[:, head_lanes(first + head)] * near_part
                    target[:, lanes] = (mixed / (far_part + near_part)).astype(target.dtype)

        sources = (*tokens, stale[0], *pieces)
        diagonal = [spot for spot in over_patch if spot[1]]
        prompt = [spot for spot in spots if spot not in diagonal]
        parts = {}

        def make_weights(group, *others, **more):
            shapes = []
            for shift, _ in group:
                seen = patch_rows * (patches if shift == 0 else patches - 1)
                shapes += [
                    pltpu.VMEM((share_heads, rows, seen), kind),
                    pltpu.VMEM((share_heads, rows, HD), jnp.float32),
                    pltpu.VMEM((rows, HD) if shift > 0 else (HD // 8, HD), kind),
                ]
            made = call(
                lambda *refs: weights_kernel(group, *refs),
                "weights",
                shapes,
                (*sources, *others),
                **more,
            )
            parts.update({spot: made[3 * i : 3 * i + 3] for i, spot in enumerate(group)})

        def mixed(spot):
            weights, shares, logs = parts[spot]
            if spot[0] == 0:
                kernel, shape, operands = mix_kernel, (rows, width), (weights, shares)
            else:
                kernel, shape, operands = mate_mix_kernel, (rows, width + HD), parts[spot]
            return call(
                lambda *refs: kernel(spot[0], *refs),
                "mix",
                pltpu.VMEM(shape, kind),
                (*operands, *sources),
            )

        now = sources
        absent = [sources[spots.index(spot)] for spot in diagonal]
        sources = tuple(own if any(a is late for late in absent) else a for a in now)
        make_weights(prompt, cost_estimate=pl.CostEstimate(flops=2000000000, bytes_accessed=7200000, transcendentals=0))
        ready = {spot: mixed(spot) for spot in prompt if spot != (0, 0)}
        sources = now
        if diagonal:
            make_weights(diagonal, *ready.values())
        ready.update({spot: mixed(spot) for spot in diagonal})
        back = [moved(ready[spot], 0, -spot[0], -spot[1]) for spot in spots[1:]]
        sources = tuple(own if any(a is late for late in absent) else a for a in now)
        if over_patch:
            back[shards - 1 :] = call(
                merge_kernel,
                "merge",
                [pltpu.VMEM((rows, width), kind)] * len(over_patch),
                (*near, *back[shards - 1 :]),
            )
        self_mixed = call(
            lambda *refs: place_kernel(spots, width, *refs),
            "place_self",
            whole,
            (mixed((0, 0)), *back),
            hbm,
            scratch=[pltpu.SemaphoreType.DMA((len(spots),))],
        )
        return (self_mixed, cross_mixed)

    token = P(("group", "cfg"), ("patch", "head"), None)
    stale = P(("group", "cfg"), "patch", "head")
    text = P(("group", "cfg"), None, "head")
    return jax.shard_map(
        per_device,
        mesh=mesh,
        in_specs=(token, token, token, stale, stale, token, text, text, P(("group", "cfg"), None)),
        out_specs=(token, token),
        check_vma=False,
    )
```

```python
import math

import jax
import jax.numpy as jnp
from jax import lax
from jax.experimental import pallas as pl
from jax.experimental.pallas import tpu as pltpu
from jax.sharding import PartitionSpec as P

HD = 128
SCALE = 1.0 / math.sqrt(HD)
TERMS = 3


def scores_of(queries, keys):
    return lax.dot_general(
        queries, keys, (((1,), (1,)), ((), ())), preferred_element_type=jnp.float32
    ) * SCALE


def weighted(weights, values):
    return lax.dot_general(
        weights, values, (((1,), (0,)), ((), ())), preferred_element_type=jnp.float32
    )


def softmax_parts(scores):
    tops = jnp.max(scores, axis=-1, keepdims=True)
    weights = jnp.exp(scores - tops)
    totals = jnp.sum(weights, axis=-1, keepdims=True)
    shape = (scores.shape[0], HD)
    shares = jnp.broadcast_to(1.0 / totals, shape)
    logs = jnp.broadcast_to(tops + jnp.log(totals), shape)
    return weights.astype(jnp.bfloat16), shares, logs


def lanes_of_logs(logs):
    lane = lax.broadcasted_iota(jnp.int32, logs[0].shape, 1)
    block = jnp.zeros(logs[0].shape, jnp.float32)
    for head, rest in enumerate(logs):
        for term in range(TERMS):
            part = rest.astype(jnp.bfloat16).astype(jnp.float32)
            block = jnp.where(lane == TERMS * head + term, part, block)
            rest = rest - part
    return block.astype(jnp.bfloat16)


def logs_of_lanes(block, head):
    lane = lax.broadcasted_iota(jnp.int32, (HD, HD), 0)
    picked = (lane >= TERMS * head) & (lane < TERMS * (head + 1))
    return weighted(block, jnp.where(picked, 1.0, 0.0).astype(block.dtype))


def run_all(copies, sems):
    started = []
    for index, (source, target) in enumerate(copies):
        started.append(pltpu.make_async_copy(source, target, sems.at[index]))
        started[-1].start()
    for copy in started:
        copy.wait()


def load_kernel(*refs):
    half = len(refs) // 2
    run_all(zip(refs[:half], refs[half:-1]), refs[-1])


def gate_kernel(*refs):
    pass


def head_lanes(head):
    return slice(head * HD, (head + 1) * HD)


def cross_kernel(shards, *refs):
    queries, (key_ref, value_ref, mask_ref) = refs[:shards], refs[shards : shards + 3]
    targets, (weights_ref, shares_ref) = refs[2 * shards + 2 : -2], refs[-2:]
    rows, cols = targets[0].shape
    usable = mask_ref[...] > 0
    for head in range(cols // HD):
        lanes = head_lanes(head)
        scores = scores_of(
            jnp.concatenate([ref[:, lanes] for ref in queries], axis=0), key_ref[0, :, lanes]
        )
        weights_ref[head], shares_ref[head], _ = softmax_parts(
            jnp.where(usable, scores, -jnp.inf)
        )
    for head in range(cols // HD):
        lanes = head_lanes(head)
        mixed = weighted(weights_ref[head], value_ref[0, :, lanes]) * shares_ref[head]
        for place, target in enumerate(targets):
            target[:, lanes] = mixed[place * rows : (place + 1) * rows].astype(target.dtype)


def solution(mesh):
    shards = mesh.shape["head"]
    patches = mesh.shape["patch"]
    axes = ("patch", "head")
    vmem = pl.BlockSpec(memory_space=pltpu.VMEM)
    hbm = pl.BlockSpec(memory_space=pltpu.HBM)
    anywhere = pl.BlockSpec(memory_space=pl.ANY)
    params = pltpu.CompilerParams(vmem_limit_bytes=32 * 1024 * 1024)

    def call(kernel, name, out_shape, operands, out_spec=vmem, in_spec=vmem, scratch=(), **more):
        return pl.pallas_call(
            kernel,
            out_shape=out_shape,
            in_specs=[in_spec] * len(operands),
            out_specs=jax.tree.map(lambda _: out_spec, out_shape),
            scratch_shapes=scratch,
            compiler_params=params,
            name=name,
            **more,
        )(*operands)

    def in_hbm(*arrays):
        return [pltpu.with_memory_space_constraint(a, pltpu.HBM) for a in arrays]

    def handed_on(arrays, others=(), **more):
        return call(
            gate_kernel,
            "gate",
            [jax.ShapeDtypeStruct(a.shape, a.dtype) for a in arrays],
            (*arrays, *others),
            anywhere,
            anywhere,
            input_output_aliases={i: i for i in range(len(arrays))},
            **more,
        )

    def per_device(
        fresh_query,
        fresh_key,
        fresh_value,
        stale_key,
        stale_value,
        cross_query,
        text_key,
        text_value,
        text_mask,
    ):
        rows, full = fresh_query.shape[1:]
        everyone = rows * shards
        patch_rows = stale_key.shape[1]
        text_rows = text_key.shape[1]
        kind = fresh_query.dtype
        cols = full // shards
        heads = cols // HD
        share = math.gcd(patches, heads)
        teams = patches // share
        width = cols // share
        share_heads = heads // share
        mates = [(j, s) for j in range(share) for s in range(shards) if (j, s) != (0, 0)]

        ring = list(range(0, teams, 2)) + list(range(1, teams, 2))[::-1]
        ring_next = dict(zip(ring, ring[1:] + ring[:1]))

        def moved(array, step, shift, turn):
            pairs = []
            for patch in range(patches):
                team, member = divmod(patch, share)
                team = ring_next[team] if step else team
                target = team * share + (member + shift) % share
                for shard in range(shards):
                    pairs.append(
                        (patch * shards + shard, target * shards + (shard + turn) % shards)
                    )
            return lax.ppermute(array, axes, pairs)

        def place_of(shift, turn, ref, size):
            shard = lax.rem(lax.axis_index("head") + turn, shards)
            member = lax.rem(lax.axis_index("patch") + shift, share)
            start = pl.multiple_of(shard * cols + member * width, HD)
            return ref.at[0, :, pl.ds(start, size)]

        over_patch = [mate for mate in mates if mate[0] != 0]
        near_blocks = [(turn, shift) for turn in range(shards) for shift in range(1, share)]
        near_width = len(near_blocks) * width
        stale_rows = 2 * patch_rows

        def fresh_start(shift, turn):
            return stale_rows if turn == 0 and shift != 0 else 0

        def message_rows(shift, turn):
            return fresh_start(shift, turn) + (3 if shift == 0 else 1) * rows

        def stale_copies(shift, sources, target):
            part = lax.rem(lax.axis_index("patch") + shift, share)
            lanes = pl.ds(pl.multiple_of(part * width, HD), width)
            return [
                (source.at[0, :, lanes], target.at[pl.ds(index * patch_rows, patch_rows)])
                for index, source in enumerate(sources)
            ]

        def stale_kernel(*refs):
            copies = []
            for shift in range(share):
                copies += stale_copies(shift, refs[:2], refs[2 + shift])
            run_all(copies, refs[-1])

        stale = call(
            stale_kernel,
            "pack_stale",
            [pltpu.VMEM((stale_rows, width), kind)] * share,
            in_hbm(stale_key, stale_value),
            in_spec=hbm,
            scratch=[pltpu.SemaphoreType.DMA((2 * share,))],
        )

        def pack_kernel(query, key, value, old_key, old_value, cross, *refs):
            own, refs = refs[0], refs[1:]
            crosses, messages = refs[:shards], refs[shards : shards + len(mates)]
            nears = refs[shards + len(mates) : -1]
            copies = []

            def fresh_copies(shift, turn, target, first):
                for index, source in enumerate((query, key, value)[: 3 if shift == 0 else 1]):
                    block = pl.ds(first + index * rows, rows)
                    copies.append((place_of(shift, turn, source, width), target.at[block]))

            for (shift, turn), message in zip(mates, messages):
                first = fresh_start(shift, turn)
                if first:
                    copies.extend(stale_copies(shift, (old_key, old_value), message))
                fresh_copies(shift, turn, message, first)
            fresh_copies(0, 0, own, 0)
            for turn, target in enumerate(crosses):
                shard = lax.rem(lax.axis_index("head") + turn, shards)
                lanes = pl.ds(pl.multiple_of(shard * cols, HD), cols)
                copies.append((cross.at[0, :, lanes], target))
            for turn, target in enumerate(nears):
                for index, source in enumerate((query, key, value)[0 if turn == 0 else 1 :]):
                    for place, (other, shift) in enumerate(near_blocks):
                        block = target.at[pl.ds(index * rows, rows), pl.ds(place * width, width)]
                        copies.append((place_of(shift, turn + other, source, width), block))
            run_all(copies, refs[-1])

        packed_shapes = (
            [(3 * rows, width)]
            + [(rows, cols)] * shards
            + [(message_rows(*mate), width) for mate in mates]
        )
        if near_blocks:
            packed_shapes += [(3 * rows, near_width)] + [(2 * rows, near_width)] * (shards - 1)
        copy_count = 3 + shards + sum(
            (3 if mate[0] == 0 else 1) + (2 if fresh_start(*mate) else 0) for mate in mates
        )
        copy_count += len(near_blocks) * (2 * shards + 1)
        packed = call(
            pack_kernel,
            "pack",
            [pltpu.VMEM(shape, kind) for shape in packed_shapes],
            in_hbm(fresh_query, fresh_key, fresh_value, stale_key, stale_value, cross_query),
            in_spec=hbm,
            scratch=[pltpu.SemaphoreType.DMA((copy_count,))],
        )
        own, packed = packed[0], packed[1:]
        crosses, messages = packed[:shards], packed[shards : shards + len(mates)]
        nears = packed[shards + len(mates) :]
        text = [text_key, text_value, text_mask]
        text = call(
            load_kernel,
            "load",
            [pltpu.VMEM(a.shape, a.dtype) for a in text],
            in_hbm(*text),
            in_spec=hbm,
            scratch=[pltpu.SemaphoreType.DMA((len(text),))],
        )

        nears = [
            moved(handed_on([a], text[-1:])[0], 0, 0, turn) if turn else a
            for turn, a in enumerate(nears)
        ]
        arrived = [
            moved(message, 0, *mate) for mate, message in zip(mates, messages)
        ]
        crosses = [crosses[0]] + [moved(a, 0, 0, turn) for turn, a in enumerate(crosses) if turn]

        pieces = []
        if teams > 1:
            latest = [moved(stale[shift], 1, shift, 0) for shift in range(share)]
            pieces += latest
            for _ in range(teams - 2):
                latest = [moved(piece, 1, 0, 0) for piece in latest]
                pieces += latest

        cost = pl.CostEstimate(flops=500000000, bytes_accessed=1800000, transcendentals=0)
        pieces = handed_on(pieces, cost_estimate=cost) if pieces else pieces

        from_shards = [a for (shift, _), a in zip(mates, arrived) if shift == 0]
        cross_own, *cross_away = call(
            lambda *refs: cross_kernel(shards, *refs),
            "cross",
            [pltpu.VMEM((rows, cols), kind)] * shards,
            (*crosses, *text, *from_shards),
            scratch=[
                pltpu.VMEM((heads, shards * rows, text_rows), kind),
                pltpu.VMEM((heads, shards * rows, HD), jnp.float32),
            ],
        )
        cross_back = [moved(a, 0, 0, -turn - 1) for turn, a in enumerate(cross_away)]

        def place_kernel(spots, size, *refs):
            run_all(
                [
                    (ref, place_of(shift, turn, refs[-2], size))
                    for (shift, turn), ref in zip(spots, refs[:-2])
                ],
                refs[-1],
            )

        def cross_place_kernel(*refs):
            copies = []
            for turn, ref in enumerate(refs[:-2]):
                shard = lax.rem(lax.axis_index("head") + turn, shards)
                start = pl.multiple_of(shard * cols, HD)
                copies.append((ref, refs[-2].at[0, :, pl.ds(start, cols)]))
            run_all(copies, refs[-1])

        whole = jax.ShapeDtypeStruct((1, rows, full), kind)
        cross_mixed = call(
            cross_place_kernel,
            "place_cross",
            whole,
            (cross_own, *cross_back),
            hbm,
            scratch=[pltpu.SemaphoreType.DMA((shards,))],
        )

        def near_kernel(*refs):
            own_ref, others, (sums_ref, logs_ref, weights_ref, shares_ref) = refs[0], refs[1:-4], refs[-4:]
            for index in range(near_width // HD):
                lanes = head_lanes(index)
                keys = [own_ref[rows : 2 * rows, lanes]] + [ref[:rows, lanes] for ref in others]
                scores = scores_of(own_ref[:rows, lanes], jnp.concatenate(keys, axis=0))
                weights_ref[index], shares_ref[index], logs_ref[index] = softmax_parts(scores)
            for index in range(near_width // HD):
                lanes = head_lanes(index)
                values = [own_ref[2 * rows :, lanes]] + [ref[rows:, lanes] for ref in others]
                sums = weighted(weights_ref[index], jnp.concatenate(values, axis=0))
                sums_ref[:, lanes] = sums * shares_ref[index]

        near = []
        if near_blocks:
            near = call(
                near_kernel,
                "near",
                [
                    pltpu.VMEM((rows, near_width), jnp.float32),
                    pltpu.VMEM((near_width // HD, rows, HD), jnp.float32),
                ],
                nears,
                scratch=[
                    pltpu.VMEM((near_width // HD, rows, everyone), kind),
                    pltpu.VMEM((near_width // HD, rows, HD), jnp.float32),
                ],
            )

        spots = [(0, 0)] + mates
        tokens = [own, *arrived]
        first_row = dict(zip(spots, [0] + [fresh_start(*mate) for mate in mates]))

        def token_rows(refs, shift, index, lanes):
            found = []
            for spot, ref in zip(spots, refs):
                if spot[0] == shift:
                    start = first_row[spot] + index * rows
                    found.append(ref[start : start + rows, lanes])
            return found

        def stale_of(refs, shift, index, lanes):
            own_stale, *others = refs[len(spots) :]
            found = []
            if shift != 0:
                found.append(own_stale)
            found += [
                ref for (other, turn), ref in zip(spots, refs) if turn == 0 and other not in (0, shift)
            ]
            block = slice(index * patch_rows, (index + 1) * patch_rows)
            return [ref[block, lanes] for ref in found + others]

        def weights_kernel(*refs):
            count = len(spots) + 1 + len(pieces)
            sources, targets, logs_of = refs[:count], refs[count:], {}
            for head in range(share_heads):
                lanes = head_lanes(head)
                for shift in range(share):
                    queries = token_rows(sources, shift, 0, lanes)
                    keys = stale_of(sources, shift, 0, lanes)
                    if shift == 0:
                        keys = token_rows(sources, shift, 1, lanes) + keys
                    weights, shares, logs = softmax_parts(
                        scores_of(jnp.concatenate(queries, axis=0), jnp.concatenate(keys, axis=0))
                    )
                    for turn in range(shards):
                        spot = spots.index((shift, turn))
                        block = slice(turn * rows, (turn + 1) * rows)
                        targets[2 * spot][head] = weights[block]
                        targets[2 * spot + 1][head] = shares[block]
                        logs_of.setdefault(spot, []).append(logs[block])
            for place, mate in enumerate(over_patch):
                targets[2 * len(spots) + place][...] = lanes_of_logs(logs_of[spots.index(mate)])

        def mix_kernel(shift, weights_ref, shares_ref, *refs):
            sources, target = refs[:-1], refs[-1]
            for head in range(share_heads):
                lanes = head_lanes(head)
                values = stale_of(sources, shift, 1, lanes)
                if shift == 0:
                    values = token_rows(sources, shift, 2, lanes) + values
                mixed = weighted(weights_ref[head], jnp.concatenate(values, axis=0))
                target[:, lanes] = (mixed * shares_ref[head]).astype(target.dtype)

        def mate_mix_kernel(shift, weights_ref, shares_ref, logs_ref, *refs):
            mix_kernel(shift, weights_ref, shares_ref, *refs[:-1], refs[-1].at[:, pl.ds(0, width)])
            refs[-1][:, width:] = logs_ref[...]

        def merge_kernel(*refs):
            (sums_ref, logs_ref), refs = refs[:2], refs[2:]
            for (shift, turn), far, target in zip(over_patch, refs, refs[len(over_patch) :]):
                first = near_blocks.index((turn, shift)) * share_heads
                for head in range(share_heads):
                    lanes = head_lanes(head)
                    far_logs, near_logs = logs_of_lanes(far[:, width:], head), logs_ref[first + head]
                    tops = jnp.maximum(far_logs, near_logs)
                    far_part, near_part = jnp.exp(far_logs - tops), jnp.exp(near_logs - tops)
                    mixed = far[:, lanes].astype(jnp.float32) * far_part
                    mixed += sums_ref[:, head_lanes(first + head)] * near_part
                    target[:, lanes] = (mixed / (far_part + near_part)).astype(target.dtype)

        sources = (*tokens, stale[0], *pieces)
        part_shapes = []
        for shift, _ in spots:
            seen = patch_rows * (patches if shift == 0 else patches - 1)
            part_shapes += [
                pltpu.VMEM((share_heads, rows, seen), kind),
                pltpu.VMEM((share_heads, rows, HD), jnp.float32),
            ]
        parts = call(
            weights_kernel,
            "weights",
            part_shapes + [pltpu.VMEM((rows, HD), kind)] * len(over_patch),
            sources,
        )

        def mixed(spot):
            pair, shift = parts[2 * spot : 2 * spot + 2], spots[spot][0]
            if shift == 0:
                kernel, shape = mix_kernel, (rows, width)
            else:
                kernel, shape = mate_mix_kernel, (rows, width + HD)
                pair = (*pair, parts[2 * len(spots) + over_patch.index(spots[spot])])
            return call(
                lambda *refs: kernel(shift, *refs), "mix", pltpu.VMEM(shape, kind), (*pair, *sources)
            )

        back = [
            moved(mixed(index), 0, -shift, -turn)
            for index, (shift, turn) in enumerate(spots)
            if index > 0
        ]
        if over_patch:
            back[shards - 1 :] = call(
                merge_kernel,
                "merge",
                [pltpu.VMEM((rows, width), kind)] * len(over_patch),
                (*near, *back[shards - 1 :]),
            )
        self_mixed = call(
            lambda *refs: place_kernel(spots, width, *refs),
            "place_self",
            whole,
            (mixed(0), *back),
            hbm,
            scratch=[pltpu.SemaphoreType.DMA((len(spots),))],
        )
        return (self_mixed, cross_mixed)

    token = P(("group", "cfg"), ("patch", "head"), None)
    stale = P(("group", "cfg"), "patch", "head")
    text = P(("group", "cfg"), None, "head")
    return jax.shard_map(
        per_device,
        mesh=mesh,
        in_specs=(token, token, token, stale, stale, token, text, text, P(("group", "cfg"), None)),
        out_specs=(token, token),
        check_vma=False,
    )
```

```python
import math

import jax
import jax.numpy as jnp
from jax import lax
from jax.experimental import pallas as pl
from jax.experimental.pallas import tpu as pltpu
from jax.sharding import PartitionSpec as P

HD = 128
SCALE = 1.0 / math.sqrt(HD)
TERMS = 3


def scores_of(queries, keys):
    return lax.dot_general(
        queries, keys, (((1,), (1,)), ((), ())), preferred_element_type=jnp.float32
    ) * SCALE


def weighted(weights, values):
    return lax.dot_general(
        weights, values, (((1,), (0,)), ((), ())), preferred_element_type=jnp.float32
    )


def softmax_parts(scores):
    tops = jnp.max(scores, axis=-1, keepdims=True)
    weights = jnp.exp(scores - tops)
    totals = jnp.sum(weights, axis=-1, keepdims=True)
    shape = (scores.shape[0], HD)
    shares = jnp.broadcast_to(1.0 / totals, shape)
    logs = jnp.broadcast_to(tops + jnp.log(totals), shape)
    return weights.astype(jnp.bfloat16), shares, logs


def lanes_of_logs(logs):
    lane = lax.broadcasted_iota(jnp.int32, logs[0].shape, 1)
    block = jnp.zeros(logs[0].shape, jnp.float32)
    for head, rest in enumerate(logs):
        for term in range(TERMS):
            part = rest.astype(jnp.bfloat16).astype(jnp.float32)
            block = jnp.where(lane == TERMS * head + term, part, block)
            rest = rest - part
    return block.astype(jnp.bfloat16)


def logs_of_lanes(block, head):
    lane = lax.broadcasted_iota(jnp.int32, (HD, HD), 0)
    picked = (lane >= TERMS * head) & (lane < TERMS * (head + 1))
    return weighted(block, jnp.where(picked, 1.0, 0.0).astype(block.dtype))


def run_all(copies, sems):
    started = []
    for index, (source, target) in enumerate(copies):
        started.append(pltpu.make_async_copy(source, target, sems.at[index]))
        started[-1].start()
    for copy in started:
        copy.wait()


def load_kernel(*refs):
    half = len(refs) // 2
    run_all(zip(refs[:half], refs[half:-1]), refs[-1])


def gate_kernel(*refs):
    pass


def head_lanes(head):
    return slice(head * HD, (head + 1) * HD)


def cross_kernel(shards, *refs):
    queries, (key_ref, value_ref, mask_ref) = refs[:shards], refs[shards : shards + 3]
    targets, (weights_ref, shares_ref) = refs[2 * shards + 2 : -2], refs[-2:]
    rows, cols = targets[0].shape
    usable = mask_ref[...] > 0
    for head in range(cols // HD):
        lanes = head_lanes(head)
        scores = scores_of(
            jnp.concatenate([ref[:, lanes] for ref in queries], axis=0), key_ref[0, :, lanes]
        )
        weights_ref[head], shares_ref[head], _ = softmax_parts(
            jnp.where(usable, scores, -jnp.inf)
        )
    for head in range(cols // HD):
        lanes = head_lanes(head)
        mixed = weighted(weights_ref[head], value_ref[0, :, lanes]) * shares_ref[head]
        for place, target in enumerate(targets):
            target[:, lanes] = mixed[place * rows : (place + 1) * rows].astype(target.dtype)


def solution(mesh):
    shards = mesh.shape["head"]
    patches = mesh.shape["patch"]
    axes = ("patch", "head")
    vmem = pl.BlockSpec(memory_space=pltpu.VMEM)
    hbm = pl.BlockSpec(memory_space=pltpu.HBM)
    anywhere = pl.BlockSpec(memory_space=pl.ANY)
    params = pltpu.CompilerParams(vmem_limit_bytes=32 * 1024 * 1024)

    def call(kernel, name, out_shape, operands, out_spec=vmem, in_spec=vmem, scratch=(), **more):
        return pl.pallas_call(
            kernel,
            out_shape=out_shape,
            in_specs=[in_spec] * len(operands),
            out_specs=jax.tree.map(lambda _: out_spec, out_shape),
            scratch_shapes=scratch,
            compiler_params=params,
            name=name,
            **more,
        )(*operands)

    def in_hbm(*arrays):
        return [pltpu.with_memory_space_constraint(a, pltpu.HBM) for a in arrays]

    def handed_on(arrays, others=(), **more):
        return call(
            gate_kernel,
            "gate",
            [jax.ShapeDtypeStruct(a.shape, a.dtype) for a in arrays],
            (*arrays, *others),
            anywhere,
            anywhere,
            input_output_aliases={i: i for i in range(len(arrays))},
            **more,
        )

    def per_device(
        fresh_query,
        fresh_key,
        fresh_value,
        stale_key,
        stale_value,
        cross_query,
        text_key,
        text_value,
        text_mask,
    ):
        rows, full = fresh_query.shape[1:]
        everyone = rows * shards
        patch_rows = stale_key.shape[1]
        text_rows = text_key.shape[1]
        kind = fresh_query.dtype
        cols = full // shards
        heads = cols // HD
        share = math.gcd(patches, heads)
        teams = patches // share
        width = cols // share
        share_heads = heads // share
        mates = [(j, s) for j in range(share) for s in range(shards) if (j, s) != (0, 0)]

        ring = list(range(0, teams, 2)) + list(range(1, teams, 2))[::-1]
        ring_next = dict(zip(ring, ring[1:] + ring[:1]))

        def moved(array, step, shift, turn):
            pairs = []
            for patch in range(patches):
                team, member = divmod(patch, share)
                team = ring_next[team] if step else team
                target = team * share + (member + shift) % share
                for shard in range(shards):
                    pairs.append(
                        (patch * shards + shard, target * shards + (shard + turn) % shards)
                    )
            return lax.ppermute(array, axes, pairs)

        def place_of(shift, turn, ref, size):
            shard = lax.rem(lax.axis_index("head") + turn, shards)
            member = lax.rem(lax.axis_index("patch") + shift, share)
            start = pl.multiple_of(shard * cols + member * width, HD)
            return ref.at[0, :, pl.ds(start, size)]

        over_patch = [mate for mate in mates if mate[0] != 0]
        near_blocks = [(turn, shift) for turn in range(shards) for shift in range(1, share)]
        near_width = len(near_blocks) * width
        stale_rows = 2 * patch_rows

        def fresh_start(shift, turn):
            return stale_rows if turn == 0 and shift != 0 else 0

        def message_rows(shift, turn):
            return fresh_start(shift, turn) + (3 if shift == 0 else 1) * rows

        def stale_copies(shift, sources, target):
            part = lax.rem(lax.axis_index("patch") + shift, share)
            lanes = pl.ds(pl.multiple_of(part * width, HD), width)
            return [
                (source.at[0, :, lanes], target.at[pl.ds(index * patch_rows, patch_rows)])
                for index, source in enumerate(sources)
            ]

        def stale_kernel(*refs):
            copies = []
            for shift in range(share):
                copies += stale_copies(shift, refs[:2], refs[2 + shift])
            run_all(copies, refs[-1])

        stale = call(
            stale_kernel,
            "pack_stale",
            [pltpu.VMEM((stale_rows, width), kind)] * share,
            in_hbm(stale_key, stale_value),
            in_spec=hbm,
            scratch=[pltpu.SemaphoreType.DMA((2 * share,))],
        )

        def pack_kernel(query, key, value, old_key, old_value, cross, *refs):
            own, refs = refs[0], refs[1:]
            crosses, messages = refs[:shards], refs[shards : shards + len(mates)]
            nears = refs[shards + len(mates) : -1]
            copies = []

            def fresh_copies(shift, turn, target, first):
                for index, source in enumerate((query, key, value)[: 3 if shift == 0 else 1]):
                    block = pl.ds(first + index * rows, rows)
                    copies.append((place_of(shift, turn, source, width), target.at[block]))

            for (shift, turn), message in zip(mates, messages):
                first = fresh_start(shift, turn)
                if first:
                    copies.extend(stale_copies(shift, (old_key, old_value), message))
                fresh_copies(shift, turn, message, first)
            fresh_copies(0, 0, own, 0)
            for turn, target in enumerate(crosses):
                shard = lax.rem(lax.axis_index("head") + turn, shards)
                lanes = pl.ds(pl.multiple_of(shard * cols, HD), cols)
                copies.append((cross.at[0, :, lanes], target))
            for turn, target in enumerate(nears):
                for index, source in enumerate((query, key, value)[0 if turn == 0 else 1 :]):
                    for place, (other, shift) in enumerate(near_blocks):
                        block = target.at[pl.ds(index * rows, rows), pl.ds(place * width, width)]
                        copies.append((place_of(shift, turn + other, source, width), block))
            run_all(copies, refs[-1])

        packed_shapes = (
            [(3 * rows, width)]
            + [(rows, cols)] * shards
            + [(message_rows(*mate), width) for mate in mates]
        )
        if near_blocks:
            packed_shapes += [(3 * rows, near_width)] + [(2 * rows, near_width)] * (shards - 1)
        copy_count = 3 + shards + sum(
            (3 if mate[0] == 0 else 1) + (2 if fresh_start(*mate) else 0) for mate in mates
        )
        copy_count += len(near_blocks) * (2 * shards + 1)
        packed = call(
            pack_kernel,
            "pack",
            [pltpu.VMEM(shape, kind) for shape in packed_shapes],
            in_hbm(fresh_query, fresh_key, fresh_value, stale_key, stale_value, cross_query),
            in_spec=hbm,
            scratch=[pltpu.SemaphoreType.DMA((copy_count,))],
        )
        own, packed = packed[0], packed[1:]
        crosses, messages = packed[:shards], packed[shards : shards + len(mates)]
        nears = packed[shards + len(mates) :]
        text = [text_key, text_value, text_mask]
        text = call(
            load_kernel,
            "load",
            [pltpu.VMEM(a.shape, a.dtype) for a in text],
            in_hbm(*text),
            in_spec=hbm,
            scratch=[pltpu.SemaphoreType.DMA((len(text),))],
        )

        arrived = [
            moved(message, 0, *mate) for mate, message in zip(mates, messages)
        ]
        crosses = [crosses[0]] + [moved(a, 0, 0, turn) for turn, a in enumerate(crosses) if turn]
        from_shards = [a for (shift, _), a in zip(mates, arrived) if shift == 0]
        nears = [
            moved(handed_on([a], [text[-1], *from_shards])[0], 0, 0, turn) if turn else a
            for turn, a in enumerate(nears)
        ]

        pieces = []
        if teams > 1:
            latest = [moved(stale[shift], 1, shift, 0) for shift in range(share)]
            pieces += latest
            for _ in range(teams - 2):
                latest = [moved(piece, 1, 0, 0) for piece in latest]
                pieces += latest

        cost = pl.CostEstimate(flops=2000000000, bytes_accessed=7200000, transcendentals=0)
        pieces = handed_on(pieces, cost_estimate=cost) if pieces else pieces

        cross_own, *cross_away = call(
            lambda *refs: cross_kernel(shards, *refs),
            "cross",
            [pltpu.VMEM((rows, cols), kind)] * shards,
            (*crosses, *text, *from_shards),
            scratch=[
                pltpu.VMEM((heads, shards * rows, text_rows), kind),
                pltpu.VMEM((heads, shards * rows, HD), jnp.float32),
            ],
        )
        cross_back = [moved(a, 0, 0, -turn - 1) for turn, a in enumerate(cross_away)]

        def place_kernel(spots, size, *refs):
            run_all(
                [
                    (ref, place_of(shift, turn, refs[-2], size))
                    for (shift, turn), ref in zip(spots, refs[:-2])
                ],
                refs[-1],
            )

        def cross_place_kernel(*refs):
            copies = []
            for turn, ref in enumerate(refs[:-2]):
                shard = lax.rem(lax.axis_index("head") + turn, shards)
                start = pl.multiple_of(shard * cols, HD)
                copies.append((ref, refs[-2].at[0, :, pl.ds(start, cols)]))
            run_all(copies, refs[-1])

        whole = jax.ShapeDtypeStruct((1, rows, full), kind)
        cross_mixed = call(
            cross_place_kernel,
            "place_cross",
            whole,
            (cross_own, *cross_back),
            hbm,
            scratch=[pltpu.SemaphoreType.DMA((shards,))],
        )

        def near_kernel(*refs):
            own_ref, others, (sums_ref, logs_ref, weights_ref, shares_ref) = refs[0], refs[1:-4], refs[-4:]
            for index in range(near_width // HD):
                lanes = head_lanes(index)
                keys = [own_ref[rows : 2 * rows, lanes]] + [ref[:rows, lanes] for ref in others]
                scores = scores_of(own_ref[:rows, lanes], jnp.concatenate(keys, axis=0))
                weights_ref[index], shares_ref[index], logs_ref[index] = softmax_parts(scores)
            for index in range(near_width // HD):
                lanes = head_lanes(index)
                values = [own_ref[2 * rows :, lanes]] + [ref[rows:, lanes] for ref in others]
                sums = weighted(weights_ref[index], jnp.concatenate(values, axis=0))
                sums_ref[:, lanes] = sums * shares_ref[index]

        near = []
        if near_blocks:
            near = call(
                near_kernel,
                "near",
                [
                    pltpu.VMEM((rows, near_width), jnp.float32),
                    pltpu.VMEM((near_width // HD, rows, HD), jnp.float32),
                ],
                nears,
                scratch=[
                    pltpu.VMEM((near_width // HD, rows, everyone), kind),
                    pltpu.VMEM((near_width // HD, rows, HD), jnp.float32),
                ],
            )

        spots = [(0, 0)] + mates
        tokens = [own, *arrived]
        first_row = dict(zip(spots, [0] + [fresh_start(*mate) for mate in mates]))

        def token_rows(refs, shift, index, lanes):
            found = []
            for spot, ref in zip(spots, refs):
                if spot[0] == shift:
                    start = first_row[spot] + index * rows
                    found.append(ref[start : start + rows, lanes])
            return found

        def stale_of(refs, shift, index, lanes):
            own_stale, *others = refs[len(spots) :]
            found = []
            if shift != 0:
                found.append(own_stale)
            found += [
                ref for (other, turn), ref in zip(spots, refs) if turn == 0 and other not in (0, shift)
            ]
            block = slice(index * patch_rows, (index + 1) * patch_rows)
            return [ref[block, lanes] for ref in found + others]

        def weights_kernel(*refs):
            count = len(spots) + 1 + len(pieces)
            sources, targets, logs_of = refs[:count], refs[count:], {}
            for head in range(share_heads):
                lanes = head_lanes(head)
                for shift in range(share):
                    queries = token_rows(sources, shift, 0, lanes)
                    keys = stale_of(sources, shift, 0, lanes)
                    if shift == 0:
                        keys = token_rows(sources, shift, 1, lanes) + keys
                    weights, shares, logs = softmax_parts(
                        scores_of(jnp.concatenate(queries, axis=0), jnp.concatenate(keys, axis=0))
                    )
                    for turn in range(shards):
                        spot = spots.index((shift, turn))
                        block = slice(turn * rows, (turn + 1) * rows)
                        targets[2 * spot][head] = weights[block]
                        targets[2 * spot + 1][head] = shares[block]
                        logs_of.setdefault(spot, []).append(logs[block])
            for place, mate in enumerate(over_patch):
                targets[2 * len(spots) + place][...] = lanes_of_logs(logs_of[spots.index(mate)])

        def mix_kernel(shift, weights_ref, shares_ref, *refs):
            sources, target = refs[:-1], refs[-1]
            for head in range(share_heads):
                lanes = head_lanes(head)
                values = stale_of(sources, shift, 1, lanes)
                if shift == 0:
                    values = token_rows(sources, shift, 2, lanes) + values
                mixed = weighted(weights_ref[head], jnp.concatenate(values, axis=0))
                target[:, lanes] = (mixed * shares_ref[head]).astype(target.dtype)

        def mate_mix_kernel(shift, weights_ref, shares_ref, logs_ref, *refs):
            mix_kernel(shift, weights_ref, shares_ref, *refs[:-1], refs[-1].at[:, pl.ds(0, width)])
            refs[-1][:, width:] = logs_ref[...]

        def merge_kernel(*refs):
            (sums_ref, logs_ref), refs = refs[:2], refs[2:]
            for (shift, turn), far, target in zip(over_patch, refs, refs[len(over_patch) :]):
                first = near_blocks.index((turn, shift)) * share_heads
                for head in range(share_heads):
                    lanes = head_lanes(head)
                    far_logs, near_logs = logs_of_lanes(far[:, width:], head), logs_ref[first + head]
                    tops = jnp.maximum(far_logs, near_logs)
                    far_part, near_part = jnp.exp(far_logs - tops), jnp.exp(near_logs - tops)
                    mixed = far[:, lanes].astype(jnp.float32) * far_part
                    mixed += sums_ref[:, head_lanes(first + head)] * near_part
                    target[:, lanes] = (mixed / (far_part + near_part)).astype(target.dtype)

        sources = (*tokens, stale[0], *pieces)
        part_shapes = []
        for shift, _ in spots:
            seen = patch_rows * (patches if shift == 0 else patches - 1)
            part_shapes += [
                pltpu.VMEM((share_heads, rows, seen), kind),
                pltpu.VMEM((share_heads, rows, HD), jnp.float32),
            ]
        parts = call(
            weights_kernel,
            "weights",
            part_shapes + [pltpu.VMEM((rows, HD), kind)] * len(over_patch),
            sources,
        )

        def mixed(spot):
            pair, shift = parts[2 * spot : 2 * spot + 2], spots[spot][0]
            if shift == 0:
                kernel, shape = mix_kernel, (rows, width)
            else:
                kernel, shape = mate_mix_kernel, (rows, width + HD)
                pair = (*pair, parts[2 * len(spots) + over_patch.index(spots[spot])])
            return call(
                lambda *refs: kernel(shift, *refs), "mix", pltpu.VMEM(shape, kind), (*pair, *sources)
            )

        back = [
            moved(mixed(index), 0, -shift, -turn)
            for index, (shift, turn) in enumerate(spots)
            if index > 0
        ]
        if over_patch:
            back[shards - 1 :] = call(
                merge_kernel,
                "merge",
                [pltpu.VMEM((rows, width), kind)] * len(over_patch),
                (*near, *back[shards - 1 :]),
            )
        self_mixed = call(
            lambda *refs: place_kernel(spots, width, *refs),
            "place_self",
            whole,
            (mixed(0), *back),
            hbm,
            scratch=[pltpu.SemaphoreType.DMA((len(spots),))],
        )
        return (self_mixed, cross_mixed)

    token = P(("group", "cfg"), ("patch", "head"), None)
    stale = P(("group", "cfg"), "patch", "head")
    text = P(("group", "cfg"), None, "head")
    return jax.shard_map(
        per_device,
        mesh=mesh,
        in_specs=(token, token, token, stale, stale, token, text, text, P(("group", "cfg"), None)),
        out_specs=(token, token),
        check_vma=False,
    )
```

```python
import math

import jax
import jax.numpy as jnp
from jax import lax
from jax.experimental import pallas as pl
from jax.experimental.pallas import tpu as pltpu
from jax.sharding import PartitionSpec as P

HD = 128
SCALE = 1.0 / math.sqrt(HD)
TERMS = 3


def scores_of(queries, keys):
    return lax.dot_general(
        queries, keys, (((1,), (1,)), ((), ())), preferred_element_type=jnp.float32
    ) * SCALE


def weighted(weights, values):
    return lax.dot_general(
        weights, values, (((1,), (0,)), ((), ())), preferred_element_type=jnp.float32
    )


def softmax_parts(scores):
    tops = jnp.max(scores, axis=-1, keepdims=True)
    weights = jnp.exp(scores - tops)
    totals = jnp.sum(weights, axis=-1, keepdims=True)
    shape = (scores.shape[0], HD)
    shares = jnp.broadcast_to(1.0 / totals, shape)
    logs = jnp.broadcast_to(tops + jnp.log(totals), shape)
    return weights.astype(jnp.bfloat16), shares, logs


def lanes_of_logs(logs):
    lane = lax.broadcasted_iota(jnp.int32, logs[0].shape, 1)
    block = jnp.zeros(logs[0].shape, jnp.float32)
    for head, rest in enumerate(logs):
        for term in range(TERMS):
            part = rest.astype(jnp.bfloat16).astype(jnp.float32)
            block = jnp.where(lane == TERMS * head + term, part, block)
            rest = rest - part
    return block.astype(jnp.bfloat16)


def logs_of_lanes(block, head):
    lane = lax.broadcasted_iota(jnp.int32, (HD, HD), 0)
    picked = (lane >= TERMS * head) & (lane < TERMS * (head + 1))
    return weighted(block, jnp.where(picked, 1.0, 0.0).astype(block.dtype))


def run_all(copies, sems):
    started = []
    for index, (source, target) in enumerate(copies):
        started.append(pltpu.make_async_copy(source, target, sems.at[index]))
        started[-1].start()
    for copy in started:
        copy.wait()


def load_kernel(*refs):
    half = len(refs) // 2
    run_all(zip(refs[:half], refs[half:-1]), refs[-1])


def gate_kernel(*refs):
    pass


def head_lanes(head):
    return slice(head * HD, (head + 1) * HD)


def cross_kernel(shards, *refs):
    queries, (key_ref, value_ref, mask_ref) = refs[:shards], refs[shards : shards + 3]
    targets, (weights_ref, shares_ref) = refs[2 * shards + 2 : -2], refs[-2:]
    rows, cols = targets[0].shape
    usable = mask_ref[...] > 0
    for head in range(cols // HD):
        lanes = head_lanes(head)
        scores = scores_of(
            jnp.concatenate([ref[:, lanes] for ref in queries], axis=0), key_ref[0, :, lanes]
        )
        weights_ref[head], shares_ref[head], _ = softmax_parts(
            jnp.where(usable, scores, -jnp.inf)
        )
    for head in range(cols // HD):
        lanes = head_lanes(head)
        mixed = weighted(weights_ref[head], value_ref[0, :, lanes]) * shares_ref[head]
        for place, target in enumerate(targets):
            target[:, lanes] = mixed[place * rows : (place + 1) * rows].astype(target.dtype)


def solution(mesh):
    shards = mesh.shape["head"]
    patches = mesh.shape["patch"]
    axes = ("patch", "head")
    vmem = pl.BlockSpec(memory_space=pltpu.VMEM)
    hbm = pl.BlockSpec(memory_space=pltpu.HBM)
    anywhere = pl.BlockSpec(memory_space=pl.ANY)
    params = pltpu.CompilerParams(vmem_limit_bytes=32 * 1024 * 1024)

    def call(kernel, name, out_shape, operands, out_spec=vmem, in_spec=vmem, scratch=(), **more):
        return pl.pallas_call(
            kernel,
            out_shape=out_shape,
            in_specs=[in_spec] * len(operands),
            out_specs=jax.tree.map(lambda _: out_spec, out_shape),
            scratch_shapes=scratch,
            compiler_params=params,
            name=name,
            **more,
        )(*operands)

    def in_hbm(*arrays):
        return [pltpu.with_memory_space_constraint(a, pltpu.HBM) for a in arrays]

    def handed_on(arrays, others=(), **more):
        return call(
            gate_kernel,
            "gate",
            [jax.ShapeDtypeStruct(a.shape, a.dtype) for a in arrays],
            (*arrays, *others),
            anywhere,
            anywhere,
            input_output_aliases={i: i for i in range(len(arrays))},
            **more,
        )

    def per_device(
        fresh_query,
        fresh_key,
        fresh_value,
        stale_key,
        stale_value,
        cross_query,
        text_key,
        text_value,
        text_mask,
    ):
        rows, full = fresh_query.shape[1:]
        everyone = rows * shards
        patch_rows = stale_key.shape[1]
        text_rows = text_key.shape[1]
        kind = fresh_query.dtype
        cols = full // shards
        heads = cols // HD
        share = math.gcd(patches, heads)
        teams = patches // share
        width = cols // share
        share_heads = heads // share
        mates = [(j, s) for j in range(share) for s in range(shards) if (j, s) != (0, 0)]

        ring = list(range(0, teams, 2)) + list(range(1, teams, 2))[::-1]
        ring_next = dict(zip(ring, ring[1:] + ring[:1]))

        def moved(array, step, shift, turn):
            pairs = []
            for patch in range(patches):
                team, member = divmod(patch, share)
                team = ring_next[team] if step else team
                target = team * share + (member + shift) % share
                for shard in range(shards):
                    pairs.append(
                        (patch * shards + shard, target * shards + (shard + turn) % shards)
                    )
            return lax.ppermute(array, axes, pairs)

        def place_of(shift, turn, ref, size):
            shard = lax.rem(lax.axis_index("head") + turn, shards)
            member = lax.rem(lax.axis_index("patch") + shift, share)
            start = pl.multiple_of(shard * cols + member * width, HD)
            return ref.at[0, :, pl.ds(start, size)]

        over_patch = [mate for mate in mates if mate[0] != 0]
        near_blocks = [(turn, shift) for turn in range(shards) for shift in range(1, share)]
        near_width = len(near_blocks) * width
        stale_rows = 2 * patch_rows

        def fresh_start(shift, turn):
            return stale_rows if turn == 0 and shift != 0 else 0

        def message_rows(shift, turn):
            return fresh_start(shift, turn) + (3 if shift == 0 else 1) * rows

        def stale_copies(shift, sources, target):
            part = lax.rem(lax.axis_index("patch") + shift, share)
            lanes = pl.ds(pl.multiple_of(part * width, HD), width)
            return [
                (source.at[0, :, lanes], target.at[pl.ds(index * patch_rows, patch_rows)])
                for index, source in enumerate(sources)
            ]

        def stale_kernel(*refs):
            copies = []
            for shift in range(share):
                copies += stale_copies(shift, refs[:2], refs[2 + shift])
            run_all(copies, refs[-1])

        stale = call(
            stale_kernel,
            "pack_stale",
            [pltpu.VMEM((stale_rows, width), kind)] * share,
            in_hbm(stale_key, stale_value),
            in_spec=hbm,
            scratch=[pltpu.SemaphoreType.DMA((2 * share,))],
        )

        def pack_kernel(query, key, value, old_key, old_value, cross, *refs):
            own, refs = refs[0], refs[1:]
            crosses, messages = refs[:shards], refs[shards : shards + len(mates)]
            nears = refs[shards + len(mates) : -1]
            copies = []

            def fresh_copies(shift, turn, target, first):
                for index, source in enumerate((query, key, value)[: 3 if shift == 0 else 1]):
                    block = pl.ds(first + index * rows, rows)
                    copies.append((place_of(shift, turn, source, width), target.at[block]))

            for (shift, turn), message in zip(mates, messages):
                first = fresh_start(shift, turn)
                if first:
                    copies.extend(stale_copies(shift, (old_key, old_value), message))
                fresh_copies(shift, turn, message, first)
            fresh_copies(0, 0, own, 0)
            for turn, target in enumerate(crosses):
                shard = lax.rem(lax.axis_index("head") + turn, shards)
                lanes = pl.ds(pl.multiple_of(shard * cols, HD), cols)
                copies.append((cross.at[0, :, lanes], target))
            for turn, target in enumerate(nears):
                for index, source in enumerate((query, key, value)[0 if turn == 0 else 1 :]):
                    for place, (other, shift) in enumerate(near_blocks):
                        block = target.at[pl.ds(index * rows, rows), pl.ds(place * width, width)]
                        copies.append((place_of(shift, turn + other, source, width), block))
            run_all(copies, refs[-1])

        packed_shapes = (
            [(3 * rows, width)]
            + [(rows, cols)] * shards
            + [(message_rows(*mate), width) for mate in mates]
        )
        if near_blocks:
            packed_shapes += [(3 * rows, near_width)] + [(2 * rows, near_width)] * (shards - 1)
        copy_count = 3 + shards + sum(
            (3 if mate[0] == 0 else 1) + (2 if fresh_start(*mate) else 0) for mate in mates
        )
        copy_count += len(near_blocks) * (2 * shards + 1)
        packed = call(
            pack_kernel,
            "pack",
            [pltpu.VMEM(shape, kind) for shape in packed_shapes],
            in_hbm(fresh_query, fresh_key, fresh_value, stale_key, stale_value, cross_query),
            in_spec=hbm,
            scratch=[pltpu.SemaphoreType.DMA((copy_count,))],
        )
        own, packed = packed[0], packed[1:]
        crosses, messages = packed[:shards], packed[shards : shards + len(mates)]
        nears = packed[shards + len(mates) :]
        text = [text_key, text_value, text_mask]
        text = call(
            load_kernel,
            "load",
            [pltpu.VMEM(a.shape, a.dtype) for a in text],
            in_hbm(*text),
            in_spec=hbm,
            scratch=[pltpu.SemaphoreType.DMA((len(text),))],
        )

        nears = [
            moved(handed_on([a], text[-1:])[0], 0, 0, turn) if turn else a
            for turn, a in enumerate(nears)
        ]
        arrived = [
            moved(message, 0, *mate) for mate, message in zip(mates, messages)
        ]
        crosses = [crosses[0]] + [moved(a, 0, 0, turn) for turn, a in enumerate(crosses) if turn]

        pieces = []
        if teams > 1:
            latest = [moved(stale[shift], 1, shift, 0) for shift in range(share)]
            pieces += latest
            for _ in range(teams - 2):
                latest = [moved(piece, 1, 0, 0) for piece in latest]
                pieces += latest

        cost = pl.CostEstimate(flops=500000000, bytes_accessed=1800000, transcendentals=0)
        pieces = handed_on(pieces, cost_estimate=cost) if pieces else pieces

        from_shards = [a for (shift, _), a in zip(mates, arrived) if shift == 0]
        cross_own, *cross_away = call(
            lambda *refs: cross_kernel(shards, *refs),
            "cross",
            [pltpu.VMEM((rows, cols), kind)] * shards,
            (*crosses, *text, *from_shards),
            scratch=[
                pltpu.VMEM((heads, shards * rows, text_rows), kind),
                pltpu.VMEM((heads, shards * rows, HD), jnp.float32),
            ],
        )
        cross_back = [moved(a, 0, 0, -turn - 1) for turn, a in enumerate(cross_away)]

        def place_kernel(spots, size, *refs):
            run_all(
                [
                    (ref, place_of(shift, turn, refs[-2], size))
                    for (shift, turn), ref in zip(spots, refs[:-2])
                ],
                refs[-1],
            )

        def cross_place_kernel(*refs):
            copies = []
            for turn, ref in enumerate(refs[:-2]):
                shard = lax.rem(lax.axis_index("head") + turn, shards)
                start = pl.multiple_of(shard * cols, HD)
                copies.append((ref, refs[-2].at[0, :, pl.ds(start, cols)]))
            run_all(copies, refs[-1])

        whole = jax.ShapeDtypeStruct((1, rows, full), kind)
        cross_mixed = call(
            cross_place_kernel,
            "place_cross",
            whole,
            (cross_own, *cross_back),
            hbm,
            scratch=[pltpu.SemaphoreType.DMA((shards,))],
        )

        def near_kernel(*refs):
            own_ref, others, (sums_ref, logs_ref, weights_ref, shares_ref) = refs[0], refs[1:-4], refs[-4:]
            for index in range(near_width // HD):
                lanes = head_lanes(index)
                keys = [own_ref[rows : 2 * rows, lanes]] + [ref[:rows, lanes] for ref in others]
                scores = scores_of(own_ref[:rows, lanes], jnp.concatenate(keys, axis=0))
                weights_ref[index], shares_ref[index], logs_ref[index] = softmax_parts(scores)
            for index in range(near_width // HD):
                lanes = head_lanes(index)
                values = [own_ref[2 * rows :, lanes]] + [ref[rows:, lanes] for ref in others]
                sums = weighted(weights_ref[index], jnp.concatenate(values, axis=0))
                sums_ref[:, lanes] = sums * shares_ref[index]

        near = []
        if near_blocks:
            near = call(
                near_kernel,
                "near",
                [
                    pltpu.VMEM((rows, near_width), jnp.float32),
                    pltpu.VMEM((near_width // HD, rows, HD), jnp.float32),
                ],
                nears,
                scratch=[
                    pltpu.VMEM((near_width // HD, rows, everyone), kind),
                    pltpu.VMEM((near_width // HD, rows, HD), jnp.float32),
                ],
            )

        spots = [(0, 0)] + mates
        tokens = [own, *arrived]
        first_row = dict(zip(spots, [0] + [fresh_start(*mate) for mate in mates]))

        def token_rows(refs, shift, index, lanes):
            found = []
            for spot, ref in zip(spots, refs):
                if spot[0] == shift:
                    start = first_row[spot] + index * rows
                    found.append(ref[start : start + rows, lanes])
            return found

        def stale_of(refs, shift, index, lanes):
            own_stale, *others = refs[len(spots) :]
            found = []
            if shift != 0:
                found.append(own_stale)
            found += [
                ref for (other, turn), ref in zip(spots, refs) if turn == 0 and other not in (0, shift)
            ]
            block = slice(index * patch_rows, (index + 1) * patch_rows)
            return [ref[block, lanes] for ref in found + others]

        def weights_kernel(*refs):
            count = len(spots) + 1 + len(pieces)
            sources, targets, logs_of = refs[:count], refs[count:], {}
            for head in range(share_heads):
                lanes = head_lanes(head)
                for shift in range(share):
                    queries = token_rows(sources, shift, 0, lanes)
                    keys = stale_of(sources, shift, 0, lanes)
                    if shift == 0:
                        keys = token_rows(sources, shift, 1, lanes) + keys
                    weights, shares, logs = softmax_parts(
                        scores_of(jnp.concatenate(queries, axis=0), jnp.concatenate(keys, axis=0))
                    )
                    for turn in range(shards):
                        spot = spots.index((shift, turn))
                        block = slice(turn * rows, (turn + 1) * rows)
                        targets[2 * spot][head] = weights[block]
                        targets[2 * spot + 1][head] = shares[block]
                        logs_of.setdefault(spot, []).append(logs[block])
            for place, mate in enumerate(over_patch):
                targets[2 * len(spots) + place][...] = lanes_of_logs(logs_of[spots.index(mate)])

        def mix_kernel(shift, weights_ref, shares_ref, *refs):
            sources, target = refs[:-1], refs[-1]
            for head in range(share_heads):
                lanes = head_lanes(head)
                values = stale_of(sources, shift, 1, lanes)
                if shift == 0:
                    values = token_rows(sources, shift, 2, lanes) + values
                mixed = weighted(weights_ref[head], jnp.concatenate(values, axis=0))
                target[:, lanes] = (mixed * shares_ref[head]).astype(target.dtype)

        def mate_mix_kernel(shift, *refs):
            parts_in, sources, targets = refs[: 3 * shards], refs[3 * shards : -shards], refs[-shards:]
            for head in range(share_heads):
                lanes = head_lanes(head)
                values = jnp.concatenate(stale_of(sources, shift, 1, lanes), axis=0)
                for turn, target in enumerate(targets):
                    weights_ref, shares_ref = parts_in[3 * turn : 3 * turn + 2]
                    mixed = weighted(weights_ref[head], values) * shares_ref[head]
                    target[:, lanes] = mixed.astype(target.dtype)
            for turn, target in enumerate(targets):
                target[:, width:] = parts_in[3 * turn + 2][...]

        def merge_kernel(*refs):
            (sums_ref, logs_ref), refs = refs[:2], refs[2:]
            for (shift, turn), far, target in zip(over_patch, refs, refs[len(over_patch) :]):
                first = near_blocks.index((turn, shift)) * share_heads
                for head in range(share_heads):
                    lanes = head_lanes(head)
                    far_logs, near_logs = logs_of_lanes(far[:, width:], head), logs_ref[first + head]
                    tops = jnp.maximum(far_logs, near_logs)
                    far_part, near_part = jnp.exp(far_logs - tops), jnp.exp(near_logs - tops)
                    mixed = far[:, lanes].astype(jnp.float32) * far_part
                    mixed += sums_ref[:, head_lanes(first + head)] * near_part
                    target[:, lanes] = (mixed / (far_part + near_part)).astype(target.dtype)

        sources = (*tokens, stale[0], *pieces)
        part_shapes = []
        for shift, _ in spots:
            seen = patch_rows * (patches if shift == 0 else patches - 1)
            part_shapes += [
                pltpu.VMEM((share_heads, rows, seen), kind),
                pltpu.VMEM((share_heads, rows, HD), jnp.float32),
            ]
        parts = call(
            weights_kernel,
            "weights",
            part_shapes + [pltpu.VMEM((rows, HD), kind)] * len(over_patch),
            sources,
        )

        def mixed(spot):
            return call(
                lambda *refs: mix_kernel(0, *refs),
                "mix",
                pltpu.VMEM((rows, width), kind),
                (*parts[2 * spot : 2 * spot + 2], *sources),
            )

        def mate_mixed(shift):
            operands = []
            for turn in range(shards):
                spot = spots.index((shift, turn))
                logs = parts[2 * len(spots) + over_patch.index((shift, turn))]
                operands += [*parts[2 * spot : 2 * spot + 2], logs]
            made = call(
                lambda *refs: mate_mix_kernel(shift, *refs),
                "mix_mate",
                [pltpu.VMEM((rows, width + HD), kind)] * shards,
                (*operands, *sources),
            )
            return {(shift, turn): a for turn, a in enumerate(made)}

        ready = {}
        for shift in range(1, share):
            ready.update(mate_mixed(shift))
        back = [
            moved(ready[shift, turn] if shift else mixed(index), 0, -shift, -turn)
            for index, (shift, turn) in enumerate(spots)
            if index > 0
        ]
        if over_patch:
            back[shards - 1 :] = call(
                merge_kernel,
                "merge",
                [pltpu.VMEM((rows, width), kind)] * len(over_patch),
                (*near, *back[shards - 1 :]),
            )
        self_mixed = call(
            lambda *refs: place_kernel(spots, width, *refs),
            "place_self",
            whole,
            (mixed(0), *back),
            hbm,
            scratch=[pltpu.SemaphoreType.DMA((len(spots),))],
        )
        return (self_mixed, cross_mixed)

    token = P(("group", "cfg"), ("patch", "head"), None)
    stale = P(("group", "cfg"), "patch", "head")
    text = P(("group", "cfg"), None, "head")
    return jax.shard_map(
        per_device,
        mesh=mesh,
        in_specs=(token, token, token, stale, stale, token, text, text, P(("group", "cfg"), None)),
        out_specs=(token, token),
        check_vma=False,
    )
```
